128 devices in a mesh: blk: 32 (over y, x_hi, z), head: 4 (over x_lo, core).
Axes of the slice: x: 4 (x_hi: 2, x_lo: 2; x = x_hi * 2 + x_lo), y: 4, z: 4, core: 2. Of those that a mesh axis runs over, the one named last changes fastest.
Arguments:
- layer_input: bfloat16 [16384, 1024], P(('blk', 'head')), may hold values from -6 to 6
- attn_gain: float32 [1024], replicated, may hold values from 0.5 to 1.5
- w_query: bfloat16 [1024, 1024], P('blk', 'head'), may hold values from -0.1875 to 0.1875
- key_weight: bfloat16 [1024, 512], P('blk', 'head'), may hold values from -0.1875 to 0.1875
- value_weight: bfloat16 [1024, 512], P('blk', 'head'), may hold values from -0.1875 to 0.1875
- w_output: bfloat16 [1024, 1024], P('blk', 'head'), may hold values from -1.5 to 1.5
- query_gain: float32 [64], replicated, may hold values from 0.1 to 1.9
- key_gain: float32 [64], replicated, may hold values from 0.1 to 1.9
- ffn_gain: float32 [1024], replicated, may hold values from 0.5 to 1.5
- router: float32 [1024, 32], replicated, may hold values from -0.09375 to 0.09375
- w_gate: bfloat16 [32, 1024, 512], P('blk'), may hold values from -0.1875 to 0.1875
- w_up: bfloat16 [32, 1024, 512], P('blk'), may hold values from -0.1875 to 0.1875
- w_down: bfloat16 [32, 512, 1024], P('blk'), may hold values from -1 to 1
- routes: int32 [16384, 8], P(('blk', 'head')), may hold values from 0 to 31, all different within a row; in each aligned block of 128 rows (0 to 127, 128 to 255, ...) at most 40 rows name the same one
- doc_lengths: int32 [3], replicated, may hold values from 1 to 16382, as said below
- cotangent: bfloat16 [16384, 1024], P(('blk', 'head')), may hold values from -6 to 6
Outputs:
- layer_output: bfloat16 [16384, 1024], P(('blk', 'head'))
- input_grad: bfloat16 [16384, 1024], P(('blk', 'head'))
- attn_gain_grad: float32 [1024], replicated
- w_query_grad: float32 [1024, 1024], P('blk', 'head')
- w_key_grad: float32 [1024, 512], P('blk', 'head')
- w_value_grad: float32 [1024, 512], P('blk', 'head')
- w_output_grad: float32 [1024, 1024], P('blk', 'head')
- query_gain_grad: float32 [64], replicated
- key_gain_grad: float32 [64], replicated
- ffn_gain_grad: float32 [1024], replicated
- router_grad: float32 [1024, 32], replicated
- w_gate_grad: float32 [32, 1024, 512], P('blk')
- w_up_grad: float32 [32, 1024, 512], P('blk')
- w_down_grad: float32 [32, 512, 1024], P('blk')
The draws below stay inside these ranges and needn't reach their ends.
Inputs may be any that keep to these rules, and one draw needn't show every extreme that they name: `routes`: in the rows of one device (its 128 tokens) no expert is named more than 40 times, and in some devices' rows one expert is named exactly 40 times; a token names 8 different experts. `doc_lengths`: the lengths sum to 16384; the first and the last are at most 256, so that the middle document begins within the first 512 positions and ends within the last 512.
All inputs are finite; a program needn't handle non-finite values.
Results may differ from the reference program's by a relative error of at most 0.035.
Values may be sent and summed in bfloat16 or wider, within the bound.
A program may use at most 128 MiB of HBM per device.

```python
import functools
import math
import jax
import jax.numpy as jnp
import numpy as np
from jax import lax

MODEL_DIM = 1024
QUERY_HEADS = 16
KEY_VALUE_HEADS = 8
HEAD_SIZE = 64
FF = 512
TOPK = 8
BLOCK = 256
TOK_DEV = 128
EXPERTS = 32
QROWS = 512
TOKENS = 16384
CAP = 40


def draw_doc_lengths(key, part):
    key = jax.random.fold_in(key, 7)
    head_key, tail_key = jax.random.split(key)
    head_length = jax.random.randint(head_key, (), 1, QROWS // 2 + 1, dtype=jnp.int32)
    tail_length = jax.random.randint(tail_key, (), 1, QROWS // 2 + 1, dtype=jnp.int32)
    return jnp.stack([head_length, TOKENS - head_length - tail_length, tail_length]).astype(jnp.int32)


def shard_levels(rng, extent, cuts, low, high):
    level = 1.0
    for axis_at, parts in cuts:
        steps = jax.random.uniform(jax.random.fold_in(jax.random.fold_in(rng, 6), axis_at), (parts,), jnp.float32, low / len(cuts), high / len(cuts))
        level = level * jnp.repeat(jnp.exp(steps), extent[axis_at] // parts).reshape((-1,) + (1,) * (len(extent) - 1 - axis_at))
    return level


def assign_block(own_key, own, number, rows, amount, top, most, skew):
    sequence = jax.random.permutation(own_key, amount)
    crowded, ordinary = load_shares(amount, rows * top, most, skew, True), load_shares(amount, rows * top, most, skew, False)
    places = jnp.arange(amount)

    def named(tallies, rotation):
        used = int((tallies > 0).sum())
        fixed = max(1, used // 4)
        passed = fixed + (places - fixed + rotation * (used - fixed)) % max(1, amount - fixed)
        return jnp.zeros((amount,), jnp.int32).at[sequence[jnp.where(places < fixed, places, passed)]].set(jnp.asarray(tallies, jnp.int32))

    tallies = jnp.where(number % 4 == 0, named(crowded, number // 4), named(ordinary, number - number // 4 - 1))
    mixed = jax.random.permutation(jax.random.fold_in(own, 3), amount)
    source_of, sink = mixed[0:amount // 2 * 2:2], mixed[1:amount // 2 * 2:2]
    slack = jnp.minimum(tallies[source_of] - 1, most - tallies[sink]) // 2
    slack = jnp.where((source_of == sequence[0]) | (sink == sequence[0]) | (tallies[sink] == 0), 0, jnp.maximum(slack, 0))
    passed = jax.random.randint(jax.random.fold_in(own, 4), (amount // 2,), 0, 1 << 20) % (slack + 1)
    tallies = tallies.at[source_of].add(-passed).at[sink].add(passed)
    members = jnp.searchsorted(jnp.cumsum(tallies), jnp.arange(rows * top), side="right").astype(jnp.int32)
    grid = members.reshape(top, rows).T
    grid = grid[jax.random.permutation(jax.random.fold_in(own, 1), rows)]
    rotation = jax.random.randint(jax.random.fold_in(own, 2), (rows, 1), 0, top)
    return jnp.take_along_axis(grid, (jnp.arange(top)[None, :] + rotation) % top, axis=1)


def load_shares(number_of, total, limit, skew, full):
    portions = [(1 << 20) // math.isqrt(standing ** skew) + 1 for standing in range(1, number_of + 1)]
    largest = limit if full else min(limit, max(-(-total // number_of), total * portions[0] // sum(portions)))
    least = 1 if total - largest >= number_of - 1 else 0
    counts, spare = [largest] + [least] * (number_of - 1), total - largest - least * (number_of - 1)
    while spare > 0:
        candidates = [i for i in range(1, number_of) if counts[i] < largest] or [i for i in range(1, number_of) if counts[i] < limit]
        pool, budget = sum([portions[i] for i in candidates]), spare
        for i in candidates:
            extra = min(limit - counts[i], max(1, budget * portions[i] // pool), spare)
            counts[i] = counts[i] + extra
            spare = spare - extra
    return np.array(counts)


def normal_values(stream_key, dims, deviation, most, pieces=(), held_as=jnp.bfloat16):
    result = jax.random.normal(stream_key, dims, jnp.float32) * deviation
    if len(pieces) > 0:
        result = shard_levels(stream_key, dims, pieces, -0.22, 0.18) * result
    return jnp.clip(result, min=-most, max=most).astype(held_as)


def setup_inputs(seed: int = 0) -> dict:
    splits = jax.random.split(jax.random.key(seed), 17)
    layer_input = normal_values(splits[0], (TOKENS, MODEL_DIM), 1.0, 6.0, ((0, 128),))
    attn_gain = jnp.clip(1.0 + 0.1 * jax.random.normal(splits[1], (MODEL_DIM,), jnp.float32), 0.5, 1.5)
    w_query = normal_values(splits[2], (MODEL_DIM, QUERY_HEADS * HEAD_SIZE), MODEL_DIM ** -0.5, 0.1875, ((0, 32), (1, 4)))
    key_weight = normal_values(splits[3], (MODEL_DIM, KEY_VALUE_HEADS * HEAD_SIZE), MODEL_DIM ** -0.5, 0.1875, ((0, 32), (1, 4)))
    value_weight = normal_values(splits[4], (MODEL_DIM, KEY_VALUE_HEADS * HEAD_SIZE), MODEL_DIM ** -0.5, 0.1875, ((0, 32), (1, 4)))
    w_output = normal_values(splits[5], (QUERY_HEADS * HEAD_SIZE, MODEL_DIM), (HEAD_SIZE // 4) ** -0.5, 1.5, ((0, 32), (1, 4)))
    query_gain = jnp.clip(1.0 + 0.18 * jax.random.normal(splits[6], (HEAD_SIZE,), jnp.float32), 0.1, 1.9)
    key_gain = jnp.clip(1.0 + 0.18 * jax.random.normal(splits[7], (HEAD_SIZE,), jnp.float32), 0.1, 1.9)
    ffn_gain = jnp.clip(1.0 + 0.1 * jax.random.normal(splits[8], (MODEL_DIM,), jnp.float32), 0.5, 1.5)
    router = normal_values(splits[9], (MODEL_DIM, EXPERTS), (4 * MODEL_DIM) ** -0.5, 0.09375, (), jnp.float32)
    w_gate = normal_values(splits[10], (EXPERTS, MODEL_DIM, FF), MODEL_DIM ** -0.5, 0.1875, ((0, 32),))
    w_up = normal_values(splits[11], (EXPERTS, MODEL_DIM, FF), MODEL_DIM ** -0.5, 0.1875, ((0, 32),))
    w_down = normal_values(splits[12], (EXPERTS, FF, MODEL_DIM), (FF // 16) ** -0.5, 1.0, ((0, 32),))
    routes_keys = jax.random.split(jax.random.fold_in(splits[13], 1), TOKENS // TOK_DEV)
    routes_turns = jax.random.permutation(jax.random.fold_in(splits[13], 3), TOKENS // TOK_DEV)
    routes = jax.vmap(lambda own, number: assign_block(jax.random.fold_in(splits[13], 2), own, number, TOK_DEV, EXPERTS, TOPK, CAP, 1))(routes_keys, routes_turns).reshape((TOKENS, TOPK))
    doc_lengths = draw_doc_lengths(jax.random.fold_in(splits[16], 71), 0)
    cotangent = normal_values(splits[15], (TOKENS, MODEL_DIM), 1.0, 6.0, ((0, 128),))
    return {"layer_input": layer_input, "attn_gain": attn_gain, "w_query": w_query, "key_weight": key_weight, "value_weight": value_weight, "w_output": w_output, "query_gain": query_gain, "key_gain": key_gain, "ffn_gain": ffn_gain, "router": router, "w_gate": w_gate, "w_up": w_up, "w_down": w_down, "routes": routes, "doc_lengths": doc_lengths, "cotangent": cotangent}


EPSILON = 1e-06
ROPE_BASE = 10000.0
PRECISE = lax.Precision.HIGHEST

@jax.custom_vjp
def low(v):
    return lax.optimization_barrier(v.astype(jnp.bfloat16)).astype(jnp.float32)

@jax.custom_vjp
def low_back(v):
    return v

def low_keep(v):
    return (low(v), None)

def low_pass(kept, grad):
    return (grad,)

def back_keep(v):
    return (v, None)

def back_low(kept, grad):
    return (low(grad),)
low.defvjp(low_keep, low_pass)
low_back.defvjp(back_keep, back_low)

def rms_scale(values, gain_row):
    return values * lax.rsqrt(lax.optimization_barrier(jnp.mean(values * values, axis=-1, keepdims=True)) + EPSILON) * gain_row

def position_tables(where_at, doc_lengths):
    endings = jnp.cumsum(doc_lengths).astype(jnp.int32)
    openings = (endings - doc_lengths).astype(jnp.int32)
    document = lax.optimization_barrier(jnp.sum((where_at[:, None] >= endings[None, :]).astype(jnp.int32), axis=1))
    numbers = jnp.arange(doc_lengths.shape[0], dtype=jnp.int32)
    opening = lax.optimization_barrier(jnp.sum(jnp.where(document[:, None] == numbers[None, :], openings[None, :], 0), axis=1)).astype(jnp.int32)
    inside = (where_at - opening).astype(jnp.int32)
    return (document, inside, inside // BLOCK)

def rotary(values, inside):
    half_dim = values.shape[-1] // 2
    frequency = jnp.power(ROPE_BASE, -2.0 * jnp.arange(half_dim, dtype=jnp.float32) / values.shape[-1])
    angles = inside.astype(jnp.float32)[:, None] * frequency[None, :]
    cosine_table = jnp.cos(angles)[:, None, :]
    sine_table = jnp.sin(angles)[:, None, :]
    first_half = values[..., :half_dim]
    second_half = values[..., half_dim:]
    return jnp.concatenate([first_half * cosine_table - second_half * sine_table, second_half * cosine_table + first_half * sine_table], axis=-1)

def head_prep(raw_heads, gain_row, inside):
    count_of_tokens = raw_heads.shape[0]
    split_heads = raw_heads.reshape(count_of_tokens, raw_heads.shape[1] // HEAD_SIZE, HEAD_SIZE)
    return rotary(rms_scale(split_heads, gain_row), inside).reshape(count_of_tokens, raw_heads.shape[1])

def attention(query_row_matrix, key_row_matrix, value_row_matrix, document, block_at):
    row_total = query_row_matrix.shape[0]
    block_extent = math.gcd(row_total, 512)
    group_factor = QUERY_HEADS // KEY_VALUE_HEADS
    scaling = HEAD_SIZE ** (-0.5)
    query_block_list = query_row_matrix.reshape(row_total // block_extent, block_extent, KEY_VALUE_HEADS, group_factor, HEAD_SIZE).transpose(0, 2, 1, 3, 4)
    key_head_split = key_row_matrix.reshape(row_total, KEY_VALUE_HEADS, HEAD_SIZE).transpose(1, 0, 2)
    value_head_split = value_row_matrix.reshape(row_total, KEY_VALUE_HEADS, HEAD_SIZE).transpose(1, 0, 2)
    doc_blocks = document.reshape(row_total // block_extent, block_extent)
    order_blocks = block_at.reshape(row_total // block_extent, block_extent)

    def one_block(block_item):
        query_part, doc_part, order_part = block_item
        allowed = (doc_part[:, None] == document[None, :]) & (block_at[None, :] <= order_part[:, None])

        def one_head(head_item):
            query_head, key_head, value_head = head_item
            raw_scores = jnp.einsum('sgd,kd->gsk', query_head, key_head, precision=PRECISE)
            scores = low_back(raw_scores * scaling)
            exponent = jnp.where(allowed[None], jnp.exp(scores), 0.0)
            totals = lax.optimization_barrier(jnp.sum(exponent, axis=-1, keepdims=True))
            numerator = low_back(jnp.einsum('gsk,kd->gsd', low(exponent), value_head, precision=PRECISE))
            return numerator / totals
        outputs = lax.map(jax.checkpoint(one_head), (query_part, key_head_split, value_head_split))
        return outputs.transpose(2, 0, 1, 3).reshape(block_extent, QUERY_HEADS * HEAD_SIZE)
    blocks_out = lax.map(jax.checkpoint(one_block), (query_block_list, doc_blocks, order_blocks))
    return blocks_out.reshape(row_total, QUERY_HEADS * HEAD_SIZE)

def slot_tables(routes):
    sources = routes.shape[0] // TOK_DEV
    picked_ids = routes.reshape(sources, TOK_DEV * TOPK)
    numbers = jnp.arange(EXPERTS, dtype=jnp.int32)
    hit_table = (picked_ids[:, :, None] == numbers[None, None, :]).astype(jnp.int32)
    placed = (lax.optimization_barrier(jnp.sum(jnp.cumsum(hit_table, axis=1) * hit_table, axis=2)) - 1).astype(jnp.int32)
    source_ids = jnp.broadcast_to(jnp.arange(sources, dtype=jnp.int32)[:, None], picked_ids.shape)
    flat_rows = jnp.broadcast_to(jnp.arange(TOK_DEV * TOPK, dtype=jnp.int32)[None, :], picked_ids.shape)
    owners = (source_ids * TOK_DEV + flat_rows // TOPK).astype(jnp.int32)
    owner_table = jnp.zeros((EXPERTS, sources, CAP), jnp.int32).at[picked_ids, source_ids, placed].set(owners)
    live_table = jnp.zeros((EXPERTS, sources, CAP), jnp.float32).at[picked_ids, source_ids, placed].set(1.0)
    slot_of = ((picked_ids * sources + source_ids) * CAP + placed).astype(jnp.int32)
    return (owner_table.reshape(EXPERTS, sources * CAP), live_table.reshape(EXPERTS, sources * CAP), slot_of.reshape(routes.shape[0], TOPK))

def layer(source, attn_gain, w_query, key_weight, value_weight, w_output, query_gain, key_gain, ffn_gain, router, w_gate, w_up, w_down, tables):
    routes, document, inside, block_at, owner_table, live_table, slot_of = tables
    normed = low(rms_scale(source, attn_gain))
    query_raw = low_back(jnp.dot(normed, w_query, precision=PRECISE))
    key_raw = low_back(jnp.dot(normed, key_weight, precision=PRECISE))
    value_raw = jnp.dot(normed, value_weight, precision=PRECISE)
    query_row_matrix = low(low_back(head_prep(query_raw, query_gain, inside)))
    key_row_matrix = low(low_back(head_prep(key_raw, key_gain, inside)))
    value_row_matrix = low(low_back(value_raw))
    context = low(low_back(attention(query_row_matrix, key_row_matrix, value_row_matrix, document, block_at)))
    middle = source + low_back(jnp.dot(context, w_output, precision=PRECISE))
    mixed_in = low(rms_scale(middle, ffn_gain))
    logits = jnp.dot(mixed_in, router, precision=PRECISE)
    picked = jnp.take_along_axis(logits, routes, axis=1)
    gates = jax.nn.softmax(picked, axis=1)

    def one_expert(expert_item):
        owners, live_rows, gate_weight, up_weight, down_weight = expert_item
        rows_in = mixed_in[owners] * live_rows[:, None]
        gate_pre = low_back(jnp.dot(rows_in, gate_weight, precision=PRECISE))
        up_pre = low_back(jnp.dot(rows_in, up_weight, precision=PRECISE))
        hidden = low(jax.nn.silu(gate_pre) * up_pre)
        return low(low_back(jnp.dot(hidden, down_weight, precision=PRECISE)))
    expert_out = lax.map(jax.checkpoint(one_expert), (owner_table, live_table, w_gate, w_up, w_down))
    flat_out = expert_out.reshape(-1, expert_out.shape[-1])
    mixture = jnp.zeros_like(middle)
    for pick_index in range(TOPK):
        mixture = mixture + gates[:, pick_index:pick_index + 1] * flat_out[slot_of[:, pick_index]]
    return middle + mixture

def reference(layer_input, attn_gain, w_query, key_weight, value_weight, w_output, query_gain, key_gain, ffn_gain, router, w_gate, w_up, w_down, routes, doc_lengths, cotangent):
    document, inside, block_at = position_tables(jnp.arange(TOKENS, dtype=jnp.int32), doc_lengths)
    owner_table, live_table, slot_of = slot_tables(routes)
    tables = (routes, document, inside, block_at, owner_table, live_table, slot_of)
    output, pullback = jax.vjp(functools.partial(layer, tables=tables), layer_input.astype(jnp.float32), attn_gain, w_query.astype(jnp.float32), key_weight.astype(jnp.float32), value_weight.astype(jnp.float32), w_output.astype(jnp.float32), query_gain, key_gain, ffn_gain, router, w_gate.astype(jnp.float32), w_up.astype(jnp.float32), w_down.astype(jnp.float32))
    gradients = pullback(cotangent.astype(jnp.float32))
    return (output.astype(jnp.bfloat16), gradients[0].astype(jnp.bfloat16), gradients[1], gradients[2], gradients[3], gradients[4], gradients[5], gradients[6], gradients[7], gradients[8], gradients[9], gradients[10], gradients[11], gradients[12])
```

```python
import functools

import jax
import jax.numpy as jnp
from jax import lax
from jax.experimental import pallas as pl
from jax.experimental.pallas import tpu as pltpu
from jax.sharding import PartitionSpec as P

HEAD_SIZE = 64
TOPK = 8
BLOCK = 256
EPSILON = 1e-06
ROPE_BASE = 10000.0
PRECISE = lax.Precision.HIGHEST
SCALE = HEAD_SIZE ** (-0.5)

NB = 32
GROUP = 4
MESH_ID = pl.DeviceIdType.MESH
F32 = jnp.float32
BF16 = jnp.bfloat16
NT = (((1,), (1,)), ((), ()))
NN = (((1,), (0,)), ((), ()))
TN = (((0,), (0,)), ((), ()))


def place():
    b = lax.axis_index("blk")
    h = lax.axis_index("head")
    y = b // 8
    r = lax.rem(b, 8)
    m = jnp.where(lax.rem(y, 2) == 0, r, 7 - r)
    return b, h // 2, lax.rem(h, 2), y, m


def member(m, j):
    return 8 * j + m + lax.rem(j, 2) * (7 - 2 * m)


def times(start, n, body):
    def step(i, carry):
        body(i)
        return carry

    lax.fori_loop(start, n, step, 0)


def signal(sem, blk, head):
    pl.semaphore_signal(sem, inc=1, device_id=(blk, head), device_id_type=MESH_ID)


def rows(start, size):
    return pl.ds(pl.multiple_of(start, size), size)


def exchange(kernel, collective_id, out_shapes, sems, *operands):
    anyspec = pl.BlockSpec(memory_space=pl.ANY)
    return pl.pallas_call(
        kernel,
        out_shape=out_shapes,
        in_specs=[anyspec] * len(operands),
        out_specs=[anyspec] * len(out_shapes),
        scratch_shapes=[pltpu.SemaphoreType.DMA(s) for s in sems],
        compiler_params=pltpu.CompilerParams(collective_id=collective_id, has_side_effects=True),
    )(*operands)


def to(src, dst, send, recv, blk, head):
    return pltpu.make_async_remote_copy(
        src, dst, send, recv, device_id=(blk, head), device_id_type=MESH_ID
    )


def weights_kernel(ws, wo, li, w_out, wo_out, li_out, s1, r1, s2, r2, s3, r3, s4, r4, sx, rx, ls):
    b, xl, c, _, _ = place()
    h = 2 * xl + c
    sib = 2 * xl + 1 - c
    over = 2 * (1 - xl) + c
    bar = pltpu.get_barrier_semaphore()
    times(1, NB, lambda d: signal(bar, lax.rem(b + d, NB), h))
    times(0, NB, lambda d: signal(bar, lax.rem(b + d, NB), over))
    signal(bar, b, sib)
    pl.semaphore_wait(bar, 2 * NB)

    def first(d):
        return to(ws, w_out.at[c, rows(b * 32, 32)], s1.at[d], r1.at[d], lax.rem(b + d, NB), h)

    def second(d):
        src = lax.rem(b + NB - d, NB)
        part = w_out.at[c, rows(src * 32, 32)]
        return to(part, part, s2.at[d], r2.at[d], b, sib)

    def third(e):
        d, x2 = lax.rem(e, NB), lax.rem(xl + e // NB, 2)
        part = wo_out.at[h, rows(b * 32, 32)]
        return to(wo, part, s3.at[e], r3.at[e], lax.rem(b + d, NB), 2 * x2 + c)

    def fourth(e):
        d, x2 = lax.rem(e, NB), lax.rem(xl + e // NB, 2)
        part = wo_out.at[2 * x2 + c, rows(lax.rem(b + NB - d, NB) * 32, 32)]
        return to(part, part, s4.at[e], r4.at[e], b, sib)

    cross = to(li, li_out.at[xl], sx, rx, b, over)
    cross.start()
    times(1, NB, lambda d: first(d).start())
    times(1, 2 * NB, lambda e: third(e).start())
    own_w = pltpu.make_async_copy(ws, w_out.at[c, rows(b * 32, 32)], ls.at[0])
    own_w.start()
    own_li = pltpu.make_async_copy(li, li_out.at[xl], ls.at[1])
    own_li.start()
    own_wo = pltpu.make_async_copy(wo, wo_out.at[h, rows(b * 32, 32)], ls.at[2])
    own_wo.start()
    to_sib = to(ws, w_out.at[c, rows(b * 32, 32)], s2.at[0], r2.at[0], b, sib)
    to_sib.start()
    wo_sib = to(wo, wo_out.at[h, rows(b * 32, 32)], s4.at[0], r4.at[0], b, sib)
    wo_sib.start()

    def relay(d):
        first(d).wait_recv()
        second(d).start()

    def relay_wo(e):
        third(e).wait_recv()
        fourth(e).start()

    times(1, NB, relay)
    times(1, 2 * NB, relay_wo)
    times(1, NB, lambda d: first(d).wait_send())
    times(1, 2 * NB, lambda e: third(e).wait_send())
    to_sib.wait()
    wo_sib.wait()
    times(1, NB, lambda d: second(d).wait())
    times(1, 2 * NB, lambda e: fourth(e).wait())
    cross.wait()
    own_w.wait()
    own_li.wait()
    own_wo.wait()


def qkv_kernel(q, kv, q_out, kv_out, s1, r1, s2, r2, ls):
    b, xl, c, y, m = place()
    h = 2 * xl + c
    bar = pltpu.get_barrier_semaphore()
    times(1, NB, lambda d: signal(bar, lax.rem(b + d, NB), h))
    for dj in range(GROUP):
        signal(bar, member(m, lax.rem(y + dj, GROUP)), 2 * xl + 1 - c)
    pl.semaphore_wait(bar, NB - 1 + GROUP)

    def big(d):
        peer = lax.rem(b + d, NB)
        cols = pl.ds(pl.multiple_of((peer // 8) * 128, 128), 128)
        return to(kv.at[:, cols], kv_out.at[b], s1.at[d], r1.at[d], peer, h)

    def small(dj, dc):
        j = lax.rem(y + dj, GROUP)
        c2 = lax.rem(c + dc, 2)
        cols = pl.ds(pl.multiple_of(j * 128, 128), 128)
        k = 2 * dj + dc
        src, dst = q.at[:, cols], q_out.at[y, rows(c * 256, 256)]
        if k == 0:
            return pltpu.make_async_copy(src, dst, ls.at[0])
        return to(src, dst, s2.at[k], r2.at[k], member(m, j), 2 * xl + c2)

    smalls = [small(dj, dc) for dj in range(GROUP) for dc in range(2)]
    for item in smalls:
        item.start()
    own_cols = pl.ds(pl.multiple_of(y * 128, 128), 128)
    own = pltpu.make_async_copy(kv.at[:, own_cols], kv_out.at[b], ls.at[1])
    own.start()
    times(1, NB, lambda d: big(d).start())
    for item in smalls:
        item.wait()
    own.wait()
    times(1, NB, lambda d: big(d).wait())


def context_kernel(ctx, out, s1, r1, ls):
    b, xl, c, y, m = place()
    bar = pltpu.get_barrier_semaphore()

    def copies(make):
        done = []
        for dj in range(GROUP):
            for dx in range(2):
                done.append(make(dj, dx))
        return done

    def greet(dj, dx):
        if dj + dx > 0:
            x2 = lax.rem(xl + dx, 2)
            signal(bar, member(m, lax.rem(y + dj, GROUP)), 2 * x2 + c)

    copies(greet)
    pl.semaphore_wait(bar, 2 * GROUP - 1)

    def piece(dj, dx):
        j = lax.rem(y + dj, GROUP)
        x2 = lax.rem(xl + dx, 2)
        cols = pl.ds(pl.multiple_of((4 * xl + y) * 128, 128), 128)
        src, dst = ctx.at[j, rows(c * 256 + x2 * 128, 128)], out.at[:, cols]
        k = 2 * dj + dx
        if k == 0:
            return pltpu.make_async_copy(src, dst, ls)
        return to(src, dst, s1.at[k], r1.at[k], member(m, j), 2 * x2 + c)

    parts = copies(piece)
    for item in parts:
        item.start()
    for item in parts:
        item.wait()


def context_grad_kernel(cg, out, s1, r1, ls):
    b, xl, c, y, m = place()
    bar = pltpu.get_barrier_semaphore()
    turns = [(dj, dx, dc) for dj in range(GROUP) for dx in range(2) for dc in range(2)]

    def where(dj, dx, dc):
        j = lax.rem(y + dj, GROUP)
        x2 = lax.rem(xl + dx, 2)
        return j, x2, member(m, j), 2 * x2 + lax.rem(c + dc, 2)

    for turn in turns[1:]:
        _, _, blk, head = where(*turn)
        signal(bar, blk, head)
    pl.semaphore_wait(bar, len(turns) - 1)

    parts = []
    for k, turn in enumerate(turns):
        j, x2, blk, head = where(*turn)
        cols = pl.ds(pl.multiple_of((4 * x2 + j) * 128, 128), 128)
        src, dst = cg.at[:, cols], out.at[y, rows(c * 256 + xl * 128, 128)]
        if k == 0:
            parts.append(pltpu.make_async_copy(src, dst, ls))
        else:
            parts.append(to(src, dst, s1.at[k], r1.at[k], blk, head))
    for item in parts:
        item.start()
    for item in parts:
        item.wait()


def qkv_grad_kernel(dq, dkv, dq_out, dkv_out, s1, r1, s2, r2, ls):
    b, xl, c, y, m = place()
    h = 2 * xl + c
    bar = pltpu.get_barrier_semaphore()
    times(1, NB, lambda d: signal(bar, lax.rem(b + d, NB), h))
    for dj in range(GROUP):
        signal(bar, member(m, lax.rem(y + dj, GROUP)), 2 * xl + 1 - c)
    pl.semaphore_wait(bar, NB - 1 + GROUP)

    def big(d):
        peer = lax.rem(b + d, NB)
        return to(dkv.at[peer], dkv_out.at[b], s1.at[d], r1.at[d], peer, h)

    def small(dj, dc):
        j = lax.rem(y + dj, GROUP)
        c2 = lax.rem(c + dc, 2)
        cols = pl.ds(pl.multiple_of(y * 128, 128), 128)
        src, dst = dq.at[j, rows(c2 * 256, 256)], dq_out.at[c, :, cols]
        k = 2 * dj + dc
        if k == 0:
            return pltpu.make_async_copy(src, dst, ls.at[0])
        return to(src, dst, s2.at[k], r2.at[k], member(m, j), 2 * xl + c2)

    smalls = [small(dj, dc) for dj in range(GROUP) for dc in range(2)]
    for item in smalls:
        item.start()
    own = pltpu.make_async_copy(dkv.at[b], dkv_out.at[b], ls.at[1])
    own.start()
    times(1, NB, lambda d: big(d).start())
    for item in smalls:
        item.wait()
    own.wait()
    times(1, NB, lambda d: big(d).wait())


def scatter_kernel(parts, out, s1, r1, ls):
    b, xl, c, _, _ = place()
    h = 2 * xl + c
    bar = pltpu.get_barrier_semaphore()
    times(1, NB, lambda d: signal(bar, lax.rem(b + d, NB), h))
    pl.semaphore_wait(bar, NB - 1)

    def big(d):
        peer = lax.rem(b + d, NB)
        return to(parts.at[peer], out.at[b], s1.at[d], r1.at[d], peer, h)

    own = pltpu.make_async_copy(parts.at[b], out.at[b], ls)
    own.start()
    times(1, NB, lambda d: big(d).start())
    own.wait()
    times(1, NB, lambda d: big(d).wait())


def small_sum_kernel(x, out, four, many, s1, r1, s2, r2):
    b = lax.axis_index("blk")
    h = lax.axis_index("head")
    bar = pltpu.get_barrier_semaphore()
    for d in range(1, 4):
        signal(bar, b, lax.rem(h + d, 4))
    times(1, NB, lambda d: signal(bar, lax.rem(b + d, NB), h))
    pl.semaphore_wait(bar, NB + 2)
    four[h] = x[...]
    near = [
        to(x, four.at[h], s1.at[d], r1.at[d], b, lax.rem(h + d, 4)) for d in range(1, 4)
    ]
    for item in near:
        item.start()
    for item in near:
        item.wait()
    many[b] = four[0] + four[1] + four[2] + four[3]

    def far(d):
        return to(many.at[b], many.at[b], s2.at[d], r2.at[d], lax.rem(b + d, NB), h)

    times(1, NB, lambda d: far(d).start())
    times(1, NB, lambda d: far(d).wait())
    total = many[0]
    for i in range(1, NB):
        total = total + many[i]
    out[...] = total


def small_sum(x):
    vm = pl.BlockSpec(memory_space=pltpu.VMEM)
    dma = pltpu.SemaphoreType.DMA
    return pl.pallas_call(
        small_sum_kernel,
        out_shape=jax.ShapeDtypeStruct(x.shape, x.dtype),
        in_specs=[vm],
        out_specs=vm,
        scratch_shapes=[
            pltpu.VMEM((4,) + x.shape, x.dtype),
            pltpu.VMEM((NB,) + x.shape, x.dtype),
            dma((4,)),
            dma((4,)),
            dma((NB,)),
            dma((NB,)),
        ],
        compiler_params=pltpu.CompilerParams(collective_id=6, has_side_effects=True),
    )(x)


def limits(pos, e0, e1, total):
    low = jnp.where(pos < e0, 0, jnp.where(pos < e1, e0, e1))
    end = jnp.where(pos < e0, e0, jnp.where(pos < e1, e1, total))
    reach = low + ((pos - low) // BLOCK + 1) * BLOCK
    return low, jnp.minimum(end, reach)


def query_positions(shape, axis, qb):
    r = lax.broadcasted_iota(jnp.int32, shape, axis)
    r = lax.rem(r, 512)
    return 512 * qb + 256 * lax.rem(r // 128, 2) + 128 * (r // 256) + lax.rem(r, 128)


def key_positions(shape, axis, kb, core):
    r = lax.broadcasted_iota(jnp.int32, shape, axis)
    return 512 * kb + 256 * (r // 128) + 128 * core + lax.rem(r, 128)


def over_keys(info, i, body):
    e0, e1, total, core = info[0], info[1], info[2], info[3]
    qb = info[4 + i]
    first_low, first_high = limits(512 * qb, e0, e1, total)
    last_low, last_high = limits(512 * qb + 511, e0, e1, total)

    def step(kb, carry):
        start = 512 * kb
        reached = last_high > start + 128 * core
        whole = (last_low <= start) & (first_high > start + 511)
        pl.when(whole)(lambda: body(kb, False))
        pl.when(reached & jnp.logical_not(whole))(lambda: body(kb, True))
        return carry

    lax.fori_loop(0, jnp.minimum(qb + 2, NB), step, 0)


def forward_kernel(info, q_ref, kv_ref, out_ref, qp, vx, acc):
    e0, e1, total, core = info[0], info[1], info[2], info[3]
    left = lax.broadcasted_iota(jnp.int32, (256, 128), 1) < 64
    left_q = lax.broadcasted_iota(jnp.int32, (512, 128), 1) < 64

    def ones(kb, carry):
        vx[kb] = jnp.where(left, 1.0, kv_ref[kb].astype(F32)).astype(BF16)
        return carry

    lax.fori_loop(0, NB, ones, 0)
    for i in range(GROUP):
        qb = info[4 + i]
        both = q_ref[i].astype(F32)
        qp[0:512] = jnp.where(left_q, both, 0.0).astype(BF16)
        qp[512:1024] = jnp.where(left_q, pltpu.roll(both, 64, 1), 0.0).astype(BF16)
        acc[...] = jnp.zeros_like(acc)

        def body(kb, masked):
            keys = kv_ref[kb]
            scores = lax.dot_general(qp[...], keys, NT, preferred_element_type=F32)
            expo = jnp.exp(scores)
            if masked:
                low, high = limits(query_positions((1024, 1), 0, qb), e0, e1, total)
                kpos = key_positions((1, 256), 1, kb, core)
                expo = jnp.where((kpos >= low) & (kpos < high), expo, 0.0)
            acc[...] += jnp.dot(expo.astype(BF16), vx[kb], preferred_element_type=F32)

        over_keys(info, i, body)
        out_ref[i, 0] = acc[0:512]
        out_ref[i, 1] = acc[512:1024]


def combine_kernel(a_ref, b_ref, ctx_ref, wide_ref, inv_ref):
    left = lax.broadcasted_iota(jnp.int32, (512, 128), 1) < 64
    for i in range(GROUP):
        one = a_ref[i, 0] + b_ref[i, 0]
        two = a_ref[i, 1] + b_ref[i, 1]
        totals = jnp.where(left, one, pltpu.roll(two, 64, 1))
        numer = jnp.where(left, pltpu.roll(one, 64, 1), two)
        wide = numer / totals
        wide_ref[i] = wide
        inv_ref[i] = 1.0 / totals
        ctx_ref[i] = wide.astype(BF16)


def backward_kernel(info, q_ref, kv_ref, cg_ref, wide_ref, inv_ref, dq_ref, dkv_ref, qp, gp, kt, dot_ref, dq_acc, dkv_acc):
    e0, e1, total, core = info[0], info[1], info[2], info[3]
    left_q = lax.broadcasted_iota(jnp.int32, (512, 128), 1) < 64

    def prepare(kb, carry):
        kt[kb] = kv_ref[kb].astype(F32).T[0:64].astype(BF16)
        dkv_acc[kb] = jnp.zeros((256, 128), F32)
        return carry

    lax.fori_loop(0, NB, prepare, 0)
    for i in range(GROUP):
        qb = info[4 + i]
        both = q_ref[i].astype(F32)
        qp[0:512] = jnp.where(left_q, both, 0.0).astype(BF16)
        qp[512:1024] = jnp.where(left_q, pltpu.roll(both, 64, 1), 0.0).astype(BF16)
        grad = cg_ref[i].astype(F32)
        inv = inv_ref[i]
        scaled = grad * inv
        gp[0:512] = jnp.where(left_q, 0.0, pltpu.roll(scaled, 64, 1)).astype(BF16)
        gp[512:1024] = jnp.where(left_q, 0.0, scaled).astype(BF16)
        terms = (scaled * wide_ref[i]).T
        dot_ref[:, 0:512] = jnp.sum(terms[0:64], axis=0, keepdims=True)
        dot_ref[:, 512:1024] = jnp.sum(terms[64:128], axis=0, keepdims=True)
        dq_acc[...] = jnp.zeros_like(dq_acc)

        def body(kb, masked):
            keys = kv_ref[kb]
            scores = lax.dot_general(keys, qp[...], NT, preferred_element_type=F32)
            expo = jnp.exp(scores)
            if masked:
                low, high = limits(query_positions((1, 1024), 1, qb), e0, e1, total)
                kpos = key_positions((256, 1), 0, kb, core)
                expo = jnp.where((kpos >= low) & (kpos < high), expo, 0.0)
            prob = lax.dot_general(keys, gp[...], NT, preferred_element_type=F32)
            score_grad = (expo * (prob - dot_ref[...])).astype(BF16)
            dkv_acc[kb] += jnp.dot(score_grad, qp[...], preferred_element_type=F32) + jnp.dot(
                expo.astype(BF16), gp[...], preferred_element_type=F32
            )
            dq_acc[...] += jnp.dot(kt[kb], score_grad, preferred_element_type=F32)

        over_keys(info, i, body)
        flat = jnp.concatenate([dq_acc[:, 0:512], dq_acc[:, 512:1024]], axis=0)
        dq_ref[i] = (flat.T * SCALE).astype(BF16)

    def finish(kb, carry):
        dkv_ref[kb] = dkv_acc[kb].astype(BF16)
        return carry

    lax.fori_loop(0, NB, finish, 0)


VM = pl.BlockSpec(memory_space=pltpu.VMEM)
SM = pl.BlockSpec(memory_space=pltpu.SMEM)
BIG = pltpu.CompilerParams(vmem_limit_bytes=56 * 1024 * 1024)


def cost(flops, size, exps):
    return pl.CostEstimate(flops=flops, bytes_accessed=size, transcendentals=exps)


def attend(info, q, kv):
    return pl.pallas_call(
        forward_kernel,
        out_shape=jax.ShapeDtypeStruct((GROUP, 2, 512, 128), F32),
        in_specs=[SM, VM, VM],
        out_specs=VM,
        scratch_shapes=[
            pltpu.VMEM((1024, 128), BF16),
            pltpu.VMEM((NB, 256, 128), BF16),
            pltpu.VMEM((1024, 128), F32),
        ],
        compiler_params=BIG,
        cost_estimate=cost(18_000_000_000, 6_000_000, 18_000_000),
    )(info, q, kv)


def combine(a, b):
    return pl.pallas_call(
        combine_kernel,
        out_shape=(
            jax.ShapeDtypeStruct((GROUP, 512, 128), BF16),
            jax.ShapeDtypeStruct((GROUP, 512, 128), F32),
            jax.ShapeDtypeStruct((GROUP, 512, 128), F32),
        ),
        in_specs=[VM, VM],
        out_specs=(VM, VM, VM),
        compiler_params=BIG,
    )(a, b)


def attend_back(info, q, kv, cg, wide, inv):
    return pl.pallas_call(
        backward_kernel,
        out_shape=(
            jax.ShapeDtypeStruct((GROUP, 512, 128), BF16),
            jax.ShapeDtypeStruct((NB, 256, 128), BF16),
        ),
        in_specs=[SM] + [VM] * 5,
        out_specs=(VM, VM),
        scratch_shapes=[
            pltpu.VMEM((1024, 128), BF16),
            pltpu.VMEM((1024, 128), BF16),
            pltpu.VMEM((NB, 64, 256), BF16),
            pltpu.VMEM((1, 1024), F32),
            pltpu.VMEM((64, 1024), F32),
            pltpu.VMEM((NB, 256, 128), F32),
        ],
        compiler_params=BIG,
        cost_estimate=cost(45_000_000_000, 8_000_000, 18_000_000),
    )(info, q, kv, cg, wide, inv)


def rms_scale(values, gain_row):
    return (
        values * lax.rsqrt(jnp.mean(values * values, axis=-1, keepdims=True) + EPSILON) * gain_row
    )


def rotary(values, inside):
    half = values.shape[-1] // 2
    frequency = jnp.power(ROPE_BASE, -2.0 * jnp.arange(half, dtype=F32) / values.shape[-1])
    angles = inside.astype(F32)[:, None] * frequency[None, :]
    cosine, sine = jnp.cos(angles)[:, None, :], jnp.sin(angles)[:, None, :]
    first, second = values[..., :half], values[..., half:]
    return jnp.concatenate(
        [first * cosine - second * sine, second * cosine + first * sine], axis=-1
    )


def head_prep(raw_heads, gain_row, inside):
    return rotary(rms_scale(raw_heads, gain_row), inside)


def from_head(value, bit):
    return lax.ppermute(value, "head", [(i, i ^ bit) for i in range(4)])


def body(
    layer_input,
    attn_gain,
    w_query,
    key_weight,
    value_weight,
    w_output,
    query_gain,
    key_gain,
    ffn_gain,
    router,
    w_gate,
    w_up,
    w_down,
    routes,
    doc_lengths,
    cotangent,
):
    b, xl, c, y, m = place()
    tokens, width = layer_input.shape
    total = tokens * 4 * NB
    experts = NB
    capacity = min(tokens, 5 * tokens * TOPK // (4 * experts))
    ends = jnp.cumsum(doc_lengths)
    info = jnp.stack(
        [ends[0], ends[1], jnp.int32(total), c] + [member(m, jnp.int32(j)) for j in range(GROUP)]
    ).astype(jnp.int32)

    chosen = jnp.any(routes[:, :, None] == jnp.arange(experts, dtype=jnp.int32), axis=1)
    before = jnp.tril(jnp.ones((tokens, tokens), BF16), -1)
    rank = jnp.dot(before, chosen.astype(BF16), preferred_element_type=F32).astype(jnp.int32)
    slot = jnp.arange(capacity, dtype=jnp.int32)
    at_slot = chosen.T[:, None, :] & (rank.T[:, None, :] == slot[None, :, None])
    pick = at_slot.astype(BF16).reshape(experts * capacity, tokens)

    def to_experts(value):
        return lax.all_to_all(value, "blk", split_axis=0, concat_axis=0, tiled=True)

    def dispatch(value):
        picked = jnp.dot(pick, value, preferred_element_type=F32).astype(BF16)
        return to_experts(picked.reshape(experts, capacity, width))

    shard = jnp.concatenate(
        [
            w_query,
            key_weight[:, :64],
            value_weight[:, :64],
            key_weight[:, 64:],
            value_weight[:, 64:],
        ],
        axis=1,
    )
    w_full, out_full, both_inputs = exchange(
        weights_kernel,
        0,
        [
            jax.ShapeDtypeStruct((2, width, 512), BF16),
            jax.ShapeDtypeStruct((4, width, width // 4), BF16),
            jax.ShapeDtypeStruct((2, tokens, width), BF16),
        ],
        [(NB,)] * 4 + [(2 * NB,)] * 4 + [(), (), (3,)],
        shard,
        w_output,
        layer_input,
    )
    source2 = both_inputs.reshape(2 * tokens, width).astype(F32)
    normed_wide, attn_pull = jax.vjp(rms_scale, source2, attn_gain)
    normed = normed_wide.astype(BF16)
    raw = [jnp.dot(normed, w_full[i], preferred_element_type=F32) for i in range(2)]
    query_raw = jnp.concatenate([raw[0][:, :256], raw[1][:, :256]], axis=1).reshape(-1, 8, 64)
    kv_raw = jnp.concatenate([raw[0][:, 256:], raw[1][:, 256:]], axis=1).reshape(-1, 4, 2, 64)
    t = jnp.arange(2 * tokens, dtype=jnp.int32)
    pos = 512 * b + 256 * (t // 128) + 128 * c + t % 128
    opening = jnp.where(pos < ends[0], 0, jnp.where(pos < ends[1], ends[0], ends[1]))
    inside = pos - opening
    prep = functools.partial(head_prep, inside=inside)
    query_prep, query_pull = jax.vjp(prep, query_raw, query_gain)
    key_prep, key_pull = jax.vjp(prep, kv_raw[:, :, 0], key_gain)
    query = (query_prep.astype(BF16) * SCALE).astype(BF16).reshape(2 * tokens, 512)
    keyval = (
        jnp.stack([key_prep, kv_raw[:, :, 1]], axis=2).astype(BF16).reshape(2 * tokens, 512)
    )
    q_group, kv_all = exchange(
        qkv_kernel,
        1,
        [
            jax.ShapeDtypeStruct((GROUP, 512, 128), BF16),
            jax.ShapeDtypeStruct((NB, 256, 128), BF16),
        ],
        [(NB,), (NB,), (8,), (8,), (2,)],
        query,
        keyval,
    )
    late_cotangent, _ = lax.optimization_barrier((cotangent, q_group))
    up_rows = dispatch(late_cotangent).reshape(experts * capacity, width)
    partial = attend(info, q_group, kv_all)
    ctx, ctx_wide, ctx_inv = combine(partial, from_head(partial, 1))
    (context,) = exchange(
        context_kernel,
        2,
        [jax.ShapeDtypeStruct((tokens, width), BF16)],
        [(8,), (8,), ()],
        ctx,
    )

    source = layer_input.astype(F32)
    projected = [jnp.dot(context, out_full[i], preferred_element_type=F32) for i in range(4)]
    middle = source + jnp.concatenate(projected, axis=1)
    mixed_wide, ffn_pull = jax.vjp(rms_scale, middle, ffn_gain)
    mixed_in = mixed_wide.astype(BF16)
    expert_in = dispatch(mixed_in).reshape(experts * capacity, width)
    logits = jnp.dot(mixed_in.astype(F32), router, precision=PRECISE)
    top = jnp.max(jnp.where(chosen, logits, -jnp.inf), axis=1, keepdims=True)
    weight = jnp.where(chosen, jnp.exp(logits - top), 0.0)
    gates = weight / jnp.sum(weight, axis=1, keepdims=True)
    slot_gates = jnp.where(at_slot, gates.T[:, None, :], 0.0)
    sent_gates = jnp.sum(slot_gates, axis=2)
    gate_rows = to_experts(sent_gates[:, None, :]).reshape(experts * capacity, 1)

    gate_w, up_w, down_w = w_gate[0], w_up[0], w_down[0]
    gate_pre = jnp.dot(expert_in, gate_w, preferred_element_type=F32)
    up_pre = jnp.dot(expert_in, up_w, preferred_element_type=F32)
    sig = jax.nn.sigmoid(gate_pre)
    activated = gate_pre * sig
    hidden = (activated * up_pre).astype(BF16)
    expert_out = jnp.dot(hidden, down_w, preferred_element_type=F32).astype(BF16)
    upstream_rows = up_rows.astype(F32)
    gate_back_rows = jnp.sum(upstream_rows * expert_out.astype(F32), axis=1)
    gate_grad_slots = to_experts(gate_back_rows.reshape(experts, 1, capacity))[:, 0]
    out_grad = (gate_rows * upstream_rows).astype(BF16)
    hidden_grad = lax.dot_general(out_grad, down_w, NT, preferred_element_type=F32)
    gate_back = (hidden_grad * up_pre * sig * (1.0 + gate_pre * (1.0 - sig))).astype(BF16)
    up_back = (hidden_grad * activated).astype(BF16)
    rows_grad = lax.dot_general(
        gate_back, gate_w, NT, preferred_element_type=F32
    ) + lax.dot_general(up_back, up_w, NT, preferred_element_type=F32)
    grads_home = to_experts(rows_grad.astype(BF16).reshape(experts, capacity, width))
    down_w_grad = lax.dot_general(hidden, out_grad, TN, preferred_element_type=F32)
    gate_w_grad = lax.dot_general(expert_in, gate_back, TN, preferred_element_type=F32)
    up_w_grad = lax.dot_general(expert_in, up_back, TN, preferred_element_type=F32)

    gate_grad = jnp.sum(
        jnp.where(at_slot, gate_grad_slots[:, :, None], 0.0), axis=1
    ).T
    logit_grad = gates * (gate_grad - jnp.sum(gates * gate_grad, axis=1, keepdims=True))
    router_grad = jnp.dot(mixed_in.astype(F32).T, logit_grad, precision=PRECISE)
    mixed_grad = lax.dot_general(
        pick, grads_home.reshape(experts * capacity, width), TN, preferred_element_type=F32
    ) + jnp.dot(logit_grad, router.T, precision=PRECISE)
    middle_norm_grad, ffn_gain_grad = ffn_pull(mixed_grad)
    upstream = cotangent.astype(F32)
    middle_grad = upstream + middle_norm_grad
    attn_grad = middle_grad.astype(BF16)
    context_grad = sum(
        lax.dot_general(
            attn_grad[:, 256 * i : 256 * i + 256], out_full[i], NT, preferred_element_type=F32
        )
        for i in range(4)
    ).astype(BF16)
    (cg_group,) = exchange(
        context_grad_kernel,
        3,
        [jax.ShapeDtypeStruct((GROUP, 512, 128), BF16)],
        [(16,), (16,), ()],
        context_grad,
    )
    late, _ = lax.optimization_barrier(
        ((expert_out, gate_w_grad, up_w_grad, down_w_grad), cg_group)
    )
    rows_home = to_experts(late[0].reshape(experts, capacity, width))
    slot_gates = slot_gates.reshape(experts * capacity, tokens)
    gates_high = slot_gates.astype(BF16)
    gates_low = (slot_gates - gates_high.astype(F32)).astype(BF16)
    rows_home = rows_home.reshape(experts * capacity, width)
    mixture = lax.dot_general(
        gates_high, rows_home, TN, preferred_element_type=F32
    ) + lax.dot_general(gates_low, rows_home, TN, preferred_element_type=F32)
    layer_output = (middle + mixture).astype(BF16)
    def shared_sum(grad):
        low = grad.astype(BF16).reshape(2, grad.shape[0] // 2, grad.shape[1])
        mine = jnp.where(c == 0, low[0], low[1])
        other = jnp.where(c == 0, low[1], low[0])
        chip = (mine.astype(F32) + from_head(other, 1).astype(F32)).astype(BF16)
        both = (chip.astype(F32) + from_head(chip, 2).astype(F32)).astype(BF16)
        back = from_head(both, 1)
        return jnp.where(
            c == 0, jnp.concatenate([both, back]), jnp.concatenate([back, both])
        ).astype(F32)

    expert_sums = [shared_sum(g) for g in late[1:]]

    out_w_parts = jnp.stack(
        [
            lax.dot_general(
                context, attn_grad[:, 256 * i : 256 * i + 256], TN, preferred_element_type=F32
            )
            for i in range(4)
        ]
    ).astype(BF16)
    out_w_parts = lax.all_to_all(
        out_w_parts.reshape(4 * NB, width // NB, width // 4),
        ("head", "blk"),
        split_axis=0,
        concat_axis=0,
        tiled=True,
    )
    w_output_grad = jnp.sum(out_w_parts.astype(F32), axis=0)
    router_grad = lax.psum(router_grad, ("blk", "head"))

    dq, dkv = attend_back(info, q_group, kv_all, cg_group, ctx_wide, ctx_inv)
    dq_parts, dkv_parts = exchange(
        qkv_grad_kernel,
        4,
        [
            jax.ShapeDtypeStruct((2, 2 * tokens, 512), BF16),
            jax.ShapeDtypeStruct((NB, 256, 128), BF16),
        ],
        [(NB,), (NB,), (8,), (8,), (2,)],
        dq,
        dkv,
    )
    query_grad = (dq_parts[0].astype(F32) + dq_parts[1].astype(F32)).astype(BF16)
    dkv_sum = jnp.sum(dkv_parts.reshape(GROUP, 8, 256, 128).astype(F32), axis=1).astype(BF16)
    dkv_sum = dkv_sum.transpose(1, 0, 2).reshape(2 * tokens, 4, 2, 64)
    query_raw_grad, query_gain_grad = query_pull(query_grad.astype(F32).reshape(-1, 8, 64))
    key_raw_grad, key_gain_grad = key_pull(dkv_sum[:, :, 0].astype(F32))
    query_low = query_raw_grad.astype(BF16).reshape(2 * tokens, 512)
    kv_low = jnp.stack([key_raw_grad.astype(BF16), dkv_sum[:, :, 1]], axis=2).reshape(
        2 * tokens, 512
    )
    lows = [
        jnp.concatenate(
            [query_low[:, 256 * i : 256 * i + 256], kv_low[:, 256 * i : 256 * i + 256]], axis=1
        )
        for i in range(2)
    ]
    w_parts = [
        lax.dot_general(normed, lows[i], TN, preferred_element_type=F32).astype(BF16)
        for i in range(2)
    ]
    mine = jnp.where(c == 0, w_parts[0], w_parts[1])
    other = jnp.where(c == 0, w_parts[1], w_parts[0])
    chip_w = (mine.astype(F32) + from_head(other, 1).astype(F32)).astype(BF16)
    normed_grad = sum(
        lax.dot_general(lows[i], w_full[i], NT, preferred_element_type=F32) for i in range(2)
    )
    norm_back, attn_gain_grad = attn_pull(normed_grad)
    halves = norm_back.reshape(2, tokens, width)
    mine = jnp.where(xl == 0, halves[0], halves[1])
    other = jnp.where(xl == 0, halves[1], halves[0])
    input_grad = (middle_grad + mine + from_head(other, 2)).astype(BF16)
    (w_shards,) = exchange(
        scatter_kernel,
        5,
        [jax.ShapeDtypeStruct((NB, width // NB, 512), BF16)],
        [(NB,), (NB,), ()],
        chip_w.reshape(NB, width // NB, 512),
    )
    w_shard = jnp.sum(w_shards.astype(F32), axis=0)
    smalls = jnp.concatenate(
        [attn_gain_grad, ffn_gain_grad, query_gain_grad, key_gain_grad, jnp.zeros((896,), F32)]
    ).reshape(24, 128)
    smalls = small_sum(smalls).reshape(-1)
    return (
        layer_output,
        input_grad,
        smalls[:1024],
        w_shard[:, :256],
        jnp.concatenate([w_shard[:, 256:320], w_shard[:, 384:448]], axis=1),
        jnp.concatenate([w_shard[:, 320:384], w_shard[:, 448:512]], axis=1),
        w_output_grad,
        smalls[2048:2112],
        smalls[2112:2176],
        smalls[1024:2048],
        router_grad,
        expert_sums[0][None],
        expert_sums[1][None],
        expert_sums[2][None],
    )


def solution(mesh):
    everyone = P(("blk", "head"), None)
    both = P("blk", "head")
    expert = P("blk", None, None)
    return jax.shard_map(
        body,
        mesh=mesh,
        in_specs=(everyone, P(), both, both, both, both, P(), P(), P(), P())
        + (expert, expert, expert, everyone, P(), everyone),
        out_specs=(everyone, everyone, P(), both, both, both, both, P(), P(), P(), P())
        + (expert, expert, expert),
        check_vma=False,
    )
```

```python
import functools

import jax
import jax.numpy as jnp
from jax import lax
from jax.experimental import pallas as pl
from jax.experimental.pallas import tpu as pltpu
from jax.sharding import PartitionSpec as P

HEAD_SIZE = 64
TOPK = 8
BLOCK = 256
EPSILON = 1e-06
ROPE_BASE = 10000.0
PRECISE = lax.Precision.HIGHEST
SCALE = HEAD_SIZE ** (-0.5)

NB = 32
SLOTS = 80
GROUP = 4
MESH_ID = pl.DeviceIdType.MESH
F32 = jnp.float32
BF16 = jnp.bfloat16
NT = (((1,), (1,)), ((), ()))
NN = (((1,), (0,)), ((), ()))
TN = (((0,), (0,)), ((), ()))


def place():
    b = lax.axis_index("blk")
    h = lax.axis_index("head")
    y = b // 8
    r = lax.rem(b, 8)
    m = jnp.where(lax.rem(y, 2) == 0, r, 7 - r)
    return b, h // 2, lax.rem(h, 2), y, m


def member(m, j):
    return 8 * j + m + lax.rem(j, 2) * (7 - 2 * m)


def times(start, n, body):
    def step(i, carry):
        body(i)
        return carry

    lax.fori_loop(start, n, step, 0)


def signal(sem, blk, head):
    pl.semaphore_signal(sem, inc=1, device_id=(blk, head), device_id_type=MESH_ID)


def rows(start, size):
    return pl.ds(pl.multiple_of(start, size), size)


def to(src, dst, send, recv, blk, head):
    return pltpu.make_async_remote_copy(
        src, dst, send, recv, device_id=(blk, head), device_id_type=MESH_ID
    )


def weights_kernel(
    ws, li, cot, routes, w_out, li_out, cot_out, routes_out, s1, r1, s2, r2, sx, rx, ls
):
    b, xl, c, _, _ = place()
    h = 2 * xl + c
    sib = 2 * xl + 1 - c
    over = 2 * (1 - xl) + c
    bar = pltpu.get_barrier_semaphore()
    times(1, NB, lambda d: signal(bar, lax.rem(b + d, NB), h))
    signal(bar, b, sib)
    signal(bar, b, over)
    pl.semaphore_wait(bar, NB + 1)

    def first(d):
        return to(ws, w_out.at[c, rows(b * 32, 32)], s1.at[d], r1.at[d], lax.rem(b + d, NB), h)

    def second(d):
        src = lax.rem(b + NB - d, NB)
        part = w_out.at[c, rows(src * 32, 32)]
        return to(part, part, s2.at[d], r2.at[d], b, sib)

    times(1, NB, lambda d: first(d).start())
    extra = [
        to(li, li_out.at[xl], sx.at[0], rx.at[0], b, over),
        to(ws, w_out.at[c, rows(b * 32, 32)], s2.at[0], r2.at[0], b, sib),
        to(cot, cot_out.at[c], sx.at[1], rx.at[1], b, sib),
        to(routes, routes_out.at[c], sx.at[2], rx.at[2], b, sib),
        pltpu.make_async_copy(ws, w_out.at[c, rows(b * 32, 32)], ls.at[0]),
        pltpu.make_async_copy(li, li_out.at[xl], ls.at[1]),
        pltpu.make_async_copy(cot, cot_out.at[c], ls.at[2]),
        pltpu.make_async_copy(routes, routes_out.at[c], ls.at[3]),
    ]
    for item in extra:
        item.start()

    def relay(d):
        first(d).wait_recv()
        second(d).start()

    times(1, NB, relay)
    times(1, NB, lambda d: first(d).wait_send())
    for item in extra:
        item.wait()
    times(1, NB, lambda d: second(d).wait())


def greet_all(bar, b, xl, c, y, m):
    h = 2 * xl + c
    times(1, NB, lambda d: signal(bar, lax.rem(b + d, NB), h))
    times(0, NB, lambda d: signal(bar, lax.rem(b + d, NB), 2 * (1 - xl) + c))
    for dj in range(GROUP):
        j = member(m, lax.rem(y + dj, GROUP))
        signal(bar, j, 2 * xl + 1 - c)
    pl.semaphore_wait(bar, 2 * NB - 1 + GROUP)


def pad_queries(both, qp, i):
    left = lax.broadcasted_iota(jnp.int32, (512, 128), 1) < 64
    qp[i, 0:512] = jnp.where(left, both, 0.0).astype(BF16)
    qp[i, 512:1024] = jnp.where(left, pltpu.roll(both, 64, 1), 0.0).astype(BF16)


def on_pair(p, m, inside, edge):
    def each(i):
        qb = member(m, i)
        whole = (p >= 1) & (2 * p + 1 <= qb - 1)
        pl.when(whole)(lambda: inside(i))
        pl.when(jnp.logical_not(whole) & (2 * p <= qb + 1))(lambda: edge(i, qb))

    times(0, GROUP, each)


def forward_kernel(
    info, query, keyval, wo, crows,
    q_out, kv_out, wo_out, c_out, ctx_out, wide_out, inv_out,
    qg, kvs, qp, vt, acc, accm, peer, ctx,
    s1, r1, s2, r2, s3, r3, s4, r4, s5, r5, s6, r6, s7, r7, ls,
):
    b, xl, c, y, m = place()
    h = 2 * xl + c
    sib = 2 * xl + 1 - c
    e0, e1, total = info[0], info[1], info[2]
    greet_all(pltpu.get_barrier_semaphore(), b, xl, c, y, m)

    def q_piece(dj, dc):
        j = lax.rem(y + dj, GROUP)
        cols = pl.ds(pl.multiple_of(j * 128, 128), 128)
        k = 2 * dj + dc
        src, dst = query.at[:, cols], qg.at[y, rows(c * 256, 256)]
        if k == 0:
            return pltpu.make_async_copy(src, dst, ls.at[0])
        return to(src, dst, s1.at[k], r1.at[k], member(m, j), 2 * xl + lax.rem(c + dc, 2))

    q_pieces = [q_piece(dj, dc) for dj in range(GROUP) for dc in range(2)]

    def kv_piece(d):
        peer_b = lax.rem(b + d, NB)
        cols = pl.ds(pl.multiple_of((peer_b // 8) * 128, 128), 128)
        return to(keyval.at[:, cols], kvs.at[b], s2.at[d], r2.at[d], peer_b, h)

    def wo_piece(e):
        d, x2 = lax.rem(e, NB), lax.rem(xl + e // NB, 2)
        part = wo_out.at[h, rows(b * 32, 32)]
        return to(wo, part, s3.at[e], r3.at[e], lax.rem(b + d, NB), 2 * x2 + c)

    def wo_relay(e):
        d, x2 = lax.rem(e, NB), lax.rem(xl + e // NB, 2)
        part = wo_out.at[2 * x2 + c, rows(lax.rem(b + NB - d, NB) * 32, 32)]
        return to(part, part, s4.at[e], r4.at[e], b, sib)

    for item in q_pieces:
        item.start()
    own_cols = pl.ds(pl.multiple_of(y * 128, 128), 128)
    own = [
        pltpu.make_async_copy(keyval.at[:, own_cols], kvs.at[b], ls.at[1]),
        pltpu.make_async_copy(wo, wo_out.at[h, rows(b * 32, 32)], ls.at[2]),
        to(wo, wo_out.at[h, rows(b * 32, 32)], s4.at[0], r4.at[0], b, sib),
    ]
    for item in own:
        item.start()
    times(1, NB, lambda d: kv_piece(d).start())
    times(1, 2 * NB, lambda e: wo_piece(e).start())
    send_rows(crows, c_out, b, c, h, s5, r5, ls.at[3], "start")
    for item in q_pieces:
        item.wait()
    own[0].wait()
    q_keep = pltpu.make_async_copy(qg, q_out, ls.at[4])
    q_keep.start()
    for i in range(GROUP):
        pad_queries(qg[i].astype(F32), qp, i)
    acc[...] = jnp.zeros_like(acc)
    accm[...] = jnp.zeros_like(accm)
    vt[64:80] = jnp.ones((16, 512), BF16)

    def pair(dp):
        p = lax.rem(b // 2 + 16 - dp, 16)
        for kb in (2 * p, 2 * p + 1):

            @pl.when(kb != b)
            def _():
                kv_piece(lax.rem(b + NB - kb, NB)).wait_recv()

        vt[0:64] = (
            kvs[pl.ds(2 * p, 2)].reshape(512, 128).astype(F32).T[64:128].astype(BF16)
        )

        def scores(i):
            keys = kvs[pl.ds(2 * p, 2)].reshape(512, 128)
            return jnp.exp(lax.dot_general(keys, qp[i], NT, preferred_element_type=F32))

        def inside(i):
            acc[i] += jnp.dot(vt[...], scores(i).astype(BF16), preferred_element_type=F32)

        def edge(i, qb):
            low, high = limits(query_positions((1, 1024), 1, qb), e0, e1, total)
            kpos = key_positions((512, 1), 0, 2 * p, c)
            expo = jnp.where((kpos >= low) & (kpos < high), scores(i), 0.0)
            accm[i] += jnp.dot(vt[...], expo.astype(BF16), preferred_element_type=F32)

        on_pair(p, m, inside, edge)

    times(0, 16, pair)
    for i in range(GROUP):
        pos = query_positions((1, 1024), 1, member(m, i))
        acc[i] = accm[i] + jnp.where((pos >= e0) & (pos < e1), acc[i], 0.0)
    swap = to(acc, peer, s6.at[0], r6.at[0], b, sib)
    swap.start()
    kv_keep = pltpu.make_async_copy(kvs, kv_out, ls.at[5])
    kv_keep.start()

    def relay(e):
        wo_piece(e).wait_recv()
        wo_relay(e).start()

    times(1, 2 * NB, relay)
    swap.wait()

    def ctx_piece(dj, dx):
        j = lax.rem(y + dj, GROUP)
        x2 = lax.rem(xl + dx, 2)
        cols = pl.ds(pl.multiple_of((4 * xl + y) * 128, 128), 128)
        src, dst = ctx.at[j, rows(c * 256 + x2 * 128, 128)], ctx_out.at[:, cols]
        k = 2 * dj + dx
        if k == 0:
            return pltpu.make_async_copy(src, dst, ls.at[6])
        return to(src, dst, s7.at[k], r7.at[k], member(m, j), 2 * x2 + c)

    ctx_pieces = [ctx_piece(dj, dx) for dj in range(GROUP) for dx in range(2)]
    for i in range(GROUP):
        both = acc[i] + peer[i]
        inverse = 1.0 / both[64:65]
        wide = both[0:64] * inverse
        flat = jnp.concatenate([wide[:, 0:512], wide[:, 512:1024]], axis=0).T
        wide_out[i] = flat
        ctx[i] = flat.astype(BF16)
        spread = jnp.broadcast_to(inverse, (64, 1024))
        inv_out[i] = jnp.concatenate([spread[:, 0:512], spread[:, 512:1024]], axis=0).T
    for item in ctx_pieces:
        item.start()
    for item in ctx_pieces:
        item.wait()
    own[1].wait()
    own[2].wait()
    times(1, NB, lambda d: kv_piece(d).wait_send())
    times(1, 2 * NB, lambda e: wo_piece(e).wait_send())
    times(1, 2 * NB, lambda e: wo_relay(e).wait())
    send_rows(crows, c_out, b, c, h, s5, r5, ls.at[3], "wait")
    q_keep.wait()
    kv_keep.wait()


def send_rows(src, dst, b, c, h, send, recv, local, what):
    odd = lax.rem(b + c, 2)

    def piece(d):
        k = lax.rem(b // 2 + d, 16)
        return to(src.at[k], dst.at[b // 2], send.at[d], recv.at[d], 2 * k + odd, h)

    def act(d):
        if what == "start":
            piece(d).start()
        else:
            piece(d).wait()

    times(1, 16, act)
    same = pltpu.make_async_copy(src.at[b // 2], dst.at[b // 2], local)

    @pl.when(c == 0)
    def _():
        if what == "start":
            same.start()
        else:
            same.wait()

    @pl.when(c == 1)
    def _():
        act(0)


def greet_rows(bar, b, c, h, sib):
    odd = lax.rem(b + c, 2)
    times(1, 16, lambda d: signal(bar, 2 * lax.rem(b // 2 + d, 16) + odd, h))
    signal(bar, b, sib)

    @pl.when(c == 1)
    def _():
        signal(bar, 2 * (b // 2) + odd, h)

    pl.semaphore_wait(bar, 16 + c)


def dispatch_kernel(mixed, gates, pick, out, gates_out, both_out, gates_both, tok, gt, stage, gstage, s1, r1, s2, r2, sx, rx, ls):
    b, xl, c, _, _ = place()
    h = 2 * xl + c
    sib = 2 * xl + 1 - c
    greet_rows(pltpu.get_barrier_semaphore(), b, c, h, sib)
    odd = lax.rem(b + c, 2)
    near = [
        to(mixed, tok.at[rows(c * 128, 128)], sx.at[0], rx.at[0], b, sib),
        to(gates, gt.at[rows(c * 128, 128)], sx.at[1], rx.at[1], b, sib),
    ]
    for item in near:
        item.start()
    tok[rows(c * 128, 128)] = mixed[...]
    gt[rows(c * 128, 128)] = gates[...]
    for item in near:
        item.wait()

    def each(d):
        k = lax.rem(b // 2 + d, 16)
        stage[k] = jnp.dot(pick[k], tok[...], preferred_element_type=F32).astype(BF16)
        piece = to(stage.at[k], out.at[b // 2], s1.at[d], r1.at[d], 2 * k + odd, h)
        if_remote(d, c, piece.start)

    times(1, 17, each)
    same = pltpu.make_async_copy(stage.at[b // 2], out.at[b // 2], ls.at[0])
    pl.when(c == 0)(same.start)
    high = gt[...].astype(BF16)
    rest = gt[...] - high.astype(F32)
    mid = rest.astype(BF16)
    low = (rest - mid.astype(F32)).astype(BF16)
    lane = lax.broadcasted_iota(jnp.int32, (80, 128), 1)

    def each_gate(d):
        k = lax.rem(b // 2 + d, 16)
        mine = pick[k]
        spread = (
            jnp.dot(mine, high, preferred_element_type=F32)
            + jnp.dot(mine, mid, preferred_element_type=F32)
            + jnp.dot(mine, low, preferred_element_type=F32)
        )
        column = jnp.sum(jnp.where(lane == 2 * k + odd, spread, 0.0), axis=1, keepdims=True)
        wide = jnp.concatenate([jnp.broadcast_to(column, (80, 128)), jnp.zeros((48, 128), F32)])
        gstage[k] = wide.T[0:8]
        piece = to(gstage.at[k], gates_out.at[b // 2], s2.at[d], r2.at[d], 2 * k + odd, h)
        if_remote(d, c, piece.start)

    times(1, 17, each_gate)
    same_gate = pltpu.make_async_copy(gstage.at[b // 2], gates_out.at[b // 2], ls.at[1])
    pl.when(c == 0)(same_gate.start)
    both_out[...] = tok[...]
    gates_both[...] = gt[...]

    def finish(d):
        k = lax.rem(b // 2 + d, 16)
        one = to(stage.at[k], out.at[b // 2], s1.at[d], r1.at[d], 2 * k + odd, h)
        two = to(gstage.at[k], gates_out.at[b // 2], s2.at[d], r2.at[d], 2 * k + odd, h)
        if_remote(d, c, one.wait)
        if_remote(d, c, two.wait)

    times(1, 17, finish)
    pl.when(c == 0)(same.wait)
    pl.when(c == 0)(same_gate.wait)


def if_remote(d, c, act):
    pl.when((d < 16) | (c == 1))(act)


def return_kernel(rg, gg, pick, pick_t, mg_out, gg_out, land, gland, mgs, ggs, s1, r1, s2, r2, sx, rx, ls):
    b, xl, c, _, _ = place()
    h = 2 * xl + c
    sib = 2 * xl + 1 - c
    greet_rows(pltpu.get_barrier_semaphore(), b, c, h, sib)
    send_rows(gg, gland, b, c, h, s2, r2, ls.at[1], "start")
    send_rows(rg, land, b, c, h, s1, r1, ls.at[0], "start")
    send_rows(gg, gland, b, c, h, s2, r2, ls.at[1], "wait")

    def each(k):
        column = jnp.concatenate([gland[k], jnp.zeros((120, 128), F32)]).T[0:80, 0:1]
        ggs[pl.ds(k, 1)] = jnp.sum(pick[k].astype(F32) * column, axis=0, keepdims=True)

    for k in range(16):
        each(k)
    send_rows(rg, land, b, c, h, s1, r1, ls.at[0], "wait")
    mgs[...] = jnp.dot(pick_t[...], land[...].reshape(1280, 1024), preferred_element_type=F32)
    away = rows((1 - c) * 128, 128)
    home = rows(c * 128, 128)
    near = [
        to(mgs.at[away], mg_out.at[1], sx.at[0], rx.at[0], b, sib),
        to(ggs.at[:, away], gg_out.at[1], sx.at[1], rx.at[1], b, sib),
        pltpu.make_async_copy(mgs.at[home], mg_out.at[0], ls.at[2]),
        pltpu.make_async_copy(ggs.at[:, home], gg_out.at[0], ls.at[3]),
    ]
    for item in near:
        item.start()
    for item in near:
        item.wait()


def backward_kernel(
    info, cg, q_ref, kv_ref, wide_ref, inv_ref, eo, wo_mine, wo_other, ex_mine, ex_other,
    dq_out, dkv_out, eo_out, wo_out, ex_out,
    cgs, qp, gp, gi, qt, gt, gti, dt, di, dqs, dkvt, stage, dq_acc,
    wo_in, wo_sum, ex_in, ex_sum, ex_cross, ex_all,
    s1, r1, s2, r2, s3, r3, s4, r4, s5, r5, sx, rx, ls,
):
    b, xl, c, y, m = place()
    h = 2 * xl + c
    sib = 2 * xl + 1 - c
    over = 2 * (1 - xl) + c
    e0, e1, total = info[0], info[1], info[2]
    bar = pltpu.get_barrier_semaphore()
    for dj in range(GROUP):
        j = member(m, lax.rem(y + dj, GROUP))
        signal(bar, j, 2 * (1 - xl) + 1 - c)
        signal(bar, j, 2 * xl + 1 - c)
    times(1, NB, lambda d: signal(bar, lax.rem(b + d, NB), h))
    times(0, NB, lambda d: signal(bar, lax.rem(b + d, NB), over))
    pl.semaphore_wait(bar, 2 * NB - 1 + 2 * GROUP)

    turns = [(dj, dx, dc) for dj in range(GROUP) for dx in range(2) for dc in range(2)]
    cg_pieces = []
    for k, (dj, dx, dc) in enumerate(turns):
        j = lax.rem(y + dj, GROUP)
        x2 = lax.rem(xl + dx, 2)
        cols = pl.ds(pl.multiple_of((4 * x2 + j) * 128, 128), 128)
        src, dst = cg.at[:, cols], cgs.at[y, rows(c * 256 + xl * 128, 128)]
        if k == 0:
            cg_pieces.append(pltpu.make_async_copy(src, dst, ls.at[0]))
        else:
            head = 2 * x2 + lax.rem(c + dc, 2)
            cg_pieces.append(to(src, dst, s1.at[k], r1.at[k], member(m, j), head))
    for item in cg_pieces:
        item.start()
    wo_swap = to(wo_other, wo_in, sx.at[0], rx.at[0], b, sib)
    wo_swap.start()
    ex_swap = to(ex_other, ex_in, sx.at[1], rx.at[1], b, sib)
    ex_swap.start()
    for i in range(GROUP):
        both = q_ref[i].astype(F32)
        pad_queries(both, qp, i)
        turned = both.T
        qt[i] = jnp.concatenate([turned[0:64], turned[64:128]], axis=1).astype(BF16)
    dq_acc[...] = jnp.zeros_like(dq_acc)
    wo_swap.wait()
    wo_sum[...] = (wo_mine[...].astype(F32) + wo_in[...].astype(F32)).astype(BF16)
    ex_swap.wait()
    ex_sum[...] = (ex_mine[...].astype(F32) + ex_in[...].astype(F32)).astype(BF16)
    cross = to(ex_sum, ex_cross, sx.at[2], rx.at[2], b, over)
    cross.start()

    def wo_piece(e):
        d, x2 = lax.rem(e, NB), lax.rem(xl + e // NB, 2)
        peer_b = lax.rem(b + d, NB)
        part = wo_sum.at[x2, rows(peer_b * 32, 32)]
        return to(part, wo_out.at[xl, b], s3.at[e], r3.at[e], peer_b, 2 * x2 + c)

    for item in cg_pieces:
        item.wait()
    wo_own = pltpu.make_async_copy(wo_sum.at[xl, rows(b * 32, 32)], wo_out.at[xl, b], ls.at[1])
    wo_own.start()
    send_rows(eo, eo_out, b, c, h, s2, r2, ls.at[2], "start")
    times(1, 2 * NB, lambda e: wo_piece(e).start())
    left = lax.broadcasted_iota(jnp.int32, (512, 128), 1) < 64
    for i in range(GROUP):
        scaled = cgs[i].astype(F32) * inv_ref[i]
        pos = query_positions((512, 1), 0, member(m, i))
        middle = (pos >= e0) & (pos < e1)
        terms = scaled * wide_ref[i]
        one = jnp.sum(jnp.where(left, terms, 0.0), axis=1, keepdims=True)
        two = jnp.sum(jnp.where(left, 0.0, terms), axis=1, keepdims=True)
        top = jnp.where(left, 0.0, pltpu.roll(scaled, 64, 1))
        low = jnp.where(left, 0.0, scaled)
        for part, val, term in ((0, top, one), (512, low, two)):
            span = pl.ds(part, 512)
            gp[i, span] = val.astype(BF16)
            gi[i, span] = jnp.where(middle, val, 0.0).astype(BF16)
            dt[i, span] = jnp.broadcast_to(term, (512, 128))
            di[i, span] = jnp.broadcast_to(jnp.where(middle, term, 0.0), (512, 128))
            lanes = pl.ds(part, 512)
            gt[i, :, lanes] = val.T[64:128].astype(BF16)
            gti[i, :, lanes] = jnp.where(middle, val, 0.0).T[64:128].astype(BF16)

    def dkv_piece(kb, slot):
        return to(stage.at[kb], dkv_out.at[b], s4.at[kb], r4.at[slot], kb, h)

    def pair(dp):
        p = lax.rem(b // 2 + 1 + dp, 16)
        dkvt[...] = jnp.zeros_like(dkvt)
        keys = kv_ref[pl.ds(2 * p, 2)].reshape(512, 128)

        def step(i, expo, g, gturn, dots):
            prob = lax.dot_general(g[i], keys, NT, preferred_element_type=F32)
            term = jnp.concatenate([dots[i]] * 4, axis=1)
            score_grad = (expo * (prob - term)).astype(BF16)
            dq_acc[i] += jnp.dot(score_grad, keys, preferred_element_type=F32)
            dkvt[0:64] += jnp.dot(qt[i], score_grad, preferred_element_type=F32)
            dkvt[64:128] += jnp.dot(gturn[i], expo.astype(BF16), preferred_element_type=F32)

        def scores(i):
            return jnp.exp(lax.dot_general(qp[i], keys, NT, preferred_element_type=F32))

        def inside(i):
            step(i, scores(i), gi, gti, di)

        def edge(i, qb):
            low, high = limits(query_positions((1024, 1), 0, qb), e0, e1, total)
            kpos = key_positions((1, 512), 1, 2 * p, c)
            expo = jnp.where((kpos >= low) & (kpos < high), scores(i), 0.0)
            step(i, expo, gp, gt, dt)

        on_pair(p, m, inside, edge)
        flat = dkvt[...].T.astype(BF16)
        for n in range(2):
            kb = 2 * p + n
            stage[kb] = flat[256 * n : 256 * n + 256]

            @pl.when(kb != b)
            def _():
                dkv_piece(kb, b).start()

    times(0, 16, pair)
    dkv_own = pltpu.make_async_copy(stage.at[b], dkv_out.at[b], ls.at[3])
    dkv_own.start()
    for i in range(GROUP):
        both = jnp.where(left, dq_acc[i, 0:512], pltpu.roll(dq_acc[i, 512:1024], 64, 1))
        dqs[i] = (both * SCALE).astype(BF16)

    def dq_piece(dj, dc):
        j = lax.rem(y + dj, GROUP)
        c2 = lax.rem(c + dc, 2)
        cols = pl.ds(pl.multiple_of(y * 128, 128), 128)
        src, dst = dqs.at[j, rows(c2 * 256, 256)], dq_out.at[c, :, cols]
        k = 2 * dj + dc
        if k == 0:
            return pltpu.make_async_copy(src, dst, ls.at[4])
        return to(src, dst, s5.at[k], r5.at[k], member(m, j), 2 * xl + c2)

    dq_pieces = [dq_piece(dj, dc) for dj in range(GROUP) for dc in range(2)]
    for item in dq_pieces:
        item.start()
    cross.wait()
    ex_all[...] = (ex_sum[...].astype(F32) + ex_cross[...].astype(F32)).astype(BF16)
    half = rows(c * 512, 512)
    ex_home = pltpu.make_async_copy(ex_all, ex_out.at[:, half], ls.at[5])
    ex_home.start()
    ex_back = to(ex_all, ex_out.at[:, half], sx.at[3], rx.at[3], b, sib)
    ex_back.start()
    for item in dq_pieces:
        item.wait()
    ex_home.wait()
    ex_back.wait()
    wo_own.wait()
    dkv_own.wait()
    times(1, 2 * NB, lambda e: wo_piece(e).wait())

    def finish(d):
        src = lax.rem(b + d, NB)
        dkv_piece(src, src).wait()

    times(1, NB, finish)
    send_rows(eo, eo_out, b, c, h, s2, r2, ls.at[2], "wait")


def tail_kernel(
    w_mine, w_other, back, mix, small, w_out, back_out, mix_out, small_out,
    w_in, w_sum, w_land, four, many, s1, r1, s2, r2, s3, r3, sx, rx, ls,
):
    b, xl, c, _, _ = place()
    h = 2 * xl + c
    sib = 2 * xl + 1 - c
    over = 2 * (1 - xl) + c
    bar = pltpu.get_barrier_semaphore()
    times(1, NB, lambda d: signal(bar, lax.rem(b + d, NB), h))
    for d in range(1, 4):
        signal(bar, b, lax.rem(h + d, 4))
    pl.semaphore_wait(bar, NB + 2)
    w_swap = to(w_other, w_in, sx.at[0], rx.at[0], b, sib)
    w_swap.start()
    near = [
        to(small, four.at[h], s2.at[d], r2.at[d], b, lax.rem(h + d, 4)) for d in range(1, 4)
    ]
    for item in near:
        item.start()
    swaps = [
        to(back, back_out, sx.at[1], rx.at[1], b, over),
        to(mix, mix_out, sx.at[2], rx.at[2], b, sib),
    ]
    for item in swaps:
        item.start()
    four[h] = small[...]
    w_swap.wait()
    w_sum[...] = (w_mine[...].astype(F32) + w_in[...].astype(F32)).astype(BF16)

    def w_piece(d):
        peer = lax.rem(b + d, NB)
        return to(w_sum.at[peer], w_land.at[b], s1.at[d], r1.at[d], peer, h)

    times(1, NB, lambda d: w_piece(d).start())
    w_land[b] = w_sum[b]
    for item in near:
        item.wait()
    many[b] = four[0] + four[1] + four[2] + four[3]

    def far(d):
        return to(many.at[b], many.at[b], s3.at[d], r3.at[d], lax.rem(b + d, NB), h)

    times(1, NB, lambda d: far(d).start())
    times(1, NB, lambda d: far(d).wait())
    total = many[0]
    for i in range(1, NB):
        total = total + many[i]
    small_out[...] = total
    times(1, NB, lambda d: w_piece(d).wait())
    shard = w_land[0].astype(F32)
    for i in range(1, NB):
        shard = shard + w_land[i].astype(F32)
    w_out[...] = shard
    for item in swaps:
        item.wait()


VM = pl.BlockSpec(memory_space=pltpu.VMEM)
SM = pl.BlockSpec(memory_space=pltpu.SMEM)
ANY = pl.BlockSpec(memory_space=pl.ANY)


def call(kernel, collective_id, ins, outs, scratch, sems, flops, *operands):
    return pl.pallas_call(
        kernel,
        out_shape=[jax.ShapeDtypeStruct(shape, dtype) for shape, dtype, _ in outs],
        in_specs=ins,
        out_specs=[spec for _, _, spec in outs],
        scratch_shapes=[pltpu.VMEM(shape, dtype) for shape, dtype in scratch]
        + [pltpu.SemaphoreType.DMA(n) for n in sems],
        compiler_params=pltpu.CompilerParams(
            collective_id=collective_id,
            has_side_effects=True,
            vmem_limit_bytes=60 * 1024 * 1024,
        ),
        cost_estimate=pl.CostEstimate(
            flops=flops, bytes_accessed=8_000_000, transcendentals=flops // 2000
        ),
    )(*operands)


def limits(pos, e0, e1, total):
    low = jnp.where(pos < e0, 0, jnp.where(pos < e1, e0, e1))
    end = jnp.where(pos < e0, e0, jnp.where(pos < e1, e1, total))
    reach = low + ((pos - low) // BLOCK + 1) * BLOCK
    return low, jnp.minimum(end, reach)


def query_positions(shape, axis, qb):
    r = lax.broadcasted_iota(jnp.int32, shape, axis)
    r = lax.rem(r, 512)
    return 512 * qb + 256 * lax.rem(r // 128, 2) + 128 * (r // 256) + lax.rem(r, 128)


def key_positions(shape, axis, kb, core):
    r = lax.broadcasted_iota(jnp.int32, shape, axis)
    return 512 * (kb + r // 256) + 256 * lax.rem(r // 128, 2) + 128 * core + lax.rem(r, 128)


def rms_scale(values, gain_row):
    return (
        values * lax.rsqrt(jnp.mean(values * values, axis=-1, keepdims=True) + EPSILON) * gain_row
    )


def rotary(values, inside):
    half = values.shape[-1] // 2
    frequency = jnp.power(ROPE_BASE, -2.0 * jnp.arange(half, dtype=F32) / values.shape[-1])
    angles = inside.astype(F32)[:, None] * frequency[None, :]
    cosine, sine = jnp.cos(angles)[:, None, :], jnp.sin(angles)[:, None, :]
    first, second = values[..., :half], values[..., half:]
    return jnp.concatenate(
        [first * cosine - second * sine, second * cosine + first * sine], axis=-1
    )


def head_prep(raw_heads, gain_row, inside):
    return rotary(rms_scale(raw_heads, gain_row), inside)


def from_head(value, bit):
    return lax.ppermute(value, "head", [(i, i ^ bit) for i in range(4)])


def body(
    layer_input,
    attn_gain,
    w_query,
    key_weight,
    value_weight,
    w_output,
    query_gain,
    key_gain,
    ffn_gain,
    router,
    w_gate,
    w_up,
    w_down,
    routes,
    doc_lengths,
    cotangent,
):
    b, xl, c, y, m = place()
    tokens, width = layer_input.shape
    total = tokens * 4 * NB
    ends = jnp.cumsum(doc_lengths)
    info = jnp.stack([ends[0], ends[1], jnp.int32(total), c]).astype(jnp.int32)

    shard = jnp.concatenate(
        [
            w_query,
            key_weight[:, :64],
            value_weight[:, :64],
            key_weight[:, 64:],
            value_weight[:, 64:],
        ],
        axis=1,
    )
    w_full, both_inputs, both_cot, both_routes = call(
        weights_kernel,
        0,
        [ANY] * 4,
        [
            ((2, width, 512), BF16, ANY),
            ((2, tokens, width), BF16, ANY),
            ((2, tokens, width), BF16, ANY),
            ((2, tokens, TOPK), jnp.int32, ANY),
        ],
        [],
        [(NB,)] * 4 + [(3,), (3,), (4,)],
        0,
        shard,
        layer_input,
        cotangent,
        routes,
    )

    routes2 = both_routes.reshape(2 * tokens, TOPK)
    chosen2 = jnp.any(routes2[:, :, None] == jnp.arange(NB, dtype=jnp.int32), axis=1)
    before = jnp.tril(jnp.ones((2 * tokens, 2 * tokens), BF16), -1)
    rank = jnp.dot(before, chosen2.astype(BF16), preferred_element_type=F32).astype(jnp.int32)
    odd = (b + c) % 2

    def of_mine(table):
        pairs = table.reshape(2 * tokens, 16, 2)
        return jnp.where(odd == 0, pairs[:, :, 0], pairs[:, :, 1]).T

    slot = jnp.arange(SLOTS, dtype=jnp.int32)
    at_slot = of_mine(chosen2)[:, None, :] & (of_mine(rank)[:, None, :] == slot[None, :, None])
    pick = at_slot.astype(BF16)
    flat_pick = pick.reshape(16 * SLOTS, 2 * tokens)
    pick_t = flat_pick.T
    cot2 = both_cot.reshape(2 * tokens, width)
    cot_rows = (
        jnp.dot(flat_pick, cot2, preferred_element_type=F32)
        .astype(BF16)
        .reshape(16, SLOTS, width)
    )

    source2 = both_inputs.reshape(2 * tokens, width).astype(F32)
    normed_wide, attn_pull = jax.vjp(rms_scale, source2, attn_gain)
    normed = normed_wide.astype(BF16)
    raw = [jnp.dot(normed, w_full[i], preferred_element_type=F32) for i in range(2)]
    query_raw = jnp.concatenate([raw[0][:, :256], raw[1][:, :256]], axis=1).reshape(-1, 8, 64)
    kv_raw = jnp.concatenate([raw[0][:, 256:], raw[1][:, 256:]], axis=1).reshape(-1, 4, 2, 64)
    t = jnp.arange(2 * tokens, dtype=jnp.int32)
    pos = 512 * b + 256 * (t // 128) + 128 * c + t % 128
    opening = jnp.where(pos < ends[0], 0, jnp.where(pos < ends[1], ends[0], ends[1]))
    inside = pos - opening
    prep = functools.partial(head_prep, inside=inside)
    query_prep, query_pull = jax.vjp(prep, query_raw, query_gain)
    key_prep, key_pull = jax.vjp(prep, kv_raw[:, :, 0], key_gain)
    query = (query_prep.astype(BF16) * SCALE).astype(BF16).reshape(2 * tokens, 512)
    keyval = (
        jnp.stack([key_prep, kv_raw[:, :, 1]], axis=2).astype(BF16).reshape(2 * tokens, 512)
    )
    q_group, kv_all, out_full, up_rows, context, ctx_wide, ctx_inv = call(
        forward_kernel,
        1,
        [SM] + [ANY] * 4,
        [
            ((GROUP, 512, 128), BF16, ANY),
            ((NB, 256, 128), BF16, ANY),
            ((4, width, width // 4), BF16, ANY),
            ((16, SLOTS, width), BF16, ANY),
            ((tokens, width), BF16, ANY),
            ((GROUP, 512, 128), F32, VM),
            ((GROUP, 512, 128), F32, VM),
        ],
        [
            ((GROUP, 512, 128), BF16),
            ((NB, 256, 128), BF16),
            ((GROUP, 1024, 128), BF16),
            ((80, 512), BF16),
            ((GROUP, 80, 1024), F32),
            ((GROUP, 80, 1024), F32),
            ((GROUP, 80, 1024), F32),
            ((GROUP, 512, 128), BF16),
        ],
        [(8,)] * 2 + [(NB,)] * 2 + [(2 * NB,)] * 4 + [(16,)] * 2 + [(1,)] * 2 + [(8,)] * 2 + [(7,)],
        18_000_000_000,
        info,
        query,
        keyval,
        w_output,
        cot_rows,
    )

    source = layer_input.astype(F32)
    projected = [jnp.dot(context, out_full[i], preferred_element_type=F32) for i in range(4)]
    middle = source + jnp.concatenate(projected, axis=1)
    mixed_wide, ffn_pull = jax.vjp(rms_scale, middle, ffn_gain)
    mixed_in = mixed_wide.astype(BF16)
    chosen = jnp.any(routes[:, :, None] == jnp.arange(NB, dtype=jnp.int32), axis=1)
    logits = jnp.dot(mixed_in.astype(F32), router, precision=PRECISE)
    top = jnp.max(jnp.where(chosen, logits, -jnp.inf), axis=1, keepdims=True)
    weight = jnp.where(chosen, jnp.exp(logits - top), 0.0)
    gates = weight / jnp.sum(weight, axis=1, keepdims=True)
    expert_in, gates_in, mixed2, gates2 = call(
        dispatch_kernel,
        2,
        [VM] * 3,
        [
            ((16, SLOTS, width), BF16, ANY),
            ((16, 8, 128), F32, ANY),
            ((2 * tokens, width), BF16, VM),
            ((2 * tokens, 128), F32, VM),
        ],
        [
            ((2 * tokens, width), BF16),
            ((2 * tokens, 128), F32),
            ((16, SLOTS, width), BF16),
            ((16, 8, 128), F32),
        ],
        [(17,)] * 4 + [(2,), (2,), (2,)],
        0,
        mixed_in,
        jnp.pad(gates, ((0, 0), (0, 96))),
        pick,
    )

    expert_in = expert_in.reshape(16 * SLOTS, width)
    gate_rows = gates_in[:, 0, :SLOTS].reshape(16 * SLOTS, 1)
    up_rows = up_rows.reshape(16 * SLOTS, width)
    gate_w, up_w, down_w = w_gate[0], w_up[0], w_down[0]
    gate_pre = jnp.dot(expert_in, gate_w, preferred_element_type=F32)
    up_pre = jnp.dot(expert_in, up_w, preferred_element_type=F32)
    sig = jax.nn.sigmoid(gate_pre)
    activated = gate_pre * sig
    hidden = (activated * up_pre).astype(BF16)
    expert_out = jnp.dot(hidden, down_w, preferred_element_type=F32).astype(BF16)
    upstream_rows = up_rows.astype(F32)
    gate_back_rows = jnp.sum(upstream_rows * expert_out.astype(F32), axis=1)
    out_grad = (gate_rows * upstream_rows).astype(BF16)
    hidden_grad = lax.dot_general(out_grad, down_w, NT, preferred_element_type=F32)
    gate_back = (hidden_grad * up_pre * sig * (1.0 + gate_pre * (1.0 - sig))).astype(BF16)
    up_back = (hidden_grad * activated).astype(BF16)
    rows_grad = lax.dot_general(
        gate_back, gate_w, NT, preferred_element_type=F32
    ) + lax.dot_general(up_back, up_w, NT, preferred_element_type=F32)
    sent_gg = jnp.pad(gate_back_rows.reshape(16, 1, SLOTS), ((0, 0), (0, 7), (0, 128 - SLOTS)))
    mg_parts, gg_parts = call(
        return_kernel,
        3,
        [ANY, ANY, VM, VM],
        [((2, tokens, width), F32, ANY), ((2, 16, tokens), F32, ANY)],
        [
            ((16, SLOTS, width), BF16),
            ((16, 8, 128), F32),
            ((2 * tokens, width), F32),
            ((16, 2 * tokens), F32),
        ],
        [(16,)] * 4 + [(2,), (2,), (4,)],
        0,
        rows_grad.astype(BF16).reshape(16, SLOTS, width),
        sent_gg,
        pick,
        pick_t,
    )

    first, second = jnp.where(odd == 0, gg_parts[0], gg_parts[1]), jnp.where(
        odd == 0, gg_parts[1], gg_parts[0]
    )
    gate_grad = jnp.stack([first, second], axis=1).reshape(NB, tokens).T
    logit_grad = gates * (gate_grad - jnp.sum(gates * gate_grad, axis=1, keepdims=True))
    router_grad = jnp.dot(mixed_in.astype(F32).T, logit_grad, precision=PRECISE)
    router_grad = lax.psum(router_grad, ("blk", "head"))
    mixed_grad = mg_parts[0] + mg_parts[1] + jnp.dot(logit_grad, router.T, precision=PRECISE)
    middle_norm_grad, ffn_gain_grad = ffn_pull(mixed_grad)
    upstream = cotangent.astype(F32)
    middle_grad = upstream + middle_norm_grad
    attn_grad = middle_grad.astype(BF16)
    context_grad = sum(
        lax.dot_general(
            attn_grad[:, 256 * i : 256 * i + 256], out_full[i], NT, preferred_element_type=F32
        )
        for i in range(4)
    ).astype(BF16)
    out_w_parts = [
        lax.dot_general(
            context, attn_grad[:, 256 * i : 256 * i + 256], TN, preferred_element_type=F32
        ).astype(BF16)
        for i in range(4)
    ]
    cores = [jnp.stack([out_w_parts[k], out_w_parts[2 + k]]) for k in range(2)]
    wo_mine = jnp.where(c == 0, cores[0], cores[1])
    wo_other = jnp.where(c == 0, cores[1], cores[0])
    down_w_grad = lax.dot_general(hidden, out_grad, TN, preferred_element_type=F32).astype(BF16)
    gate_w_grad = lax.dot_general(expert_in, gate_back, TN, preferred_element_type=F32)
    up_w_grad = lax.dot_general(expert_in, up_back, TN, preferred_element_type=F32)
    expert_grads = jnp.stack(
        [
            gate_w_grad.astype(BF16),
            up_w_grad.astype(BF16),
            jnp.concatenate([down_w_grad[:, :512], down_w_grad[:, 512:]], axis=0),
        ]
    )
    ex_mine = lax.dynamic_slice_in_dim(expert_grads, 512 * c, 512, axis=1)
    ex_other = lax.dynamic_slice_in_dim(expert_grads, 512 * (1 - c), 512, axis=1)
    dq_parts, dkv_parts, rows_home, wo_parts, ex_sums = call(
        backward_kernel,
        4,
        [SM, ANY, VM, VM, VM, VM, ANY, VM, ANY, VM, ANY],
        [
            ((2, 2 * tokens, 512), BF16, ANY),
            ((NB, 256, 128), BF16, ANY),
            ((16, SLOTS, width), BF16, ANY),
            ((2, NB, 32, 256), BF16, ANY),
            ((3, 1024, 512), BF16, ANY),
        ],
        [
            ((GROUP, 512, 128), BF16),
            ((GROUP, 1024, 128), BF16),
            ((GROUP, 1024, 128), BF16),
            ((GROUP, 1024, 128), BF16),
            ((GROUP, 64, 1024), BF16),
            ((GROUP, 64, 1024), BF16),
            ((GROUP, 64, 1024), BF16),
            ((GROUP, 1024, 128), F32),
            ((GROUP, 1024, 128), F32),
            ((GROUP, 512, 128), BF16),
            ((128, 512), F32),
            ((NB, 256, 128), BF16),
            ((GROUP, 1024, 128), F32),
            ((2, 1024, 256), BF16),
            ((2, 1024, 256), BF16),
            ((3, 512, 512), BF16),
            ((3, 512, 512), BF16),
            ((3, 512, 512), BF16),
            ((3, 512, 512), BF16),
        ],
        [(16,)] * 4 + [(2 * NB,)] * 2 + [(NB,)] * 2 + [(8,)] * 2 + [(4,)] * 2 + [(6,)],
        45_000_000_000,
        info,
        context_grad,
        q_group,
        kv_all,
        ctx_wide,
        ctx_inv,
        expert_out.reshape(16, SLOTS, width),
        wo_mine,
        wo_other,
        ex_mine,
        ex_other,
    )

    query_grad = (dq_parts[0].astype(F32) + dq_parts[1].astype(F32)).astype(BF16)
    dkv_sum = jnp.sum(dkv_parts.reshape(GROUP, 8, 256, 128).astype(F32), axis=1).astype(BF16)
    dkv_sum = dkv_sum.transpose(1, 0, 2).reshape(2 * tokens, 4, 2, 64)
    query_raw_grad, query_gain_grad = query_pull(query_grad.astype(F32).reshape(-1, 8, 64))
    key_raw_grad, key_gain_grad = key_pull(dkv_sum[:, :, 0].astype(F32))
    query_low = query_raw_grad.astype(BF16).reshape(2 * tokens, 512)
    kv_low = jnp.stack([key_raw_grad.astype(BF16), dkv_sum[:, :, 1]], axis=2).reshape(
        2 * tokens, 512
    )
    lows = [
        jnp.concatenate(
            [query_low[:, 256 * i : 256 * i + 256], kv_low[:, 256 * i : 256 * i + 256]], axis=1
        )
        for i in range(2)
    ]
    w_parts = [
        lax.dot_general(normed, lows[i], TN, preferred_element_type=F32).astype(BF16)
        for i in range(2)
    ]
    w_mine = jnp.where(c == 0, w_parts[0], w_parts[1]).reshape(NB, width // NB, 512)
    w_other = jnp.where(c == 0, w_parts[1], w_parts[0]).reshape(NB, width // NB, 512)
    normed_grad = sum(
        lax.dot_general(lows[i], w_full[i], NT, preferred_element_type=F32) for i in range(2)
    )
    norm_back, attn_gain_grad = attn_pull(normed_grad)
    halves = norm_back.reshape(2, tokens, width)
    back_mine = jnp.where(xl == 0, halves[0], halves[1])
    back_other = jnp.where(xl == 0, halves[1], halves[0])
    gates_t = gates2[:, :NB].reshape(2 * tokens, 16, 2)
    gates_t = jnp.where(odd == 0, gates_t[:, :, 0], gates_t[:, :, 1])
    weights = jnp.where(at_slot, gates_t.T[:, None, :], 0.0).reshape(16 * SLOTS, 2 * tokens)
    high = weights.astype(BF16)
    low = (weights - high.astype(F32)).astype(BF16)
    flat_home = rows_home.reshape(16 * SLOTS, width)
    mixture = lax.dot_general(high, flat_home, TN, preferred_element_type=F32) + lax.dot_general(
        low, flat_home, TN, preferred_element_type=F32
    )
    mixture = mixture.reshape(2, tokens, width)
    mix_mine = jnp.where(c == 0, mixture[0], mixture[1])
    mix_other = jnp.where(c == 0, mixture[1], mixture[0])
    smalls = jnp.concatenate(
        [attn_gain_grad, ffn_gain_grad, query_gain_grad, key_gain_grad, jnp.zeros((896,), F32)]
    ).reshape(24, 128)
    w_shard, back_in, mix_in, smalls = call(
        tail_kernel,
        5,
        [VM, ANY, ANY, ANY, VM],
        [
            ((width // NB, 512), F32, VM),
            ((tokens, width), F32, ANY),
            ((tokens, width), F32, ANY),
            ((24, 128), F32, VM),
        ],
        [
            ((NB, width // NB, 512), BF16),
            ((NB, width // NB, 512), BF16),
            ((NB, width // NB, 512), BF16),
            ((4, 24, 128), F32),
            ((NB, 24, 128), F32),
        ],
        [(NB,)] * 2 + [(4,)] * 2 + [(NB,)] * 2 + [(3,)] * 2 + [(1,)],
        0,
        w_mine,
        w_other,
        back_other,
        mix_other,
        smalls,
    )
    input_grad = (middle_grad + back_mine + back_in).astype(BF16)
    layer_output = (middle + mix_mine + mix_in).astype(BF16)
    w_output_grad = jnp.sum(wo_parts.reshape(2 * NB, 32, 256).astype(F32), axis=0)
    smalls = smalls.reshape(-1)
    down_sum = jnp.concatenate([ex_sums[2, :512], ex_sums[2, 512:]], axis=1)
    return (
        layer_output,
        input_grad,
        smalls[:1024],
        w_shard[:, :256],
        jnp.concatenate([w_shard[:, 256:320], w_shard[:, 384:448]], axis=1),
        jnp.concatenate([w_shard[:, 320:384], w_shard[:, 448:512]], axis=1),
        w_output_grad,
        smalls[2048:2112],
        smalls[2112:2176],
        smalls[1024:2048],
        router_grad,
        ex_sums[0].astype(F32)[None],
        ex_sums[1].astype(F32)[None],
        down_sum.astype(F32)[None],
    )


def solution(mesh):
    everyone = P(("blk", "head"), None)
    both = P("blk", "head")
    expert = P("blk", None, None)
    return jax.shard_map(
        body,
        mesh=mesh,
        in_specs=(everyone, P(), both, both, both, both, P(), P(), P(), P())
        + (expert, expert, expert, everyone, P(), everyone),
        out_specs=(everyone, everyone, P(), both, both, both, both, P(), P(), P(), P())
        + (expert, expert, expert),
        check_vma=False,
    )
```

```python
import jax
import jax.numpy as jnp
import numpy as np
from jax import lax
from jax.experimental import pallas as pl
from jax.experimental.pallas import tpu as pltpu
from jax.sharding import PartitionSpec as P

HEAD_SIZE = 64
TOPK = 8
BLOCK = 256
EPSILON = 1e-06
ROPE_BASE = 10000.0
PRECISE = lax.Precision.HIGHEST
SCALE = HEAD_SIZE ** (-0.5)

NB = 32
EARLY = 7
SLOTS = 80
GROUP = 4
MESH_ID = pl.DeviceIdType.MESH
F32 = jnp.float32
BF16 = jnp.bfloat16
NT = (((1,), (1,)), ((), ()))
NN = (((1,), (0,)), ((), ()))
TN = (((0,), (0,)), ((), ()))


def place():
    b = lax.axis_index("blk")
    h = lax.axis_index("head")
    y = b // 8
    r = lax.rem(b, 8)
    m = jnp.where(lax.rem(y, 2) == 0, r, 7 - r)
    return b, h // 2, lax.rem(h, 2), y, m


def member(m, j):
    return 8 * j + m + lax.rem(j, 2) * (7 - 2 * m)


def times(start, n, body):
    def step(i, carry):
        body(i)
        return carry

    lax.fori_loop(start, n, step, 0)


def signal(sem, blk, head):
    pl.semaphore_signal(sem, inc=1, device_id=(blk, head), device_id_type=MESH_ID)


def rows(start, size):
    return pl.ds(pl.multiple_of(start, size), size)


def to(src, dst, send, recv, blk, head):
    return pltpu.make_async_remote_copy(
        src, dst, send, recv, device_id=(blk, head), device_id_type=MESH_ID
    )


def settle(sem, part):
    pltpu.make_async_copy(part, part, sem).wait()


def settle_rows(sem, blocks, c):
    pl.when(c == 0)(lambda: settle(sem, blocks.at[pl.ds(0, 15)]))
    pl.when(c == 1)(lambda: settle(sem, blocks))


def greet_all(bar, b, xl, c, y, m):
    h = 2 * xl + c
    times(1, NB, lambda d: signal(bar, lax.rem(b + d, NB), h))
    times(0, NB, lambda d: signal(bar, lax.rem(b + d, NB), 2 * (1 - xl) + c))
    for dj in range(GROUP):
        j = member(m, lax.rem(y + dj, GROUP))
        signal(bar, j, 2 * xl + 1 - c)
    pl.semaphore_wait(bar, 2 * NB - 1 + GROUP)


def pad_queries(both, qp, i):
    left = lax.broadcasted_iota(jnp.int32, (512, 128), 1) < 64
    qp[i, 0:512] = jnp.where(left, both, 0.0).astype(BF16)
    qp[i, 512:1024] = jnp.where(left, pltpu.roll(both, 64, 1), 0.0).astype(BF16)


def on_pair(p, m, inside, edge):
    def each(i):
        qb = member(m, i)
        whole = (p >= 1) & (2 * p + 1 <= qb - 1)
        pl.when(whole)(lambda: inside(i))
        pl.when(jnp.logical_not(whole) & (2 * p <= qb + 1))(lambda: edge(i, qb))

    times(0, GROUP, each)


def by_head(values, left):
    one = jnp.sum(jnp.where(left, values, 0.0), axis=1, keepdims=True) / HEAD_SIZE
    two = jnp.sum(jnp.where(left, 0.0, values), axis=1, keepdims=True) / HEAD_SIZE
    return jnp.where(left, one, two)


def swapped(values, first):
    return jnp.where(first, pltpu.roll(values, 96, 1), pltpu.roll(values, 32, 1))


def row_scale(values):
    return lax.rsqrt(jnp.mean(values * values, axis=1, keepdims=True) + EPSILON)


def lanes_of(shape):
    lane = lax.broadcasted_iota(jnp.int32, shape, 1)
    return lane < 64, lax.rem(lane, 64) < 32


def slab(j):
    return j // 2, slice(128 * (j % 2), 128 * (j % 2) + 128), slice(
        256 + 128 * (j % 2), 384 + 128 * (j % 2)
    )


def forward_kernel(
    lengths, wq, wk, wvl, wo, li, cot, routes_t, attn_gain, q_gain, k_gain, pace, ffn_gain, router_t,
    w_out, far_out, li_out, q_out, kv_out, c_out,
    pick, raw, normed, wide_out, inv_out, ctx_out, mid_out, mixed_out, gates_out, turn, head_gain, router,
    ws, wv, far, li2, cot2, rt, xs, qs, kvst, qg, kvs, qp, vt, acc, accm, peer, ctx, ctx_in,
    sw, rw, sx, rx, s1, r1, s2, r2, s5, r5, s7, r7, ls,
):
    b, xl, c, y, m = place()
    h = 2 * xl + c
    sib = 2 * xl + 1 - c
    over = 2 * (1 - xl) + c
    odd = lax.rem(b + c, 2)
    e0, e1, total = lengths[0], lengths[0] + lengths[1], 512 * NB
    pairs = jnp.concatenate([wk[...].astype(F32), wvl[...].astype(F32)], axis=1)
    even = jnp.concatenate([pairs[:, 0:64], pairs[:, 128:192]], axis=1)
    other = jnp.concatenate([pairs[:, 64:128], pairs[:, 192:256]], axis=1)
    ws[:, 0:256] = wq[...]
    ws[:, 256:384] = even.astype(BF16)
    ws[:, 384:512] = other.astype(BF16)
    ws[:, 512:768] = wo[...]
    greet_all(pltpu.get_barrier_semaphore(), b, xl, c, y, m)

    def w_first(d):
        part = wv.at[c, rows(b * 32, 32)]
        return to(ws, part, sw.at[0], rw.at[0], lax.rem(b + d, NB), h)

    near = [
        to(routes_t, rt.at[c], sx.at[0], rx.at[0], b, sib),
        to(cot, cot2.at[rows(c * 128, 128)], sx.at[1], rx.at[1], b, sib),
        to(li, li2.at[xl], sx.at[2], rx.at[2], b, over),
    ]
    for item in near:
        item.start()
    times(1, NB, lambda d: w_first(d).start())
    wv[c, rows(b * 32, 32)] = ws[...]
    li2[xl] = li[...]
    cot2[rows(c * 128, 128)] = cot[...]
    rt[c] = routes_t[...]

    near[0].wait()
    both_routes = jnp.concatenate([rt[0], rt[1]], axis=1)
    mine = 2 * lax.broadcasted_iota(jnp.int32, (16, 256), 0) + odd
    chosen = jnp.zeros((16, 256), F32)
    for k in range(TOPK):
        chosen = jnp.where(both_routes[k : k + 1] == mine, 1.0, chosen)
    earlier = lax.broadcasted_iota(jnp.int32, (256, 256), 0) < lax.broadcasted_iota(
        jnp.int32, (256, 256), 1
    )
    rank = jnp.dot(
        chosen.astype(BF16), jnp.where(earlier, 1.0, 0.0).astype(BF16), preferred_element_type=F32
    )
    slot = lax.broadcasted_iota(jnp.int32, (80, 256), 0).astype(F32)
    for k in range(16):
        at = jnp.where(rank[k : k + 1] == slot, chosen[k : k + 1], 0.0)
        pick[k] = at.astype(BF16)
    near[1].wait()
    c_piece = rows_out(xs, c_out, b, xl, c, s5.at[0], lambda d: r5.at[0])
    c_same = pltpu.make_async_copy(xs.at[b // 2], c_out.at[15], ls.at[3])

    def fetch(d):
        k = lax.rem(b // 2 + d, 16)
        xs[k] = jnp.dot(pick[k], cot2[...], preferred_element_type=F32).astype(BF16)
        start_rows(c_piece, d, c, c_same)

    times(1, EARLY, fetch)

    near[2].wait()
    li_keep = pltpu.make_async_copy(li2, li_out, ls.at[7])
    li_keep.start()
    source2 = li2[...].reshape(256, 1024).astype(F32)
    normed[...] = (source2 * row_scale(source2) * attn_gain[...]).astype(BF16)

    settle(rw.at[0], wv.at[c, rows(0, 992)])
    w_sib = to(wv.at[c], wv.at[c], sx.at[3], rx.at[3], b, sib)
    w_sib.start()
    wo_over = to(wv.at[c, :, pl.ds(512, 256)], far.at[c], sx.at[4], rx.at[4], b, over)
    wo_over.start()
    left, first = lanes_of((256, 128))
    t = lax.broadcasted_iota(jnp.int32, (256, 128), 0)
    pos = 512 * b + 256 * (t // 128) + 128 * c + lax.rem(t, 128)
    opening = jnp.where(pos < e0, 0, jnp.where(pos < e1, e0, e1))
    angles = (pos - opening).astype(F32) * pace[...]
    turn[0] = jnp.cos(angles)
    sine = jnp.sin(angles)
    turn[1] = jnp.where(first, -sine, sine)
    head_gain[0:1] = jnp.concatenate([q_gain[...], q_gain[...]], axis=1)
    head_gain[1:2] = jnp.concatenate([k_gain[...], jnp.ones((1, 64), F32)], axis=1)
    router[...] = jnp.zeros_like(router)
    router[0:NB] = router_t[...]
    w_sib.wait()
    w_keep = pltpu.make_async_copy(wv, w_out, ls.at[8])
    w_keep.start()
    for i in range(2):
        raw[i] = jnp.dot(normed[...], wv[i, :, 0:512], preferred_element_type=F32)
    for j in range(GROUP):
        i, q_cols, kv_cols = slab(j)
        span = slice(128 * j, 128 * j + 128)
        u = raw[i, :, q_cols]
        n = u * lax.rsqrt(by_head(u * u, left) + EPSILON) * head_gain[0:1]
        turned = n * turn[0] + swapped(n, first) * turn[1]
        qs[:, span] = (turned.astype(BF16).astype(F32) * SCALE).astype(BF16)
        u = raw[i, :, kv_cols]
        n = u * lax.rsqrt(by_head(u * u, left) + EPSILON) * head_gain[1:2]
        turned = n * turn[0] + swapped(n, first) * turn[1]
        kvst[:, span] = jnp.where(left, turned, u).astype(BF16)

    def q_piece(dj, dc):
        j = lax.rem(y + dj, GROUP)
        cols = pl.ds(pl.multiple_of(j * 128, 128), 128)
        k = 2 * dj + dc
        src, dst = qs.at[:, cols], qg.at[y, rows(c * 256, 256)]
        if k == 0:
            return pltpu.make_async_copy(src, dst, ls.at[0])
        return to(src, dst, s1.at[k], r1.at[k], member(m, j), 2 * xl + lax.rem(c + dc, 2))

    q_pieces = [q_piece(dj, dc) for dj in range(GROUP) for dc in range(2)]

    def kv_piece(d):
        peer_b = lax.rem(b + d, NB)
        cols = pl.ds(pl.multiple_of((peer_b // 8) * 128, 128), 128)
        return to(kvst.at[:, cols], kvs.at[b], s2.at[0], r2.at[d], peer_b, h)

    for item in q_pieces:
        item.start()
    own_cols = pl.ds(pl.multiple_of(y * 128, 128), 128)
    kv_own = pltpu.make_async_copy(kvst.at[:, own_cols], kvs.at[b], ls.at[1])
    kv_own.start()
    times(1, NB, lambda d: kv_piece(d).start())
    times(EARLY, 17, fetch)
    for item in q_pieces:
        item.wait()
    kv_own.wait()
    q_keep = pltpu.make_async_copy(qg, q_out, ls.at[4])
    q_keep.start()
    for i in range(GROUP):
        pad_queries(qg[i].astype(F32), qp, i)
    acc[...] = jnp.zeros_like(acc)
    accm[...] = jnp.zeros_like(accm)
    vt[64:80] = jnp.ones((16, 512), BF16)

    def pair(dp):
        p = lax.rem(b // 2 + 16 - dp, 16)
        for kb in (2 * p, 2 * p + 1):

            @pl.when(kb != b)
            def _():
                kv_piece(lax.rem(b + NB - kb, NB)).wait_recv()

        vt[0:64] = (
            kvs[pl.ds(2 * p, 2)].reshape(512, 128).astype(F32).T[64:128].astype(BF16)
        )

        def scores(i):
            keys = kvs[pl.ds(2 * p, 2)].reshape(512, 128)
            return jnp.exp(lax.dot_general(keys, qp[i], NT, preferred_element_type=F32))

        def inside(i):
            acc[i] += jnp.dot(vt[...], scores(i).astype(BF16), preferred_element_type=F32)

        def edge(i, qb):
            low, high = limits(query_positions((1, 1024), 1, qb), e0, e1, total)
            kpos = key_positions((512, 1), 0, 2 * p, c)
            expo = jnp.where((kpos >= low) & (kpos < high), scores(i), 0.0)
            accm[i] += jnp.dot(vt[...], expo.astype(BF16), preferred_element_type=F32)

        on_pair(p, m, inside, edge)

    times(0, 16, pair)
    for i in range(GROUP):
        pos = query_positions((1, 1024), 1, member(m, i))
        acc[i] = accm[i] + jnp.where((pos >= e0) & (pos < e1), acc[i], 0.0)
    swap = to(acc, peer, sx.at[5], rx.at[5], b, sib)
    swap.start()
    kv_keep = pltpu.make_async_copy(kvs, kv_out, ls.at[5])
    kv_keep.start()
    wo_over.wait()
    far_sib = to(far.at[c], far.at[c], sx.at[6], rx.at[6], b, sib)
    far_sib.start()
    swap.wait()

    def ctx_piece(dj, dx):
        j = lax.rem(y + dj, GROUP)
        x2 = lax.rem(xl + dx, 2)
        cols = pl.ds(pl.multiple_of((4 * xl + y) * 128, 128), 128)
        src, dst = ctx.at[j, rows(c * 256 + x2 * 128, 128)], ctx_in.at[:, cols]
        k = 2 * dj + dx
        if k == 0:
            return pltpu.make_async_copy(src, dst, ls.at[6])
        return to(src, dst, s7.at[k], r7.at[k], member(m, j), 2 * x2 + c)

    ctx_pieces = [ctx_piece(dj, dx) for dj in range(GROUP) for dx in range(2)]
    for i in range(GROUP):
        both = acc[i] + peer[i]
        inverse = 1.0 / both[64:65]
        wide = both[0:64] * inverse
        flat = jnp.concatenate([wide[:, 0:512], wide[:, 512:1024]], axis=0).T
        wide_out[i] = flat
        ctx[i] = flat.astype(BF16)
        spread = jnp.broadcast_to(inverse, (64, 1024))
        inv_out[i] = jnp.concatenate([spread[:, 0:512], spread[:, 512:1024]], axis=0).T
    for item in ctx_pieces:
        item.start()
    far_sib.wait()
    wo_keep = pltpu.make_async_copy(far, far_out, ls.at[2])
    wo_keep.start()
    for item in ctx_pieces:
        item.wait()

    context = ctx_in[...]
    ctx_out[...] = context
    for i in range(2):
        for x2, part in ((xl, wv[i, :, 512:768]), (1 - xl, far[i])):
            cols = rows(512 * x2 + 256 * i, 256)
            mid_out[:, cols] = li[:, cols].astype(F32) + jnp.dot(
                context, part, preferred_element_type=F32
            )
    middle = mid_out[...]
    mixed = (middle * row_scale(middle) * ffn_gain[...]).astype(BF16)
    mixed_out[...] = mixed
    logits = lax.dot_general(
        mixed.astype(F32), router[...], NT, preferred_element_type=F32, precision=PRECISE
    )
    expert = lax.broadcasted_iota(jnp.int32, (128, 128), 0)
    hit = jnp.zeros((128, 128), F32)
    for k in range(TOPK):
        hit = jnp.where(routes_t[k : k + 1] == expert, 1.0, hit)
    hit = hit.T
    top = jnp.max(jnp.where(hit > 0.0, logits, -1e30), axis=1, keepdims=True)
    weight = jnp.where(hit > 0.0, jnp.exp(logits - top), 0.0)
    gates_out[...] = weight / jnp.sum(weight, axis=1, keepdims=True)

    settle(sw.at[0], wv.at[0, rows(0, 992)])
    settle(s2.at[0], kvs.at[pl.ds(0, NB - 1)])
    settle_rows(s5.at[0], xs, c)
    settle_rows(r5.at[0], xs, c)
    pl.when(c == 0)(c_same.wait)
    for item in (li_keep, w_keep, q_keep, kv_keep, wo_keep):
        item.wait()


def row_peer(b, xl, c, k):
    e = 2 * k + lax.rem(b + c, 2)
    apart = lax.rem(b // 4 + e // 4, 2)
    return e, 2 * (xl + apart - 2 * xl * apart) + c


def rows_out(src, dst, b, xl, c, send, recv):
    def piece(d):
        k = lax.rem(b // 2 + d, 16)
        e, head = row_peer(b, xl, c, k)
        return to(src.at[k], dst.at[d - 1], send, recv(d), e, head)

    return piece


def rows_home(src, dst, b, xl, c, send, recv):
    def piece(d):
        k = lax.rem(b // 2 + 16 - d, 16)
        e, head = row_peer(b, xl, c, k)
        return to(src.at[d - 1], dst.at[b // 2], send, recv, e, head)

    return piece


def start_rows(piece, d, c, local):
    pl.when((d < 16) | (c == 1))(lambda: piece(d).start())
    pl.when((d == 16) & (c == 0))(local.start)


def experts_kernel(
    mixed, gates, pick, up_rows, gate_w, up_w, down_w, middle_ref, cot, ffn_gain, router,
    wts_out, eo_out, ex_out, grad_out, low_out, small_out, router_out,
    tok, gt, xs, xl_rows, gs, gl, rs, rl, ggs, ggl, hid, gb, ub, og, mgs, ggt, mg_in, gg_in, gg_all,
    s1, r1, s2, r2, s3, r3, s4, r4, sx, rx, ls,
):
    b, xl, c, _, _ = place()
    h = 2 * xl + c
    sib = 2 * xl + 1 - c
    odd = lax.rem(b + c, 2)
    bar = pltpu.get_barrier_semaphore()

    def greet(d):
        e, head = row_peer(b, xl, c, lax.rem(b // 2 + d, 16))
        signal(bar, e, head)

    times(1, 16, greet)
    signal(bar, b, sib)
    pl.when(c == 1)(lambda: greet(0))
    pl.semaphore_wait(bar, 16 + c)
    near = [
        to(mixed, tok.at[rows(c * 128, 128)], sx.at[0], rx.at[0], b, sib),
        to(gates, gt.at[rows(c * 128, 128)], sx.at[1], rx.at[1], b, sib),
    ]
    for item in near:
        item.start()
    tok[rows(c * 128, 128)] = mixed[...]
    gt[rows(c * 128, 128)] = gates[...]
    near[0].wait()
    x_piece = rows_out(xs, xl_rows, b, xl, c, s1.at[0], lambda d: r1.at[(d - 1) // 4])
    x_same = pltpu.make_async_copy(xs.at[b // 2], xl_rows.at[15], ls.at[0])

    def fetch(d):
        k = lax.rem(b // 2 + d, 16)
        xs[k] = jnp.dot(pick[k], tok[...], preferred_element_type=F32).astype(BF16)
        start_rows(x_piece, d, c, x_same)

    times(1, 17, fetch)
    near[1].wait()
    high = gt[...].astype(BF16)
    rest = gt[...] - high.astype(F32)
    mid = rest.astype(BF16)
    low = (rest - mid.astype(F32)).astype(BF16)
    lane = lax.broadcasted_iota(jnp.int32, (80, 128), 1)
    g_piece = rows_out(gs, gl, b, xl, c, s2.at[0], lambda d: r2.at[(d - 1) // 4])
    g_same = pltpu.make_async_copy(gs.at[b // 2], gl.at[15], ls.at[1])

    def as_row(column):
        wide = jnp.concatenate([jnp.broadcast_to(column, (80, 128)), jnp.zeros((48, 128), F32)])
        return wide.T[0:8]

    def fetch_gate(d):
        k = lax.rem(b // 2 + d, 16)
        mine = pick[k]
        spread = (
            jnp.dot(mine, high, preferred_element_type=F32)
            + jnp.dot(mine, mid, preferred_element_type=F32)
            + jnp.dot(mine, low, preferred_element_type=F32)
        )
        column = jnp.sum(jnp.where(lane == 2 * k + odd, spread, 0.0), axis=1, keepdims=True)
        gs[k] = as_row(column)
        start_rows(g_piece, d, c, g_same)
        weights = mine.astype(F32) * column
        weights_high = weights.astype(BF16)
        wts_out[0, k] = weights_high
        wts_out[1, k] = (weights - weights_high.astype(F32)).astype(BF16)

    times(1, 17, fetch_gate)
    home = rows_home(rs, rl, b, xl, c, s3.at[0], r3.at[0])
    home_same = pltpu.make_async_copy(rs.at[15], rl.at[b // 2], ls.at[2])
    gg_home = rows_home(ggs, ggl, b, xl, c, s4.at[0], r4.at[0])
    gg_same = pltpu.make_async_copy(ggs.at[15], ggl.at[b // 2], ls.at[3])

    def arrived(sem, blocks, g, same):
        @pl.when((g < 3) | (c == 1))
        def _():
            settle(sem.at[g], blocks.at[pl.ds(0, 4)])

        @pl.when((g == 3) & (c == 0))
        def _():
            settle(sem.at[g], blocks.at[pl.ds(0, 3)])
            same.wait()

    def group(g):
        arrived(r1, xl_rows, g, x_same)
        x = xl_rows[pl.ds(4 * g, 4)].reshape(320, 1024)
        u = up_rows[pl.ds(4 * g, 4)].reshape(320, 1024).astype(F32)
        gate_pre = jnp.dot(x, gate_w[0], preferred_element_type=F32)
        up_pre = jnp.dot(x, up_w[0], preferred_element_type=F32)
        sig = jax.nn.sigmoid(gate_pre)
        act = gate_pre * sig
        hidden = (act * up_pre).astype(BF16)
        out = jnp.dot(hidden, down_w[0], preferred_element_type=F32).astype(BF16)
        eo_out[pl.ds(4 * g, 4)] = out.reshape(4, 80, 1024)
        gate_grad = jnp.sum(u * out.astype(F32), axis=1, keepdims=True)
        columns = []
        arrived(r2, gl, g, g_same)
        for n in range(4):
            ggs[4 * g + n] = as_row(gate_grad[80 * n : 80 * n + 80])
            start_rows(gg_home, 4 * g + n + 1, c, gg_same)
            row = jnp.concatenate([gl[4 * g + n], jnp.zeros((120, 128), F32)])
            columns.append(row.T[0:80, 0:1])
        out_grad = (jnp.concatenate(columns) * u).astype(BF16)
        hidden_grad = lax.dot_general(out_grad, down_w[0], NT, preferred_element_type=F32)
        gate_back = (hidden_grad * up_pre * sig * (1.0 + gate_pre * (1.0 - sig))).astype(BF16)
        up_back = (hidden_grad * act).astype(BF16)
        back = lax.dot_general(
            gate_back, gate_w[0], NT, preferred_element_type=F32
        ) + lax.dot_general(up_back, up_w[0], NT, preferred_element_type=F32)
        rs[pl.ds(4 * g, 4)] = back.astype(BF16).reshape(4, 80, 1024)
        for n in range(1, 5):
            start_rows(home, 4 * g + n, c, home_same)
        span = rows(320 * g, 320)
        hid[span] = hidden
        gb[span] = gate_back
        ub[span] = up_back
        og[span] = out_grad

    times(0, 4, group)
    for j in range(4):
        part = slice(256 * j, 256 * j + 256)
        x_turned = xl_rows[:, :, part].reshape(1280, 256)
        ex_out[0, part] = lax.dot_general(x_turned, gb[...], TN, preferred_element_type=F32).astype(BF16)
        ex_out[1, part] = lax.dot_general(x_turned, ub[...], TN, preferred_element_type=F32).astype(BF16)
        half = slice(512 * (j // 2), 512 * (j // 2) + 512)
        turned = hid[:, 256 * (j % 2) : 256 * (j % 2) + 256]
        ex_out[2, part] = lax.dot_general(turned, og[:, half], TN, preferred_element_type=F32).astype(BF16)

    settle_rows(r4.at[0], ggl, c)
    pl.when(c == 0)(gg_same.wait)
    for k in range(16):
        column = jnp.concatenate([ggl[k], jnp.zeros((120, 128), F32)]).T[0:80, 0:1]
        ggt[pl.ds(k, 1)] = jnp.sum(pick[k].astype(F32) * column, axis=0, keepdims=True)
    settle_rows(r3.at[0], rl, c)
    pl.when(c == 0)(home_same.wait)
    mgs[...] = lax.dot_general(
        pick[...].reshape(1280, 256), rl[...].reshape(1280, 1024), TN, preferred_element_type=F32
    )
    away = rows((1 - c) * 128, 128)
    own = rows(c * 128, 128)
    back_near = [
        to(ggt.at[:, away], gg_in, sx.at[3], rx.at[3], b, sib),
        to(mgs.at[away], mg_in, sx.at[2], rx.at[2], b, sib),
    ]
    for item in back_near:
        item.start()
    settle_rows(s1.at[0], xs, c)
    settle_rows(s2.at[0], gs, c)
    settle_rows(s3.at[0], rs, c)
    settle_rows(s4.at[0], ggs, c)
    back_near[0].wait()

    gg_all[...] = jnp.zeros_like(gg_all)
    for k in range(16):
        gg_all[pl.ds(2 * k + odd, 1)] = ggt[pl.ds(k, 1), own]
        gg_all[pl.ds(2 * k + 1 - odd, 1)] = gg_in[pl.ds(k, 1)]
    gate_grad = gg_all[...].T
    own_gates = gates[...]
    logit_grad = own_gates * (
        gate_grad - jnp.sum(own_gates * gate_grad, axis=1, keepdims=True)
    )
    router_out[...] = lax.dot_general(
        logit_grad, mixed[...].astype(F32), TN, preferred_element_type=F32, precision=PRECISE
    )[0:NB]
    routed = jnp.dot(
        logit_grad, router[...], preferred_element_type=F32, precision=PRECISE
    )
    back_near[1].wait()
    mixed_grad = mgs[own] + mg_in[...] + routed
    middle = middle_ref[...]
    scale = row_scale(middle)
    unit = middle * scale
    small_out[...] = jnp.sum(mixed_grad * unit, axis=0, keepdims=True)
    inner = mixed_grad * ffn_gain[...]
    grad = cot[...].astype(F32) + scale * (
        inner - unit * jnp.mean(inner * unit, axis=1, keepdims=True)
    )
    grad_out[...] = grad
    low_out[...] = grad.astype(BF16)


def backward_kernel(
    lengths, attn_grad, context, wv, far, q_ref, kv_ref, wide_ref, inv_ref, eo, ex,
    raw, normed, li2, head_gain, turn, attn_gain, ffn_part, wts, middle, grad, router_part,
    out, in_grad, w_out, wo_grad, small_out, router_out, ex_out,
    cg, cgs, qp, gp, gi, qt, gt, gti, dt, di, dqs, dkvt, stage, dq_acc,
    wo_other, wo_in, wo_sum, ex_in, ex_sum, ex_cross, dq, dkv, home, wo_parts,
    low, w_other, w_in, w_sum, w_land, back, back_in, mix, mix_in, small, four, many,
    r_land, r_four, r_tot,
    s1, r1, s2, r2, s3, r3, s4, r4, s5, r5, s6, r6, s7, r7, s8, r8, s9, r9, sa, ra, sx, rx, ls,
):
    b, xl, c, y, m = place()
    h = 2 * xl + c
    sib = 2 * xl + 1 - c
    over = 2 * (1 - xl) + c
    e0, e1, total = lengths[0], lengths[0] + lengths[1], 512 * NB
    bar = pltpu.get_barrier_semaphore()
    for dj in range(GROUP):
        j = member(m, lax.rem(y + dj, GROUP))
        signal(bar, j, 2 * (1 - xl) + 1 - c)
        signal(bar, j, 2 * xl + 1 - c)
    times(1, NB, lambda d: signal(bar, lax.rem(b + d, NB), h))
    times(0, NB, lambda d: signal(bar, lax.rem(b + d, NB), over))
    pl.semaphore_wait(bar, 2 * NB - 1 + 2 * GROUP)

    ex_swap = to(ex.at[:, rows((1 - c) * 512, 512)], ex_in, sx.at[1], rx.at[1], b, sib)
    ex_swap.start()
    ex_own = pltpu.make_async_copy(ex.at[:, rows(c * 512, 512)], ex_sum, ls.at[1])
    ex_own.start()
    turned_back = jnp.zeros((128, 1024), F32)
    for i in range(2):
        for x2, part in ((xl, wv[i, :, 512:768]), (1 - xl, far[i])):
            turned_back = turned_back + lax.dot_general(
                attn_grad[:, rows(512 * x2 + 256 * i, 256)], part, NT, preferred_element_type=F32
            )
    cg[...] = turned_back.astype(BF16)
    turns = [(dj, dx, dc) for dj in range(GROUP) for dx in range(2) for dc in range(2)]
    cg_pieces = []
    for k, (dj, dx, dc) in enumerate(turns):
        j = lax.rem(y + dj, GROUP)
        x2 = lax.rem(xl + dx, 2)
        cols = pl.ds(pl.multiple_of((4 * x2 + j) * 128, 128), 128)
        src, dst = cg.at[:, cols], cgs.at[y, rows(c * 256 + xl * 128, 128)]
        if k == 0:
            cg_pieces.append(pltpu.make_async_copy(src, dst, ls.at[0]))
        else:
            head = 2 * x2 + lax.rem(c + dc, 2)
            cg_pieces.append(to(src, dst, s1.at[0], r1.at[0], member(m, j), head))
    for item in cg_pieces:
        item.start()

    def tile(n):
        return router_part.at[rows(8 * (n // 8), 8), rows(128 * lax.rem(n, 8), 128)]

    def router_first(d):
        to_b = lax.rem(b + d, NB)
        return to(tile(to_b), r_land.at[b], s8.at[0], r8.at[0], to_b, h)

    times(1, NB, lambda d: router_first(d).start())
    r_land[b] = router_part[rows(8 * (b // 8), 8), rows(128 * lax.rem(b, 8), 128)]

    def out_part(x2, core):
        cols = pl.ds(pl.multiple_of(512 * x2 + 256 * core, 256), 256)
        return lax.dot_general(
            context[...], attn_grad[:, cols], TN, preferred_element_type=F32
        )

    for x2 in range(2):
        wo_other[x2] = out_part(x2, 1 - c).astype(BF16)
    wo_swap = to(wo_other, wo_in, sx.at[0], rx.at[0], b, sib)
    wo_swap.start()
    for i in range(GROUP):
        both = q_ref[i].astype(F32)
        pad_queries(both, qp, i)
        turned = both.T
        qt[i] = jnp.concatenate([turned[0:64], turned[64:128]], axis=1).astype(BF16)
    dq_acc[...] = jnp.zeros_like(dq_acc)
    wo_swap.wait()
    for x2 in range(2):
        wo_sum[x2] = (out_part(x2, c) + wo_in[x2].astype(F32)).astype(BF16)
    ex_swap.wait()
    ex_own.wait()
    ex_sum[...] = (ex_sum[...].astype(F32) + ex_in[...].astype(F32)).astype(BF16)
    cross = to(ex_sum, ex_cross, sx.at[2], rx.at[2], b, over)
    cross.start()

    def wo_piece(e):
        d, x2 = lax.rem(e, NB), lax.rem(xl + e // NB, 2)
        peer_b = lax.rem(b + d, NB)
        part = wo_sum.at[x2, rows(peer_b * 32, 32)]
        return to(part, wo_parts.at[NB * (e // NB) + b], s3.at[0], r3.at[0], peer_b, 2 * x2 + c)

    cg_pieces[0].wait()
    settle(r1.at[0], home.at[pl.ds(0, 3)])
    wo_parts[b] = wo_sum[xl, rows(b * 32, 32)]
    eo_piece = rows_home(eo, home, b, xl, c, s2.at[0], r2.at[0])
    eo_same = pltpu.make_async_copy(eo.at[15], home.at[b // 2], ls.at[2])
    times(1, 17, lambda d: start_rows(eo_piece, d, c, eo_same))
    times(1, 2 * NB, lambda e: wo_piece(e).start())
    left = lax.broadcasted_iota(jnp.int32, (512, 128), 1) < 64
    for i in range(GROUP):
        scaled = cgs[i].astype(F32) * inv_ref[i]
        pos = query_positions((512, 1), 0, member(m, i))
        mid_doc = (pos >= e0) & (pos < e1)
        terms = scaled * wide_ref[i]
        one = jnp.sum(jnp.where(left, terms, 0.0), axis=1, keepdims=True)
        two = jnp.sum(jnp.where(left, 0.0, terms), axis=1, keepdims=True)
        upper = jnp.where(left, 0.0, pltpu.roll(scaled, 64, 1))
        lower = jnp.where(left, 0.0, scaled)
        for part, val, term in ((0, upper, one), (512, lower, two)):
            span = pl.ds(part, 512)
            gp[i, span] = val.astype(BF16)
            gi[i, span] = jnp.where(mid_doc, val, 0.0).astype(BF16)
            dt[i, span] = jnp.broadcast_to(term, (512, 128))
            di[i, span] = jnp.broadcast_to(jnp.where(mid_doc, term, 0.0), (512, 128))
            lanes = pl.ds(part, 512)
            gt[i, :, lanes] = val.T[64:128].astype(BF16)
            gti[i, :, lanes] = jnp.where(mid_doc, val, 0.0).T[64:128].astype(BF16)

    def dkv_piece(kb):
        return to(stage.at[kb], dkv.at[b], s4.at[0], r4.at[0], kb, h)

    def pair(dp):
        p = lax.rem(b // 2 + 1 + dp, 16)
        dkvt[...] = jnp.zeros_like(dkvt)
        keys = kv_ref[pl.ds(2 * p, 2)].reshape(512, 128)

        def step(i, expo, g, gturn, dots):
            prob = lax.dot_general(g[i], keys, NT, preferred_element_type=F32)
            term = jnp.concatenate([dots[i]] * 4, axis=1)
            score_grad = (expo * (prob - term)).astype(BF16)
            dq_acc[i] += jnp.dot(score_grad, keys, preferred_element_type=F32)
            dkvt[0:64] += jnp.dot(qt[i], score_grad, preferred_element_type=F32)
            dkvt[64:128] += jnp.dot(gturn[i], expo.astype(BF16), preferred_element_type=F32)

        def scores(i):
            return jnp.exp(lax.dot_general(qp[i], keys, NT, preferred_element_type=F32))

        def inside(i):
            step(i, scores(i), gi, gti, di)

        def edge(i, qb):
            low, high = limits(query_positions((1024, 1), 0, qb), e0, e1, total)
            kpos = key_positions((1, 512), 1, 2 * p, c)
            expo = jnp.where((kpos >= low) & (kpos < high), scores(i), 0.0)
            step(i, expo, gp, gt, dt)

        on_pair(p, m, inside, edge)
        flat = dkvt[...].T.astype(BF16)
        for n in range(2):
            kb = 2 * p + n
            stage[kb] = flat[256 * n : 256 * n + 256]

            @pl.when(kb != b)
            def _():
                dkv_piece(kb).start()

    times(0, 6, pair)
    settle(r8.at[0], r_land.at[pl.ds(0, NB - 1)])
    part = r_land[0]
    for n in range(1, NB):
        part = part + r_land[n]
    r_four[h] = part
    router_near = [
        to(r_four.at[h], r_four.at[h], s9.at[d], r9.at[d], b, lax.rem(h + d, 4))
        for d in range(1, 4)
    ]
    for item in router_near:
        item.start()
    times(6, 11, pair)
    for item in router_near:
        item.wait()
    r_tot[...] = r_four[0] + r_four[1] + r_four[2] + r_four[3]
    home_tile = (rows(8 * (b // 8), 8), rows(128 * lax.rem(b, 8), 128))
    router_out[home_tile] = r_tot[...]

    def router_last(d):
        return to(r_tot, router_out.at[home_tile], sa.at[0], ra.at[0], lax.rem(b + d, NB), h)

    times(1, NB, lambda d: router_last(d).start())
    times(11, 16, pair)
    dkv[b] = stage[b]
    for i in range(GROUP):
        both = jnp.where(left, dq_acc[i, 0:512], pltpu.roll(dq_acc[i, 512:1024], 64, 1))
        dqs[i] = (both * SCALE).astype(BF16)

    def dq_piece(dj, dc):
        j = lax.rem(y + dj, GROUP)
        c2 = lax.rem(c + dc, 2)
        cols = pl.ds(pl.multiple_of(y * 128, 128), 128)
        src, dst = dqs.at[j, rows(c2 * 256, 256)], dq.at[c, :, cols]
        k = 2 * dj + dc
        if k == 0:
            return pltpu.make_async_copy(src, dst, ls.at[4])
        return to(src, dst, s5.at[k], r5.at[k], member(m, j), 2 * xl + c2)

    dq_pieces = [dq_piece(dj, dc) for dj in range(GROUP) for dc in range(2)]
    for item in dq_pieces:
        item.start()
    cross.wait()
    ex_in[...] = (ex_sum[...].astype(F32) + ex_cross[...].astype(F32)).astype(BF16)
    half = rows(c * 512, 512)
    ex_home = pltpu.make_async_copy(ex_in, ex_out.at[:, half], ls.at[5])
    ex_home.start()
    ex_back = to(ex_in, ex_out.at[:, half], sx.at[3], rx.at[3], b, sib)
    ex_back.start()
    for item in dq_pieces:
        item.wait()
    settle(r4.at[0], dkv.at[pl.ds(0, NB - 1)])

    left, first = lanes_of((256, 128))
    q_gain = jnp.zeros((1, 128), F32)
    k_gain = jnp.zeros((1, 128), F32)

    def unprep(d, u, gain, row):
        turned = d * turn[0] - swapped(d, first) * turn[1]
        scale = lax.rsqrt(by_head(u * u, left) + EPSILON)
        unit = u * scale
        inner = turned * row
        gain = gain + jnp.sum(turned * unit, axis=0, keepdims=True)
        return scale * (inner - unit * by_head(inner * unit, left)), gain

    for j in range(GROUP):
        i, q_cols, kv_cols = slab(j)
        span = slice(128 * j, 128 * j + 128)
        d = (dq[0, :, span].astype(F32) + dq[1, :, span].astype(F32)).astype(BF16).astype(F32)
        got, q_gain = unprep(d, raw[i, :, q_cols], q_gain, head_gain[0:1])
        low[i, :, q_cols] = got.astype(BF16)
        d = dkv[8 * j].astype(F32)
        for n in range(1, 8):
            d = d + dkv[8 * j + n].astype(F32)
        d = d.astype(BF16).astype(F32)
        got, k_gain = unprep(d, raw[i, :, kv_cols], k_gain, head_gain[1:2])
        low[i, :, kv_cols] = jnp.where(left, got, d).astype(BF16)
    w_other[...] = lax.dot_general(
        normed[...], low[1 - c], TN, preferred_element_type=F32
    ).astype(BF16).reshape(NB, 32, 512)
    w_swap = to(w_other, w_in, sx.at[4], rx.at[4], b, sib)
    w_swap.start()
    normed_grad = lax.dot_general(low[0], wv[0, :, 0:512], NT, preferred_element_type=F32) + lax.dot_general(
        low[1], wv[1, :, 0:512], NT, preferred_element_type=F32
    )
    source2 = li2[...].reshape(256, 1024).astype(F32)
    scale = row_scale(source2)
    unit = source2 * scale
    inner = normed_grad * attn_gain[...]
    back[...] = (scale * (inner - unit * jnp.mean(inner * unit, axis=1, keepdims=True))).reshape(
        2, 128, 1024
    )
    back_swap = to(back.at[1 - xl], back_in, sx.at[5], rx.at[5], b, over)
    back_swap.start()
    small[:, 0:1024] = jnp.sum(normed_grad * unit, axis=0, keepdims=True)
    small[:, 1024:2048] = ffn_part[...]
    small[:, 2048:2176] = q_gain
    small[:, 2176:2304] = k_gain
    near = [
        to(small, four.at[h], sx.at[6 + d], rx.at[6 + d], b, lax.rem(h + d, 4)) for d in range(1, 4)
    ]
    for item in near:
        item.start()
    four[h] = small[...]
    mine = lax.dot_general(normed[...], low[c], TN, preferred_element_type=F32)
    w_swap.wait()
    w_sum[...] = (mine.reshape(NB, 32, 512) + w_in[...].astype(F32)).astype(BF16)

    def w_piece(d):
        peer = lax.rem(b + d, NB)
        return to(w_sum.at[peer], w_land.at[b], s6.at[0], r6.at[0], peer, h)

    times(1, NB, lambda d: w_piece(d).start())
    w_land[b] = w_sum[b]
    for item in near:
        item.wait()
    many[b] = four[0] + four[1] + four[2] + four[3]

    def spread(d):
        return to(many.at[b], many.at[b], s7.at[0], r7.at[0], lax.rem(b + d, NB), h)

    times(1, NB, lambda d: spread(d).start())

    settle_rows(r2.at[0], home, c)
    pl.when(c == 0)(eo_same.wait)
    flat = home[...].reshape(1280, 1024)
    mix[...] = (
        lax.dot_general(wts[0].reshape(1280, 256), flat, TN, preferred_element_type=F32)
        + lax.dot_general(wts[1].reshape(1280, 256), flat, TN, preferred_element_type=F32)
    ).reshape(2, 128, 1024)
    mix_swap = to(mix.at[1 - c], mix_in, sx.at[6], rx.at[6], b, sib)
    mix_swap.start()
    settle(r3.at[0], wo_parts.at[pl.ds(0, 2 * NB - 1)])
    total = wo_parts[0].astype(F32)
    for n in range(1, 2 * NB):
        total = total + wo_parts[n].astype(F32)
    wo_grad[...] = total
    back_swap.wait()
    in_grad[...] = (grad[...] + back[xl] + back_in[...]).astype(BF16)
    mix_swap.wait()
    out[...] = (middle[...] + mix[c] + mix_in[...]).astype(BF16)
    settle(r7.at[0], many.at[pl.ds(0, NB - 1)])
    total = many[0]
    for n in range(1, NB):
        total = total + many[n]
    small_out[...] = total
    settle(r6.at[0], w_land.at[pl.ds(0, NB - 1)])
    shard = w_land[0].astype(F32)
    for n in range(1, NB):
        shard = shard + w_land[n].astype(F32)
    w_out[...] = shard
    ex_home.wait()
    ex_back.wait()
    settle(ra.at[0], r_land.at[pl.ds(0, NB - 1)])
    settle(s1.at[0], home.at[pl.ds(0, 3)])
    settle_rows(s2.at[0], home, c)
    settle(s3.at[0], wo_parts.at[pl.ds(0, 2 * NB - 1)])
    settle(s4.at[0], dkv.at[pl.ds(0, NB - 1)])
    settle(s6.at[0], w_land.at[pl.ds(0, NB - 1)])
    settle(s7.at[0], many.at[pl.ds(0, NB - 1)])
    settle(s8.at[0], r_land.at[pl.ds(0, NB - 1)])
    settle(sa.at[0], r_land.at[pl.ds(0, NB - 1)])


VM = pl.BlockSpec(memory_space=pltpu.VMEM)
SM = pl.BlockSpec(memory_space=pltpu.SMEM)
ANY = pl.BlockSpec(memory_space=pl.ANY)


def call(kernel, collective_id, ins, outs, scratch, sems, flops, *operands):
    return pl.pallas_call(
        kernel,
        out_shape=[jax.ShapeDtypeStruct(shape, dtype) for shape, dtype, _ in outs],
        in_specs=ins,
        out_specs=[spec for _, _, spec in outs],
        scratch_shapes=[pltpu.VMEM(shape, dtype) for shape, dtype in scratch]
        + [pltpu.SemaphoreType.DMA(n) for n in sems],
        compiler_params=pltpu.CompilerParams(
            collective_id=collective_id,
            has_side_effects=True,
            vmem_limit_bytes=60 * 1024 * 1024,
        ),
        cost_estimate=pl.CostEstimate(
            flops=flops, bytes_accessed=8_000_000, transcendentals=flops // 2000
        ),
    )(*operands)


def limits(pos, e0, e1, total):
    low = jnp.where(pos < e0, 0, jnp.where(pos < e1, e0, e1))
    end = jnp.where(pos < e0, e0, jnp.where(pos < e1, e1, total))
    reach = low + ((pos - low) // BLOCK + 1) * BLOCK
    return low, jnp.minimum(end, reach)


def query_positions(shape, axis, qb):
    r = lax.broadcasted_iota(jnp.int32, shape, axis)
    r = lax.rem(r, 512)
    return 512 * qb + 256 * lax.rem(r // 128, 2) + 128 * (r // 256) + lax.rem(r, 128)


def key_positions(shape, axis, kb, core):
    r = lax.broadcasted_iota(jnp.int32, shape, axis)
    return 512 * (kb + r // 256) + 256 * lax.rem(r // 128, 2) + 128 * core + lax.rem(r, 128)


def body(
    layer_input,
    attn_gain,
    w_query,
    key_weight,
    value_weight,
    w_output,
    query_gain,
    key_gain,
    ffn_gain,
    router,
    w_gate,
    w_up,
    w_down,
    routes,
    doc_lengths,
    cotangent,
):
    tokens, width = layer_input.shape
    lane = np.arange(128) % (HEAD_SIZE // 2)
    pace = jnp.asarray(ROPE_BASE ** (-2.0 * lane / HEAD_SIZE), F32)[None]
    (
        w_full, w_far, both_inputs, q_group, kv_all, up_rows,
        pick, raw, normed, ctx_wide, ctx_inv, context, middle, mixed_in, gates, turn, head_gain, router_wide,
    ) = call(
        forward_kernel,
        0,
        [SM] + [VM] * 13,
        [
            ((2, width, 768), BF16, ANY),
            ((2, width, width // 4), BF16, ANY),
            ((2, tokens, width), BF16, ANY),
            ((GROUP, 512, 128), BF16, ANY),
            ((NB, 256, 128), BF16, ANY),
            ((16, SLOTS, width), BF16, ANY),
            ((16, SLOTS, 2 * tokens), BF16, VM),
            ((2, 2 * tokens, 512), F32, VM),
            ((2 * tokens, width), BF16, VM),
            ((GROUP, 512, 128), F32, VM),
            ((GROUP, 512, 128), F32, VM),
            ((tokens, width), BF16, VM),
            ((tokens, width), F32, VM),
            ((tokens, width), BF16, VM),
            ((tokens, 128), F32, VM),
            ((2, 2 * tokens, 128), F32, VM),
            ((2, 128), F32, VM),
            ((128, width), F32, VM),
        ],
        [
            ((32, 768), BF16),
            ((2, width, 768), BF16),
            ((2, width, width // 4), BF16),
            ((2, tokens, width), BF16),
            ((2 * tokens, width), BF16),
            ((2, 8, 128), jnp.int32),
            ((16, SLOTS, width), BF16),
            ((2 * tokens, 512), BF16),
            ((2 * tokens, 512), BF16),
            ((GROUP, 512, 128), BF16),
            ((NB, 256, 128), BF16),
            ((GROUP, 1024, 128), BF16),
            ((80, 512), BF16),
            ((GROUP, 80, 1024), F32),
            ((GROUP, 80, 1024), F32),
            ((GROUP, 80, 1024), F32),
            ((GROUP, 512, 128), BF16),
            ((tokens, width), BF16),
        ],
        [(1,)] * 2 + [(7,)] * 2 + [(8,)] * 2 + [(1,), (NB,)] + [(1,)] * 2 + [(8,)] * 2 + [(9,)],
        18_000_000_000,
        doc_lengths,
        w_query,
        key_weight,
        value_weight,
        w_output,
        layer_input,
        cotangent,
        routes.T,
        attn_gain[None],
        query_gain[None],
        key_gain[None],
        pace,
        ffn_gain[None],
        router.T,
    )
    wts, expert_out, ex_grads, middle_grad, attn_grad, ffn_part, router_part = call(
        experts_kernel,
        1,
        [VM] * 11,
        [
            ((2, 16, SLOTS, 2 * tokens), BF16, VM),
            ((16, SLOTS, width), BF16, VM),
            ((3, 1024, 512), BF16, VM),
            ((tokens, width), F32, VM),
            ((tokens, width), BF16, VM),
            ((1, width), F32, VM),
            ((NB, width), F32, VM),
        ],
        [
            ((2 * tokens, width), BF16),
            ((2 * tokens, 128), F32),
            ((16, SLOTS, width), BF16),
            ((16, SLOTS, width), BF16),
            ((16, 8, 128), F32),
            ((16, 8, 128), F32),
            ((16, SLOTS, width), BF16),
            ((16, SLOTS, width), BF16),
            ((16, 8, 128), F32),
            ((16, 8, 128), F32),
            ((16 * SLOTS, 512), BF16),
            ((16 * SLOTS, 512), BF16),
            ((16 * SLOTS, 512), BF16),
            ((16 * SLOTS, width), BF16),
            ((2 * tokens, width), F32),
            ((16, 2 * tokens), F32),
            ((tokens, width), F32),
            ((16, tokens), F32),
            ((128, tokens), F32),
        ],
        [(1,), (4,), (1,), (4,)] + [(1,)] * 4 + [(4,)] * 2 + [(4,)],
        12_000_000_000,
        mixed_in,
        gates,
        pick,
        up_rows,
        w_gate,
        w_up,
        w_down,
        middle,
        cotangent,
        ffn_gain[None],
        router_wide,
    )
    layer_output, input_grad, w_shard, w_output_grad, smalls, router_grad, ex_sums = call(
        backward_kernel,
        2,
        [SM] + [VM] * 8 + [ANY, ANY] + [VM] * 11,
        [
            ((tokens, width), BF16, VM),
            ((tokens, width), BF16, VM),
            ((width // NB, 512), F32, VM),
            ((32, 256), F32, VM),
            ((1, 2304), F32, VM),
            ((NB, width), F32, VM),
            ((3, 1024, 512), BF16, ANY),
        ],
        [
            ((tokens, width), BF16),
            ((GROUP, 512, 128), BF16),
            ((GROUP, 1024, 128), BF16),
            ((GROUP, 1024, 128), BF16),
            ((GROUP, 1024, 128), BF16),
            ((GROUP, 64, 1024), BF16),
            ((GROUP, 64, 1024), BF16),
            ((GROUP, 64, 1024), BF16),
            ((GROUP, 1024, 128), F32),
            ((GROUP, 1024, 128), F32),
            ((GROUP, 512, 128), BF16),
            ((128, 512), F32),
            ((NB, 256, 128), BF16),
            ((GROUP, 1024, 128), F32),
            ((2, 1024, 256), BF16),
            ((2, 1024, 256), BF16),
            ((2, 1024, 256), BF16),
            ((3, 512, 512), BF16),
            ((3, 512, 512), BF16),
            ((3, 512, 512), BF16),
            ((2, 2 * tokens, 512), BF16),
            ((NB, 256, 128), BF16),
            ((16, SLOTS, width), BF16),
            ((2 * NB, 32, 256), BF16),
            ((2, 2 * tokens, 512), BF16),
            ((NB, 32, 512), BF16),
            ((NB, 32, 512), BF16),
            ((NB, 32, 512), BF16),
            ((NB, 32, 512), BF16),
            ((2, tokens, width), F32),
            ((tokens, width), F32),
            ((2, tokens, width), F32),
            ((tokens, width), F32),
            ((1, 2304), F32),
            ((4, 1, 2304), F32),
            ((NB, 1, 2304), F32),
            ((NB, 8, 128), F32),
            ((4, 8, 128), F32),
            ((8, 128), F32),
        ],
        [(1,)] * 8 + [(8,)] * 2 + [(1,)] * 6 + [(4,)] * 2 + [(1,)] * 2 + [(10,)] * 2 + [(6,)],
        45_000_000_000,
        doc_lengths,
        attn_grad,
        context,
        w_full,
        w_far,
        q_group,
        kv_all,
        ctx_wide,
        ctx_inv,
        expert_out,
        ex_grads,
        raw,
        normed,
        both_inputs,
        head_gain,
        turn,
        attn_gain[None],
        ffn_part,
        wts,
        middle,
        middle_grad,
        router_part,
    )
    smalls = smalls[0]
    down_sum = jnp.concatenate([ex_sums[2, :512], ex_sums[2, 512:]], axis=1)
    return (
        layer_output,
        input_grad,
        smalls[:1024],
        w_shard[:, :256],
        jnp.concatenate([w_shard[:, 256:320], w_shard[:, 384:448]], axis=1),
        jnp.concatenate([w_shard[:, 320:384], w_shard[:, 448:512]], axis=1),
        w_output_grad,
        smalls[2048:2112] + smalls[2112:2176],
        smalls[2176:2240],
        smalls[1024:2048],
        router_grad.T,
        ex_sums[0].astype(F32)[None],
        ex_sums[1].astype(F32)[None],
        down_sum.astype(F32)[None],
    )


def solution(mesh):
    everyone = P(("blk", "head"), None)
    both = P("blk", "head")
    expert = P("blk", None, None)
    return jax.shard_map(
        body,
        mesh=mesh,
        in_specs=(everyone, P(), both, both, both, both, P(), P(), P(), P())
        + (expert, expert, expert, everyone, P(), everyone),
        out_specs=(everyone, everyone, P(), both, both, both, both, P(), P(), P(), P())
        + (expert, expert, expert),
        check_vma=False,
    )
```

```python
import jax
import jax.numpy as jnp
import numpy as np
from jax import lax
from jax.experimental import pallas as pl
from jax.experimental.pallas import tpu as pltpu
from jax.sharding import PartitionSpec as P

HEAD_SIZE = 64
TOPK = 8
BLOCK = 256
EPSILON = 1e-06
ROPE_BASE = 10000.0
PRECISE = lax.Precision.HIGHEST
SCALE = HEAD_SIZE ** (-0.5)

NB = 32
ROUNDS = 5
SLOTS = 80
GROUP = 4
MESH_ID = pl.DeviceIdType.MESH
F32 = jnp.float32
BF16 = jnp.bfloat16
NT = (((1,), (1,)), ((), ()))
NN = (((1,), (0,)), ((), ()))
TN = (((0,), (0,)), ((), ()))


def place():
    b = lax.axis_index("blk")
    h = lax.axis_index("head")
    y = b // 8
    r = lax.rem(b, 8)
    m = jnp.where(lax.rem(y, 2) == 0, r, 7 - r)
    return b, h // 2, lax.rem(h, 2), y, m


def member(m, j):
    return 8 * j + m + lax.rem(j, 2) * (7 - 2 * m)


def times(start, n, body):
    def step(i, carry):
        body(i)
        return carry

    lax.fori_loop(start, n, step, 0)


def signal(sem, blk, head):
    pl.semaphore_signal(sem, inc=1, device_id=(blk, head), device_id_type=MESH_ID)


def rows(start, size):
    return pl.ds(pl.multiple_of(start, size), size)


def to(src, dst, send, recv, blk, head):
    return pltpu.make_async_remote_copy(
        src, dst, send, recv, device_id=(blk, head), device_id_type=MESH_ID
    )


def settle(sem, part):
    pltpu.make_async_copy(part, part, sem).wait()


def settle_rows(sem, blocks, c):
    pl.when(c == 0)(lambda: settle(sem, blocks.at[pl.ds(0, 15)]))
    pl.when(c == 1)(lambda: settle(sem, blocks))


def greet_all(bar, b, xl, c, y, m):
    h = 2 * xl + c
    times(1, NB, lambda d: signal(bar, lax.rem(b + d, NB), h))
    times(0, NB, lambda d: signal(bar, lax.rem(b + d, NB), 2 * (1 - xl) + c))
    for dj in range(GROUP):
        j = member(m, lax.rem(y + dj, GROUP))
        signal(bar, j, 2 * xl + 1 - c)
    pl.semaphore_wait(bar, 2 * NB - 1 + GROUP)


def pad_queries(both, qp, i):
    left = lax.broadcasted_iota(jnp.int32, (512, 128), 1) < 64
    qp[i, 0:512] = jnp.where(left, both, 0.0).astype(BF16)
    qp[i, 512:1024] = jnp.where(left, pltpu.roll(both, 64, 1), 0.0).astype(BF16)


def on_pair(p, m, inside, edge):
    def each(i):
        qb = member(m, i)
        whole = (p >= 1) & (2 * p + 1 <= qb - 1)
        pl.when(whole)(lambda: inside(i))
        pl.when(jnp.logical_not(whole) & (2 * p <= qb + 1))(lambda: edge(i, qb))

    times(0, GROUP, each)


def by_head(values, left):
    one = jnp.sum(jnp.where(left, values, 0.0), axis=1, keepdims=True) / HEAD_SIZE
    two = jnp.sum(jnp.where(left, 0.0, values), axis=1, keepdims=True) / HEAD_SIZE
    return jnp.where(left, one, two)


def swapped(values, first):
    return jnp.where(first, pltpu.roll(values, 96, 1), pltpu.roll(values, 32, 1))


def row_scale(values):
    return lax.rsqrt(jnp.mean(values * values, axis=1, keepdims=True) + EPSILON)


def lanes_of(shape):
    lane = lax.broadcasted_iota(jnp.int32, shape, 1)
    return lane < 64, lax.rem(lane, 64) < 32


def slab(j):
    return j // 2, slice(128 * (j % 2), 128 * (j % 2) + 128), slice(
        256 + 128 * (j % 2), 384 + 128 * (j % 2)
    )


def forward_kernel(
    lengths, wq, wk, wvl, wo, li, cot, routes_t, attn_gain, q_gain, k_gain, pace, ffn_gain, router_t,
    w_out, wo_out, li_out, q_out, kv_out, c_out, raw_out, normed_out, wide_out, inv_out, turn_out, router_out,
    pick, ctx_out, mid_out, mixed_out, gates_out, head_gain,
    raw, normed, wide_all, inv_all, turn, router,
    ws, wv, wov, li2, cot2, rt, xs, qs, kvst, qg, kvs, qp, vt, acc, accm, peer, ctx, ctx_in,
    sw, rw, so, ro, sx, rx, s1, r1, s2, r2, s5, r5, s7, r7, ls, lk,
):
    b, xl, c, y, m = place()
    h = 2 * xl + c
    sib = 2 * xl + 1 - c
    over = 2 * (1 - xl) + c
    odd = lax.rem(b + c, 2)
    e0, e1, total = lengths[0], lengths[0] + lengths[1], 512 * NB
    pairs = jnp.concatenate([wk[...].astype(F32), wvl[...].astype(F32)], axis=1)
    even = jnp.concatenate([pairs[:, 0:64], pairs[:, 128:192]], axis=1)
    other = jnp.concatenate([pairs[:, 64:128], pairs[:, 192:256]], axis=1)
    ws[:, 0:256] = wq[...]
    ws[:, 256:384] = even.astype(BF16)
    ws[:, 384:512] = other.astype(BF16)
    greet_all(pltpu.get_barrier_semaphore(), b, xl, c, y, m)

    def w_first(d):
        part = wv.at[c, rows(b * 32, 32)]
        return to(ws, part, sw.at[0], rw.at[0], lax.rem(b + d, NB), h)

    def wo_first(d):
        part = wov.at[0, c, rows(b * 32, 32)]
        return to(wo, part, so.at[0], ro.at[0], lax.rem(b + d, NB), h)

    keeps = []

    def keep(part, out):
        item = pltpu.make_async_copy(part, out, lk.at[len(keeps)])
        item.start()
        keeps.append(item)

    near = [
        to(routes_t, rt.at[c], sx.at[0], rx.at[0], b, sib),
        to(cot, cot2.at[rows(c * 128, 128)], sx.at[1], rx.at[1], b, sib),
        to(li, li2.at[xl], sx.at[2], rx.at[2], b, over),
    ]
    for item in near:
        item.start()
    times(1, NB, lambda d: w_first(d).start())
    wv[c, rows(b * 32, 32)] = ws[...]
    li2[xl] = li[...]
    cot2[rows(c * 128, 128)] = cot[...]
    rt[c] = routes_t[...]

    near[0].wait()
    both_routes = jnp.concatenate([rt[0], rt[1]], axis=1)
    mine = 2 * lax.broadcasted_iota(jnp.int32, (16, 256), 0) + odd
    chosen = jnp.zeros((16, 256), F32)
    for k in range(TOPK):
        chosen = jnp.where(both_routes[k : k + 1] == mine, 1.0, chosen)
    earlier = lax.broadcasted_iota(jnp.int32, (256, 256), 0) < lax.broadcasted_iota(
        jnp.int32, (256, 256), 1
    )
    rank = jnp.dot(
        chosen.astype(BF16), jnp.where(earlier, 1.0, 0.0).astype(BF16), preferred_element_type=F32
    )
    slot = lax.broadcasted_iota(jnp.int32, (80, 256), 0).astype(F32)
    for k in range(16):
        at = jnp.where(rank[k : k + 1] == slot, chosen[k : k + 1], 0.0)
        pick[k] = at.astype(BF16)
    near[1].wait()
    c_piece = rows_out(xs, c_out, b, xl, c, lambda r: s5.at[0], lambda r: r5.at[0])
    c_same = pltpu.make_async_copy(xs.at[b // 2], c_out.at[15], ls.at[3])

    def fetch(d):
        k = stride(b, d)
        xs[k] = jnp.dot(pick[k], cot2[...], preferred_element_type=F32).astype(BF16)

    times(1, 17, fetch)
    pl.when(c == 0)(c_same.start)

    near[2].wait()
    keep(li2, li_out)
    source2 = li2[...].reshape(256, 1024).astype(F32)
    normed[...] = (source2 * row_scale(source2) * attn_gain[...]).astype(BF16)

    keep(normed, normed_out)
    settle(rw.at[0], wv.at[c, rows(0, 992)])
    w_sib = to(wv.at[c], wv.at[c], sx.at[3], rx.at[3], b, sib)
    w_sib.start()
    wov[0, c, rows(b * 32, 32)] = wo[...]
    left, first = lanes_of((256, 128))
    t = lax.broadcasted_iota(jnp.int32, (256, 128), 0)
    pos = 512 * b + 256 * (t // 128) + 128 * c + lax.rem(t, 128)
    opening = jnp.where(pos < e0, 0, jnp.where(pos < e1, e0, e1))
    angles = (pos - opening).astype(F32) * pace[...]
    turn[0] = jnp.cos(angles)
    sine = jnp.sin(angles)
    turn[1] = jnp.where(first, -sine, sine)
    head_gain[0:1] = jnp.concatenate([q_gain[...], q_gain[...]], axis=1)
    head_gain[1:2] = jnp.concatenate([k_gain[...], jnp.ones((1, 64), F32)], axis=1)
    router[...] = jnp.zeros_like(router)
    router[0:NB] = router_t[...]
    keep(turn, turn_out)
    keep(router, router_out)
    w_sib.wait()
    keep(wv, w_out)
    for i in range(2):
        raw[i] = jnp.dot(normed[...], wv[i], preferred_element_type=F32)
    for j in range(GROUP):
        i, q_cols, kv_cols = slab(j)
        span = slice(128 * j, 128 * j + 128)
        u = raw[i, :, q_cols]
        n = u * lax.rsqrt(by_head(u * u, left) + EPSILON) * head_gain[0:1]
        turned = n * turn[0] + swapped(n, first) * turn[1]
        qs[:, span] = (turned.astype(BF16).astype(F32) * SCALE).astype(BF16)
        u = raw[i, :, kv_cols]
        n = u * lax.rsqrt(by_head(u * u, left) + EPSILON) * head_gain[1:2]
        turned = n * turn[0] + swapped(n, first) * turn[1]
        kvst[:, span] = jnp.where(left, turned, u).astype(BF16)

    def q_piece(dj, dc):
        j = lax.rem(y + dj, GROUP)
        cols = pl.ds(pl.multiple_of(j * 128, 128), 128)
        k = 2 * dj + dc
        src, dst = qs.at[:, cols], qg.at[y, rows(c * 256, 256)]
        if k == 0:
            return pltpu.make_async_copy(src, dst, ls.at[0])
        return to(src, dst, s1.at[k], r1.at[k], member(m, j), 2 * xl + lax.rem(c + dc, 2))

    q_pieces = [q_piece(dj, dc) for dj in range(GROUP) for dc in range(2)]

    def kv_piece(i):
        d, half = lax.rem(i, NB), rows(128 * (i // NB), 128)
        peer_b = lax.rem(b + d, NB)
        cols = pl.ds(pl.multiple_of((peer_b // 8) * 128, 128), 128)
        return to(kvst.at[half, cols], kvs.at[b, half], s2.at[0], r2.at[d], peer_b, h)

    for item in q_pieces:
        item.start()
    own_cols = pl.ds(pl.multiple_of(y * 128, 128), 128)
    kv_own = pltpu.make_async_copy(kvst.at[:, own_cols], kvs.at[b], ls.at[1])
    kv_own.start()
    times(1, NB, lambda d: kv_piece(d).start())
    times(NB + 1, 2 * NB, lambda i: kv_piece(i).start())
    for item in q_pieces:
        item.wait()
    kv_own.wait()
    keep(qg, q_out)
    keep(raw, raw_out)
    for i in range(GROUP):
        pad_queries(qg[i].astype(F32), qp, i)
    acc[...] = jnp.zeros_like(acc)
    accm[...] = jnp.zeros_like(accm)
    vt[64:80] = jnp.ones((16, 512), BF16)

    def pair(dp):
        p = lax.rem(b // 2 + 16 - dp, 16)
        send_pieces(c_piece, 5 * dp, 5 * dp + 5, c)
        times(jnp.minimum(16 * dp, NB) + (dp == 0), jnp.minimum(16 * dp + 16, NB), lambda d: wo_first(d).start())
        for kb in (2 * p, 2 * p + 1):

            @pl.when(kb != b)
            def _():
                settle(r2.at[lax.rem(b + NB - kb, NB)], kvs.at[kb])

        vt[0:64] = (
            kvs[pl.ds(2 * p, 2)].reshape(512, 128).astype(F32).T[64:128].astype(BF16)
        )

        def scores(i):
            keys = kvs[pl.ds(2 * p, 2)].reshape(512, 128)
            return jnp.exp(lax.dot_general(keys, qp[i], NT, preferred_element_type=F32))

        def inside(i):
            acc[i] += jnp.dot(vt[...], scores(i).astype(BF16), preferred_element_type=F32)

        def edge(i, qb):
            low, high = limits(query_positions((1, 1024), 1, qb), e0, e1, total)
            kpos = key_positions((512, 1), 0, 2 * p, c)
            expo = jnp.where((kpos >= low) & (kpos < high), scores(i), 0.0)
            accm[i] += jnp.dot(vt[...], expo.astype(BF16), preferred_element_type=F32)

        on_pair(p, m, inside, edge)

    times(0, 10, pair)
    settle(ro.at[0], wov.at[0, c, rows(0, 992)])
    wo_moves = [
        to(wov.at[0, c], wov.at[0, c], sx.at[6], rx.at[6], b, sib),
        to(wov.at[0, c], wov.at[1, c], sx.at[4], rx.at[4], b, over),
    ]
    for item in wo_moves:
        item.start()
    times(10, 16, pair)
    for i in range(GROUP):
        pos = query_positions((1, 1024), 1, member(m, i))
        acc[i] = accm[i] + jnp.where((pos >= e0) & (pos < e1), acc[i], 0.0)
    swap = to(acc, peer, sx.at[5], rx.at[5], b, sib)
    swap.start()
    keep(kvs, kv_out)
    for item in wo_moves:
        item.wait()
    far_sib = to(wov.at[1, c], wov.at[1, c], sx.at[7], rx.at[7], b, sib)
    far_sib.start()
    swap.wait()

    def ctx_piece(dj, dx):
        j = lax.rem(y + dj, GROUP)
        x2 = lax.rem(xl + dx, 2)
        cols = pl.ds(pl.multiple_of((4 * xl + y) * 128, 128), 128)
        src, dst = ctx.at[j, rows(c * 256 + x2 * 128, 128)], ctx_in.at[:, cols]
        k = 2 * dj + dx
        if k == 0:
            return pltpu.make_async_copy(src, dst, ls.at[6])
        return to(src, dst, s7.at[k], r7.at[k], member(m, j), 2 * x2 + c)

    ctx_pieces = [ctx_piece(dj, dx) for dj in range(GROUP) for dx in range(2)]
    for i in range(GROUP):
        both = acc[i] + peer[i]
        inverse = 1.0 / both[64:65]
        wide = both[0:64] * inverse
        flat = jnp.concatenate([wide[:, 0:512], wide[:, 512:1024]], axis=0).T
        wide_all[i] = flat
        ctx[i] = flat.astype(BF16)
        spread = jnp.broadcast_to(inverse, (64, 1024))
        inv_all[i] = jnp.concatenate([spread[:, 0:512], spread[:, 512:1024]], axis=0).T
    for item in ctx_pieces:
        item.start()
    keep(wide_all, wide_out)
    keep(inv_all, inv_out)
    far_sib.wait()
    keep(wov, wo_out)
    for item in ctx_pieces:
        item.wait()

    context = ctx_in[...]
    ctx_out[...] = context
    for i in range(2):
        for x2, part in ((xl, wov[0, i]), (1 - xl, wov[1, i])):
            cols = rows(512 * x2 + 256 * i, 256)
            mid_out[:, cols] = li[:, cols].astype(F32) + jnp.dot(
                context, part, preferred_element_type=F32
            )
    middle = mid_out[...]
    mixed = (middle * row_scale(middle) * ffn_gain[...]).astype(BF16)
    mixed_out[...] = mixed
    logits = lax.dot_general(
        mixed.astype(F32), router[...], NT, preferred_element_type=F32, precision=PRECISE
    )
    expert = lax.broadcasted_iota(jnp.int32, (128, 128), 0)
    hit = jnp.zeros((128, 128), F32)
    for k in range(TOPK):
        hit = jnp.where(routes_t[k : k + 1] == expert, 1.0, hit)
    hit = hit.T
    top = jnp.max(jnp.where(hit > 0.0, logits, -1e30), axis=1, keepdims=True)
    weight = jnp.where(hit > 0.0, jnp.exp(logits - top), 0.0)
    gates_out[...] = weight / jnp.sum(weight, axis=1, keepdims=True)

    settle(sw.at[0], wv.at[0, rows(0, 992)])
    settle(so.at[0], wov.at[0, 0, rows(0, 992)])
    settle(s2.at[0], kvs.at[pl.ds(0, NB - 1)])
    settle_rows(s5.at[0], xs, c)
    settle_rows(r5.at[0], xs, c)
    pl.when(c == 0)(c_same.wait)
    for item in keeps:
        item.wait()


def row_peer(b, xl, c, k):
    e = 2 * k + lax.rem(b + c, 2)
    apart = lax.rem(b // 4 + e // 4, 2)
    return e, 2 * (xl + apart - 2 * xl * apart) + c


def stride(b, d):
    return lax.rem(b // 2 + 5 * d, 16)


def rows_out(src, dst, b, xl, c, send, recv):
    def piece(d, r):
        k = stride(b, d)
        e, head = row_peer(b, xl, c, k)
        if src.shape[1] < 16:
            return to(src.at[k], dst.at[d - 1], send(r), recv(r), e, head)
        part = rows(16 * r, 16)
        return to(src.at[k, part], dst.at[d - 1, part], send(r), recv(r), e, head)

    return piece


def rows_home(src, dst, b, xl, c, send, recv):
    def piece(d, r):
        e, head = row_peer(b, xl, c, stride(b, 16 - d))
        if src.shape[1] < 16:
            return to(src.at[d - 1], dst.at[b // 2], send(r), recv(r), e, head)
        part = rows(16 * r, 16)
        return to(src.at[d - 1, part], dst.at[b // 2, part], send(r), recv(r), e, head)

    return piece


def send_pieces(piece, start, stop, c):
    def one(i):
        d = lax.rem(i, 16) + 1
        pl.when((d < 16) | (c == 1))(lambda: piece(d, i // 16).start())

    times(start, stop, one)


def start_tiles(piece, d, c, local):
    pl.when((d < 16) | (c == 1))(lambda: piece(d, 0).start())
    pl.when((d == 16) & (c == 0))(local.start)


def experts_kernel(
    mixed, gates, pick, up_hbm, gate_hbm, upw_hbm, down_hbm, middle_hbm, cot_hbm, ffn_gain, router_hbm,
    wts_hbm, eo_hbm, ex_hbm, grad_out, low_out, small_out, router_out,
    up_rows, gate_w, up_w, down_w, middle_ref, cot, router, wts_out, eo_out, ex_out,
    tok, gt, xs, xl_rows, gs, gl, rs, rl, ggs, ggl, hid, gb, ub, og, mgs, ggt, mg_in, gg_in, gg_all, gcol, ggcol,
    s1, r1, s2, r2, s3, r3, s4, r4, sx, rx, ls, li, lo,
):
    b, xl, c, _, _ = place()
    h = 2 * xl + c
    sib = 2 * xl + 1 - c
    odd = lax.rem(b + c, 2)
    brought = [
        pltpu.make_async_copy(src, dst, li.at[n])
        for n, (src, dst) in enumerate(
            (
                (gate_hbm, gate_w),
                (upw_hbm, up_w),
                (down_hbm, down_w),
                (up_hbm, up_rows),
                (middle_hbm, middle_ref),
                (cot_hbm, cot),
                (router_hbm, router),
            )
        )
    ]
    for item in brought:
        item.start()
    bar = pltpu.get_barrier_semaphore()

    def greet(d):
        e, head = row_peer(b, xl, c, stride(b, d))
        signal(bar, e, head)

    times(1, 16, greet)
    signal(bar, b, sib)
    pl.when(c == 1)(lambda: greet(0))
    pl.semaphore_wait(bar, 16 + c)
    near = [
        to(mixed, tok.at[rows(c * 128, 128)], sx.at[0], rx.at[0], b, sib),
        to(gates, gt.at[rows(c * 128, 128)], sx.at[1], rx.at[1], b, sib),
    ]
    for item in near:
        item.start()
    tok[rows(c * 128, 128)] = mixed[...]
    gt[rows(c * 128, 128)] = gates[...]
    near[0].wait()
    x_piece = rows_out(xs, xl_rows, b, xl, c, lambda r: s1.at[0], lambda r: r1.at[r])
    x_same = pltpu.make_async_copy(xs.at[b // 2], xl_rows.at[15], ls.at[0])

    def fetch(d):
        k = stride(b, d)
        xs[k] = jnp.dot(pick[k], tok[...], preferred_element_type=F32).astype(BF16)

    times(1, 17, fetch)
    pl.when(c == 0)(x_same.start)
    send_pieces(x_piece, 0, 32, c)
    near[1].wait()
    high = gt[...].astype(BF16)
    rest = gt[...] - high.astype(F32)
    mid = rest.astype(BF16)
    low = (rest - mid.astype(F32)).astype(BF16)
    g_piece = rows_out(gs, gl, b, xl, c, lambda r: s2.at[0], lambda r: r2.at[0])
    g_same = pltpu.make_async_copy(gs.at[b // 2], gl.at[15], ls.at[1])

    def as_row(column):
        wide = jnp.concatenate([jnp.broadcast_to(column, (80, 128)), jnp.zeros((48, 128), F32)])
        return wide.T[0:8]

    spread = jnp.dot(
        pick[...].reshape(1280, 256),
        jnp.concatenate([high, mid, low], axis=1),
        preferred_element_type=F32,
    )
    spread = spread[:, 0:128] + spread[:, 128:256] + spread[:, 256:384]
    lane = lax.broadcasted_iota(jnp.int32, (1280, 128), 1)
    expert = 2 * (lax.broadcasted_iota(jnp.int32, (1280, 128), 0) // 80) + odd
    column = jnp.sum(jnp.where(lane == expert, spread, 0.0), axis=1, keepdims=True)
    for k in range(16):
        gs[k] = as_row(column[80 * k : 80 * k + 80])
    times(1, 17, lambda d: start_tiles(g_piece, d, c, g_same))
    send_pieces(x_piece, 32, 80, c)
    weights = pick[...].reshape(1280, 256).astype(F32) * column
    weights_high = weights.astype(BF16)
    wts_out[0] = weights_high.reshape(16, 80, 256)
    wts_out[1] = (weights - weights_high.astype(F32)).astype(BF16).reshape(16, 80, 256)
    wts_keep = pltpu.make_async_copy(wts_out, wts_hbm, lo.at[0])
    wts_keep.start()
    for item in brought:
        item.wait()
    home = rows_home(rs, rl, b, xl, c, lambda r: s3.at[0], lambda r: r3.at[0])
    home_same = pltpu.make_async_copy(rs.at[15], rl.at[b // 2], ls.at[2])
    gg_home = rows_home(ggs, ggl, b, xl, c, lambda r: s4.at[0], lambda r: r4.at[0])
    gg_same = pltpu.make_async_copy(ggs.at[15], ggl.at[b // 2], ls.at[3])

    pl.when(c == 0)(x_same.wait)

    def group(r):
        part = rows(16 * r, 16)
        pl.when(c == 0)(lambda: settle(r1.at[r], xl_rows.at[pl.ds(0, 15), part]))
        pl.when(c == 1)(lambda: settle(r1.at[r], xl_rows.at[:, part]))
        x = xl_rows[:, part].reshape(256, 1024)
        u = up_rows[:, part].reshape(256, 1024).astype(F32)
        gate_pre = jnp.dot(x, gate_w[0], preferred_element_type=F32)
        up_pre = jnp.dot(x, up_w[0], preferred_element_type=F32)
        sig = jax.nn.sigmoid(gate_pre)
        act = gate_pre * sig
        hidden = (act * up_pre).astype(BF16)
        out = jnp.dot(hidden, down_w[0], preferred_element_type=F32).astype(BF16)
        eo_out[:, part] = out.reshape(16, 16, 1024)
        gate_grad = jnp.sum(u * out.astype(F32), axis=1, keepdims=True)
        ggcol[:, part] = jnp.broadcast_to(gate_grad, (256, 128)).reshape(16, 16, 128)
        @pl.when(r == 0)
        def _():
            settle_rows(r2.at[0], gl, c)
            pl.when(c == 0)(g_same.wait)
            for n in range(16):
                row = jnp.concatenate([gl[n], jnp.zeros((120, 128), F32)])
                gcol[n] = jnp.broadcast_to(row.T[0:80, 0:1], (80, 128))

        out_grad = (gcol[:, part].reshape(256, 128)[:, 0:1] * u).astype(BF16)
        hidden_grad = lax.dot_general(out_grad, down_w[0], NT, preferred_element_type=F32)
        gate_back = (hidden_grad * up_pre * sig * (1.0 + gate_pre * (1.0 - sig))).astype(BF16)
        up_back = (hidden_grad * act).astype(BF16)
        back = lax.dot_general(
            gate_back, gate_w[0], NT, preferred_element_type=F32
        ) + lax.dot_general(up_back, up_w[0], NT, preferred_element_type=F32)
        rs[:, part] = back.astype(BF16).reshape(16, 16, 1024)
        send_pieces(home, 16 * r, 16 * r + 16, c)
        hid[:, part] = hidden.reshape(16, 16, 512)
        gb[:, part] = gate_back.reshape(16, 16, 512)
        ub[:, part] = up_back.reshape(16, 16, 512)
        og[:, part] = out_grad.reshape(16, 16, 1024)

    times(0, ROUNDS, group)
    pl.when(c == 0)(home_same.start)
    for n in range(16):
        ggs[n] = as_row(ggcol[n, :, 0:1])
        start_tiles(gg_home, n + 1, c, gg_same)
    eo_keep = pltpu.make_async_copy(eo_out, eo_hbm, lo.at[1])
    eo_keep.start()
    for j in range(4):
        part = slice(256 * j, 256 * j + 256)
        x_turned = xl_rows[:, :, part].reshape(1280, 256)
        for n, grads in ((0, gb), (1, ub)):
            ex_out[n, part] = lax.dot_general(
                x_turned, grads[...].reshape(1280, 512), TN, preferred_element_type=F32
            ).astype(BF16)
        half = slice(512 * (j // 2), 512 * (j // 2) + 512)
        place_at = 512 * (j % 2) + 256 * (j // 2)
        turned = hid[:, :, 256 * (j % 2) : 256 * (j % 2) + 256].reshape(1280, 256)
        ex_out[2, place_at : place_at + 256] = lax.dot_general(
            turned, og[:, :, half].reshape(1280, 512), TN, preferred_element_type=F32
        ).astype(BF16)

    ex_keep = pltpu.make_async_copy(ex_out, ex_hbm, lo.at[2])
    ex_keep.start()
    settle_rows(r4.at[0], ggl, c)
    pl.when(c == 0)(gg_same.wait)
    for k in range(16):
        column = jnp.concatenate([ggl[k], jnp.zeros((120, 128), F32)]).T[0:80, 0:1]
        ggt[pl.ds(k, 1)] = jnp.sum(pick[k].astype(F32) * column, axis=0, keepdims=True)
    settle_rows(r3.at[0], rl, c)
    pl.when(c == 0)(home_same.wait)
    mgs[...] = lax.dot_general(
        pick[...].reshape(1280, 256), rl[...].reshape(1280, 1024), TN, preferred_element_type=F32
    )
    away = rows((1 - c) * 128, 128)
    own = rows(c * 128, 128)
    back_near = [
        to(ggt.at[:, away], gg_in, sx.at[3], rx.at[3], b, sib),
        to(mgs.at[away], mg_in, sx.at[2], rx.at[2], b, sib),
    ]
    for item in back_near:
        item.start()
    settle_rows(s1.at[0], xs, c)
    settle_rows(s2.at[0], gs, c)
    settle_rows(s3.at[0], rs, c)
    settle_rows(s4.at[0], ggs, c)
    back_near[0].wait()

    gg_all[...] = jnp.zeros_like(gg_all)
    for k in range(16):
        gg_all[pl.ds(2 * k + odd, 1)] = ggt[pl.ds(k, 1), own]
        gg_all[pl.ds(2 * k + 1 - odd, 1)] = gg_in[pl.ds(k, 1)]
    gate_grad = gg_all[...].T
    own_gates = gates[...]
    logit_grad = own_gates * (
        gate_grad - jnp.sum(own_gates * gate_grad, axis=1, keepdims=True)
    )
    router_out[...] = lax.dot_general(
        logit_grad, mixed[...].astype(F32), TN, preferred_element_type=F32, precision=PRECISE
    )[0:NB]
    routed = jnp.dot(
        logit_grad, router[...], preferred_element_type=F32, precision=PRECISE
    )
    back_near[1].wait()
    mixed_grad = mgs[own] + mg_in[...] + routed
    middle = middle_ref[...]
    scale = row_scale(middle)
    unit = middle * scale
    small_out[...] = jnp.sum(mixed_grad * unit, axis=0, keepdims=True)
    inner = mixed_grad * ffn_gain[...]
    grad = cot[...].astype(F32) + scale * (
        inner - unit * jnp.mean(inner * unit, axis=1, keepdims=True)
    )
    grad_out[...] = grad
    low_out[...] = grad.astype(BF16)
    for item in (wts_keep, eo_keep, ex_keep):
        item.wait()


def backward_kernel(
    lengths, attn_grad, context, wo, head_gain, attn_gain, ffn_part, router_part, eo, ex,
    q_hbm, kv_hbm, wide_hbm, inv_hbm, wv_hbm, raw_hbm, normed_hbm, li_hbm, turn_hbm, wts_hbm, mid_hbm, grad_hbm,
    out, in_grad, wq_grad, wk_grad, wv_grad, wo_grad, attn_small, q_small, k_small, ffn_small, router_grad,
    exg_out, exu_out, exd_out,
    q_ref, kv_ref, wide_ref, inv_ref, wv, raw, normed, li2, turn, wts, middle, grad,
    cg, cgs, qp, gp, gi, qt, gt, gti, dt, di, dqs, dkvt, stage, dq_acc,
    wo_other, wo_in, wo_sum, ex_in, ex_sum, ex_cross, dq, dkv, home, wo_parts,
    low, w_other, w_in, w_sum, w_land, back, back_low, back_in, mix, mix_in, small, four, many,
    r_land, r_four, r_tot, router_out,
    s1, r1, s2, r2, s3, r3, s4, r4, s5, r5, s6, r6, s7, r7, s8, r8, s9, r9, sa, ra, sx, rx, ls, li, se, re, le,
):
    b, xl, c, y, m = place()
    h = 2 * xl + c
    sib = 2 * xl + 1 - c
    over = 2 * (1 - xl) + c
    e0, e1, total = lengths[0], lengths[0] + lengths[1], 512 * NB
    brought = [
        pltpu.make_async_copy(src, dst, li.at[n])
        for n, (src, dst) in enumerate(
            (
                (q_hbm, q_ref),
                (kv_hbm, kv_ref),
                (wide_hbm, wide_ref),
                (inv_hbm, inv_ref),
                (wv_hbm, wv),
                (raw_hbm, raw),
                (normed_hbm, normed),
                (li_hbm, li2),
                (turn_hbm, turn),
                (wts_hbm, wts),
                (mid_hbm, middle),
                (grad_hbm, grad),
            )
        )
    ]
    for item in brought:
        item.start()
    bar = pltpu.get_barrier_semaphore()
    for dj in range(GROUP):
        j = member(m, lax.rem(y + dj, GROUP))
        signal(bar, j, 2 * (1 - xl) + 1 - c)
        signal(bar, j, 2 * xl + 1 - c)
    times(1, NB, lambda d: signal(bar, lax.rem(b + d, NB), h))
    times(0, NB, lambda d: signal(bar, lax.rem(b + d, NB), over))
    pl.semaphore_wait(bar, 2 * NB - 1 + 2 * GROUP)

    ex_swap = to(ex.at[:, rows((1 - c) * 512, 512)], ex_in, sx.at[1], rx.at[1], b, sib)
    ex_swap.start()
    ex_own = pltpu.make_async_copy(ex.at[:, rows(c * 512, 512)], ex_sum, ls.at[1])
    ex_own.start()
    turned_back = jnp.zeros((128, 1024), F32)
    for i in range(2):
        for x2, part in ((xl, wo[0, i]), (1 - xl, wo[1, i])):
            turned_back = turned_back + lax.dot_general(
                attn_grad[:, rows(512 * x2 + 256 * i, 256)], part, NT, preferred_element_type=F32
            )
    cg[...] = turned_back.astype(BF16)
    turns = [(dj, dx, dc) for dj in range(GROUP) for dx in range(2) for dc in range(2)]
    cg_pieces = []
    for k, (dj, dx, dc) in enumerate(turns):
        j = lax.rem(y + dj, GROUP)
        x2 = lax.rem(xl + dx, 2)
        cols = pl.ds(pl.multiple_of((4 * x2 + j) * 128, 128), 128)
        src, dst = cg.at[:, cols], cgs.at[y, rows(c * 256 + xl * 128, 128)]
        if k == 0:
            cg_pieces.append(pltpu.make_async_copy(src, dst, ls.at[0]))
        else:
            head = 2 * x2 + lax.rem(c + dc, 2)
            cg_pieces.append(to(src, dst, s1.at[0], r1.at[0], member(m, j), head))
    for item in cg_pieces:
        item.start()

    def tile(n):
        return router_part.at[rows(8 * (n // 8), 8), rows(128 * lax.rem(n, 8), 128)]

    def router_first(d):
        to_b = lax.rem(b + d, NB)
        return to(tile(to_b), r_land.at[b], s8.at[0], r8.at[0], to_b, h)

    times(1, NB, lambda d: router_first(d).start())
    r_land[b] = router_part[rows(8 * (b // 8), 8), rows(128 * lax.rem(b, 8), 128)]

    eo_piece = rows_home(eo, home, b, xl, c, lambda r: s2.at[0], lambda r: r2.at[0])
    eo_same = pltpu.make_async_copy(eo.at[15], home.at[b // 2], ls.at[2])
    pl.when(c == 0)(eo_same.start)
    send_pieces(eo_piece, 0, 32, c)

    def out_part(x2, core):
        cols = pl.ds(pl.multiple_of(512 * x2 + 256 * core, 256), 256)
        return lax.dot_general(
            context[...], attn_grad[:, cols], TN, preferred_element_type=F32
        )

    for x2 in range(2):
        wo_other[x2] = out_part(x2, 1 - c).astype(BF16)
    wo_swap = to(wo_other, wo_in, sx.at[0], rx.at[0], b, sib)
    wo_swap.start()
    brought[0].wait()
    for i in range(GROUP):
        both = q_ref[i].astype(F32)
        pad_queries(both, qp, i)
        turned = both.T
        qt[i] = jnp.concatenate([turned[0:64], turned[64:128]], axis=1).astype(BF16)
    dq_acc[...] = jnp.zeros_like(dq_acc)
    wo_swap.wait()
    for x2 in range(2):
        wo_sum[x2] = (out_part(x2, c) + wo_in[x2].astype(F32)).astype(BF16)
    ex_swap.wait()
    ex_own.wait()
    ex_sum[...] = (ex_sum[...].astype(F32) + ex_in[...].astype(F32)).astype(BF16)

    def cross_piece(n, j):
        part = rows(32 * j, 32)
        return to(ex_sum.at[n, part], ex_cross.at[n, part], sx.at[2], rx.at[2], b, over)


    def wo_piece(e):
        d, x2 = lax.rem(e, NB), lax.rem(xl + e // NB, 2)
        peer_b = lax.rem(b + d, NB)
        part = wo_sum.at[x2, rows(peer_b * 32, 32)]
        return to(part, wo_parts.at[NB * (e // NB) + b], s3.at[0], r3.at[0], peer_b, 2 * x2 + c)

    for n in range(3):
        times(0, 8, lambda j, n=n: cross_piece(n, j).start())
    cg_pieces[0].wait()
    settle(r1.at[0], home.at[pl.ds(0, 3)])
    wo_parts[b] = wo_sum[xl, rows(b * 32, 32)]
    for item in brought[1:4]:
        item.wait()
    left = lax.broadcasted_iota(jnp.int32, (512, 128), 1) < 64
    for i in range(GROUP):
        scaled = cgs[i].astype(F32) * inv_ref[i]
        pos = query_positions((512, 1), 0, member(m, i))
        mid_doc = (pos >= e0) & (pos < e1)
        terms = scaled * wide_ref[i]
        one = jnp.sum(jnp.where(left, terms, 0.0), axis=1, keepdims=True)
        two = jnp.sum(jnp.where(left, 0.0, terms), axis=1, keepdims=True)
        upper = jnp.where(left, 0.0, pltpu.roll(scaled, 64, 1))
        lower = jnp.where(left, 0.0, scaled)
        for part, val, term in ((0, upper, one), (512, lower, two)):
            span = pl.ds(part, 512)
            gp[i, span] = val.astype(BF16)
            gi[i, span] = jnp.where(mid_doc, val, 0.0).astype(BF16)
            dt[i, span] = jnp.broadcast_to(term, (512, 128))
            di[i, span] = jnp.broadcast_to(jnp.where(mid_doc, term, 0.0), (512, 128))
            lanes = pl.ds(part, 512)
            gt[i, :, lanes] = val.T[64:128].astype(BF16)
            gti[i, :, lanes] = jnp.where(mid_doc, val, 0.0).T[64:128].astype(BF16)

    def dkv_piece(kb):
        return to(stage.at[kb], dkv.at[b], s4.at[0], r4.at[0], kb, h)

    def pair(dp):
        p = lax.rem(b // 2 + 1 + dp, 16)
        send_pieces(eo_piece, jnp.minimum(32 + 5 * dp, 80), jnp.minimum(37 + 5 * dp, 80), c)
        for n in range(3):
            pl.when(dp < 8)(lambda n=n: cross_piece(n, dp + 8).start())
        dkvt[...] = jnp.zeros_like(dkvt)
        keys = kv_ref[pl.ds(2 * p, 2)].reshape(512, 128)

        def step(i, expo, g, gturn, dots):
            prob = lax.dot_general(g[i], keys, NT, preferred_element_type=F32)
            term = jnp.concatenate([dots[i]] * 4, axis=1)
            score_grad = (expo * (prob - term)).astype(BF16)
            dq_acc[i] += jnp.dot(score_grad, keys, preferred_element_type=F32)
            dkvt[0:64] += jnp.dot(qt[i], score_grad, preferred_element_type=F32)
            dkvt[64:128] += jnp.dot(gturn[i], expo.astype(BF16), preferred_element_type=F32)

        def scores(i):
            return jnp.exp(lax.dot_general(qp[i], keys, NT, preferred_element_type=F32))

        def inside(i):
            step(i, scores(i), gi, gti, di)

        def edge(i, qb):
            low, high = limits(query_positions((1024, 1), 0, qb), e0, e1, total)
            kpos = key_positions((1, 512), 1, 2 * p, c)
            expo = jnp.where((kpos >= low) & (kpos < high), scores(i), 0.0)
            step(i, expo, gp, gt, dt)

        on_pair(p, m, inside, edge)
        flat = dkvt[...].T.astype(BF16)
        for n in range(2):
            kb = 2 * p + n
            stage[kb] = flat[256 * n : 256 * n + 256]

            @pl.when(kb != b)
            def _():
                dkv_piece(kb).start()

    times(0, 6, pair)
    settle(r8.at[0], r_land.at[pl.ds(0, NB - 1)])
    part = r_land[0]
    for n in range(1, NB):
        part = part + r_land[n]
    r_four[h] = part
    router_near = [
        to(r_four.at[h], r_four.at[h], s9.at[d], r9.at[d], b, lax.rem(h + d, 4))
        for d in range(1, 4)
    ]
    for item in router_near:
        item.start()
    times(6, 16, pair)
    dkv[b] = stage[b]
    for i in range(GROUP):
        both = jnp.where(left, dq_acc[i, 0:512], pltpu.roll(dq_acc[i, 512:1024], 64, 1))
        dqs[i] = (both * SCALE).astype(BF16)

    def dq_piece(dj, dc):
        j = lax.rem(y + dj, GROUP)
        c2 = lax.rem(c + dc, 2)
        cols = pl.ds(pl.multiple_of(y * 128, 128), 128)
        src, dst = dqs.at[j, rows(c2 * 256, 256)], dq.at[c, :, cols]
        k = 2 * dj + dc
        if k == 0:
            return pltpu.make_async_copy(src, dst, ls.at[4])
        return to(src, dst, s5.at[k], r5.at[k], member(m, j), 2 * xl + c2)

    dq_pieces = [dq_piece(dj, dc) for dj in range(GROUP) for dc in range(2)]
    for item in dq_pieces:
        item.start()
    times(1, 2 * NB, lambda e: wo_piece(e).start())
    for item in router_near:
        item.wait()
    r_tot[...] = r_four[0] + r_four[1] + r_four[2] + r_four[3]
    home_tile = (rows(8 * (b // 8), 8), rows(128 * lax.rem(b, 8), 128))
    router_out[home_tile] = r_tot[...]

    def router_last(d):
        return to(r_tot, router_out.at[home_tile], sa.at[0], ra.at[0], lax.rem(b + d, NB), h)

    times(1, NB, lambda d: router_last(d).start())
    settle(sx.at[2], ex_cross)
    settle(rx.at[2], ex_cross)
    ex_in[...] = (ex_sum[...].astype(F32) + ex_cross[...].astype(F32)).astype(BF16)
    half, quarter = rows(c * 512, 512), rows(c * 256, 256)
    ex_moves = []
    for n, (src, dst) in enumerate(
        (
            (ex_in.at[0], exg_out.at[half]),
            (ex_in.at[1], exu_out.at[half]),
            (ex_in.at[2, pl.ds(0, 256)], exd_out.at[quarter, pl.ds(0, 512)]),
            (ex_in.at[2, pl.ds(256, 256)], exd_out.at[quarter, pl.ds(512, 512)]),
        )
    ):
        ex_moves.append(pltpu.make_async_copy(src, dst, le.at[n]))
        ex_moves.append(to(src, dst, se.at[n], re.at[n], b, sib))
    for item in ex_moves:
        item.start()
    for item in dq_pieces:
        item.wait()
    settle(r4.at[0], dkv.at[pl.ds(0, NB - 1)])

    for item in brought[4:]:
        item.wait()
    left, first = lanes_of((256, 128))
    q_gain = jnp.zeros((1, 128), F32)
    k_gain = jnp.zeros((1, 128), F32)

    def unprep(d, u, gain, row):
        turned = d * turn[0] - swapped(d, first) * turn[1]
        scale = lax.rsqrt(by_head(u * u, left) + EPSILON)
        unit = u * scale
        inner = turned * row
        gain = gain + jnp.sum(turned * unit, axis=0, keepdims=True)
        return scale * (inner - unit * by_head(inner * unit, left)), gain

    for j in range(GROUP):
        i, q_cols, kv_cols = slab(j)
        span = slice(128 * j, 128 * j + 128)
        d = (dq[0, :, span].astype(F32) + dq[1, :, span].astype(F32)).astype(BF16).astype(F32)
        got, q_gain = unprep(d, raw[i, :, q_cols], q_gain, head_gain[0:1])
        low[i, :, q_cols] = got.astype(BF16)
        d = dkv[8 * j].astype(F32)
        for n in range(1, 8):
            d = d + dkv[8 * j + n].astype(F32)
        d = d.astype(BF16).astype(F32)
        got, k_gain = unprep(d, raw[i, :, kv_cols], k_gain, head_gain[1:2])
        low[i, :, kv_cols] = jnp.where(left, got, d).astype(BF16)
    normed_grad = lax.dot_general(low[0], wv[0], NT, preferred_element_type=F32) + lax.dot_general(
        low[1], wv[1], NT, preferred_element_type=F32
    )
    source2 = li2[...].reshape(256, 1024).astype(F32)
    scale = row_scale(source2)
    unit = source2 * scale
    inner = normed_grad * attn_gain[...]
    attn_part = jnp.sum(normed_grad * unit, axis=0, keepdims=True)
    small[...] = jnp.zeros_like(small)
    for n in range(8):
        lanes = slice(128 * n, 128 * n + 128)
        small[n : n + 1] = attn_part[:, lanes]
        small[8 + n : 9 + n] = ffn_part[:, lanes]
    small[16:17] = q_gain
    small[17:18] = k_gain
    near = [
        to(small, four.at[h], sx.at[6 + d], rx.at[6 + d], b, lax.rem(h + d, 4)) for d in range(1, 4)
    ]
    for item in near:
        item.start()
    four[h] = small[...]
    w_other[...] = lax.dot_general(
        normed[...], low[1 - c], TN, preferred_element_type=F32
    ).astype(BF16).reshape(NB, 32, 512)
    w_swap = to(w_other, w_in, sx.at[4], rx.at[4], b, sib)
    w_swap.start()
    back[...] = (scale * (inner - unit * jnp.mean(inner * unit, axis=1, keepdims=True))).reshape(
        2, 128, 1024
    )
    back_low[...] = back[1 - xl].astype(BF16)
    back_swap = to(back_low, back_in, sx.at[5], rx.at[5], b, over)
    back_swap.start()
    mine = lax.dot_general(normed[...], low[c], TN, preferred_element_type=F32)
    for item in near:
        item.wait()
    many[b] = four[0] + four[1] + four[2] + four[3]

    def spread(d):
        return to(many.at[b], many.at[b], s7.at[0], r7.at[0], lax.rem(b + d, NB), h)

    times(1, NB, lambda d: spread(d).start())
    w_swap.wait()
    w_sum[...] = (mine.reshape(NB, 32, 512) + w_in[...].astype(F32)).astype(BF16)

    def w_piece(d):
        peer = lax.rem(b + d, NB)
        return to(w_sum.at[peer], w_land.at[b], s6.at[0], r6.at[0], peer, h)

    times(1, NB, lambda d: w_piece(d).start())
    w_land[b] = w_sum[b]

    settle_rows(r2.at[0], home, c)
    pl.when(c == 0)(eo_same.wait)
    flat = home[...].reshape(1280, 1024)
    mix[...] = (
        lax.dot_general(wts[0].reshape(1280, 256), flat, TN, preferred_element_type=F32)
        + lax.dot_general(wts[1].reshape(1280, 256), flat, TN, preferred_element_type=F32)
    ).reshape(2, 128, 1024)
    mix_swap = to(mix.at[1 - c], mix_in, sx.at[6], rx.at[6], b, sib)
    mix_swap.start()
    back_swap.wait()
    in_grad[...] = (grad[...] + back[xl] + back_in[...].astype(F32)).astype(BF16)
    mix_swap.wait()
    out[...] = (middle[...] + mix[c] + mix_in[...]).astype(BF16)
    settle(r7.at[0], many.at[pl.ds(0, NB - 1)])
    total = many[0]
    for n in range(1, NB):
        total = total + many[n]
    for n in range(8):
        lanes = slice(128 * n, 128 * n + 128)
        attn_small[:, lanes] = total[n : n + 1]
        ffn_small[:, lanes] = total[8 + n : 9 + n]
    q_small[...] = total[16:17, 0:64] + total[16:17, 64:128]
    k_small[...] = total[17:18, 0:64]
    settle(r6.at[0], w_land.at[pl.ds(0, NB - 1)])
    shard = w_land[0].astype(F32)
    for n in range(1, NB):
        shard = shard + w_land[n].astype(F32)
    wq_grad[...] = shard[:, 0:256]
    wk_grad[...] = jnp.concatenate([shard[:, 256:320], shard[:, 384:448]], axis=1)
    wv_grad[...] = jnp.concatenate([shard[:, 320:384], shard[:, 448:512]], axis=1)
    settle(r3.at[0], wo_parts.at[pl.ds(0, 2 * NB - 1)])
    total = wo_parts[0].astype(F32)
    for n in range(1, 2 * NB):
        total = total + wo_parts[n].astype(F32)
    wo_grad[...] = total
    for item in ex_moves:
        item.wait()
    settle(ra.at[0], r_land.at[pl.ds(0, NB - 1)])
    router_grad[...] = router_out[...].T
    settle(s1.at[0], home.at[pl.ds(0, 3)])
    settle_rows(s2.at[0], home, c)
    settle(s3.at[0], wo_parts.at[pl.ds(0, 2 * NB - 1)])
    settle(s4.at[0], dkv.at[pl.ds(0, NB - 1)])
    settle(s6.at[0], w_land.at[pl.ds(0, NB - 1)])
    settle(s7.at[0], many.at[pl.ds(0, NB - 1)])
    settle(s8.at[0], r_land.at[pl.ds(0, NB - 1)])
    settle(sa.at[0], r_land.at[pl.ds(0, NB - 1)])


VM = pl.BlockSpec(memory_space=pltpu.VMEM)
SM = pl.BlockSpec(memory_space=pltpu.SMEM)
ANY = pl.BlockSpec(memory_space=pl.ANY)


def call(kernel, collective_id, ins, outs, scratch, sems, flops, *operands):
    return pl.pallas_call(
        kernel,
        out_shape=[jax.ShapeDtypeStruct(shape, dtype) for shape, dtype, _ in outs],
        in_specs=ins,
        out_specs=[spec for _, _, spec in outs],
        scratch_shapes=[pltpu.VMEM(shape, dtype) for shape, dtype in scratch]
        + [pltpu.SemaphoreType.DMA(n) for n in sems],
        compiler_params=pltpu.CompilerParams(
            collective_id=collective_id,
            has_side_effects=True,
            vmem_limit_bytes=60 * 1024 * 1024,
        ),
        cost_estimate=pl.CostEstimate(
            flops=flops, bytes_accessed=8_000_000, transcendentals=flops // 2000
        ),
    )(*operands)


def limits(pos, e0, e1, total):
    low = jnp.where(pos < e0, 0, jnp.where(pos < e1, e0, e1))
    end = jnp.where(pos < e0, e0, jnp.where(pos < e1, e1, total))
    reach = low + ((pos - low) // BLOCK + 1) * BLOCK
    return low, jnp.minimum(end, reach)


def query_positions(shape, axis, qb):
    r = lax.broadcasted_iota(jnp.int32, shape, axis)
    r = lax.rem(r, 512)
    return 512 * qb + 256 * lax.rem(r // 128, 2) + 128 * (r // 256) + lax.rem(r, 128)


def key_positions(shape, axis, kb, core):
    r = lax.broadcasted_iota(jnp.int32, shape, axis)
    return 512 * (kb + r // 256) + 256 * lax.rem(r // 128, 2) + 128 * core + lax.rem(r, 128)


def body(
    layer_input,
    attn_gain,
    w_query,
    key_weight,
    value_weight,
    w_output,
    query_gain,
    key_gain,
    ffn_gain,
    router,
    w_gate,
    w_up,
    w_down,
    routes,
    doc_lengths,
    cotangent,
):
    tokens, width = layer_input.shape
    lane = np.arange(128) % (HEAD_SIZE // 2)
    pace = jnp.asarray(ROPE_BASE ** (-2.0 * lane / HEAD_SIZE), F32)[None]
    (
        w_full, wo_full, both_inputs, q_group, kv_all, up_rows, raw, normed, ctx_wide, ctx_inv, turn, router_wide,
        pick, context, middle, mixed_in, gates, head_gain,
    ) = call(
        forward_kernel,
        0,
        [SM] + [VM] * 13,
        [
            ((2, width, 512), BF16, ANY),
            ((2, 2, width, width // 4), BF16, ANY),
            ((2, tokens, width), BF16, ANY),
            ((GROUP, 512, 128), BF16, ANY),
            ((NB, 256, 128), BF16, ANY),
            ((16, SLOTS, width), BF16, ANY),
            ((2, 2 * tokens, 512), F32, ANY),
            ((2 * tokens, width), BF16, ANY),
            ((GROUP, 512, 128), F32, ANY),
            ((GROUP, 512, 128), F32, ANY),
            ((2, 2 * tokens, 128), F32, ANY),
            ((128, width), F32, ANY),
            ((16, SLOTS, 2 * tokens), BF16, VM),
            ((tokens, width), BF16, VM),
            ((tokens, width), F32, VM),
            ((tokens, width), BF16, VM),
            ((tokens, 128), F32, VM),
            ((2, 128), F32, VM),
        ],
        [
            ((2, 2 * tokens, 512), F32),
            ((2 * tokens, width), BF16),
            ((GROUP, 512, 128), F32),
            ((GROUP, 512, 128), F32),
            ((2, 2 * tokens, 128), F32),
            ((128, width), F32),
            ((32, 512), BF16),
            ((2, width, 512), BF16),
            ((2, 2, width, width // 4), BF16),
            ((2, tokens, width), BF16),
            ((2 * tokens, width), BF16),
            ((2, 8, 128), jnp.int32),
            ((16, SLOTS, width), BF16),
            ((2 * tokens, 512), BF16),
            ((2 * tokens, 512), BF16),
            ((GROUP, 512, 128), BF16),
            ((NB, 256, 128), BF16),
            ((GROUP, 1024, 128), BF16),
            ((80, 512), BF16),
            ((GROUP, 80, 1024), F32),
            ((GROUP, 80, 1024), F32),
            ((GROUP, 80, 1024), F32),
            ((GROUP, 512, 128), BF16),
            ((tokens, width), BF16),
        ],
        [(1,)] * 4 + [(8,)] * 4 + [(1,), (NB,)] + [(1,)] * 2 + [(8,)] * 2 + [(9,), (12,)],
        18_000_000_000,
        doc_lengths,
        w_query,
        key_weight,
        value_weight,
        w_output,
        layer_input,
        cotangent,
        routes.T,
        attn_gain[None],
        query_gain[None],
        key_gain[None],
        pace,
        ffn_gain[None],
        router.T,
    )
    wts, expert_out, ex_grads, middle_grad, attn_grad, ffn_part, router_part = call(
        experts_kernel,
        1,
        [VM] * 3 + [ANY] * 6 + [VM, ANY],
        [
            ((2, 16, SLOTS, 2 * tokens), BF16, ANY),
            ((16, SLOTS, width), BF16, ANY),
            ((3, 1024, 512), BF16, ANY),
            ((tokens, width), F32, VM),
            ((tokens, width), BF16, VM),
            ((1, width), F32, VM),
            ((NB, width), F32, VM),
        ],
        [
            ((16, SLOTS, width), BF16),
            ((1, width, 512), BF16),
            ((1, width, 512), BF16),
            ((1, 512, width), BF16),
            ((tokens, width), F32),
            ((tokens, width), BF16),
            ((128, width), F32),
            ((2, 16, SLOTS, 2 * tokens), BF16),
            ((16, SLOTS, width), BF16),
            ((3, 1024, 512), BF16),
            ((2 * tokens, width), BF16),
            ((2 * tokens, 128), F32),
            ((16, SLOTS, width), BF16),
            ((16, SLOTS, width), BF16),
            ((16, 8, 128), F32),
            ((16, 8, 128), F32),
            ((16, SLOTS, width), BF16),
            ((16, SLOTS, width), BF16),
            ((16, 8, 128), F32),
            ((16, 8, 128), F32),
            ((16, SLOTS, 512), BF16),
            ((16, SLOTS, 512), BF16),
            ((16, SLOTS, 512), BF16),
            ((16, SLOTS, width), BF16),
            ((2 * tokens, width), F32),
            ((16, 2 * tokens), F32),
            ((tokens, width), F32),
            ((16, tokens), F32),
            ((128, tokens), F32),
            ((16, SLOTS, 128), F32),
            ((16, SLOTS, 128), F32),
        ],
        [(1,), (ROUNDS,)] + [(1,)] * 6 + [(4,)] * 2 + [(4,), (7,), (3,)],
        12_000_000_000,
        mixed_in,
        gates,
        pick,
        up_rows,
        w_gate,
        w_up,
        w_down,
        middle,
        cotangent,
        ffn_gain[None],
        router_wide,
    )
    results = call(
        backward_kernel,
        2,
        [SM] + [VM] * 7 + [ANY] * 14,
        [
            ((tokens, width), BF16, VM),
            ((tokens, width), BF16, VM),
            ((32, 256), F32, VM),
            ((32, 128), F32, VM),
            ((32, 128), F32, VM),
            ((32, 256), F32, VM),
            ((1, width), F32, VM),
            ((1, HEAD_SIZE), F32, VM),
            ((1, HEAD_SIZE), F32, VM),
            ((1, width), F32, VM),
            ((width, NB), F32, VM),
            ((width, 512), BF16, ANY),
            ((width, 512), BF16, ANY),
            ((512, width), BF16, ANY),
        ],
        [
            ((GROUP, 512, 128), BF16),
            ((NB, 256, 128), BF16),
            ((GROUP, 512, 128), F32),
            ((GROUP, 512, 128), F32),
            ((2, width, 512), BF16),
            ((2, 2 * tokens, 512), F32),
            ((2 * tokens, width), BF16),
            ((2, tokens, width), BF16),
            ((2, 2 * tokens, 128), F32),
            ((2, 16, SLOTS, 2 * tokens), BF16),
            ((tokens, width), F32),
            ((tokens, width), F32),
            ((tokens, width), BF16),
            ((GROUP, 512, 128), BF16),
            ((GROUP, 1024, 128), BF16),
            ((GROUP, 1024, 128), BF16),
            ((GROUP, 1024, 128), BF16),
            ((GROUP, 64, 1024), BF16),
            ((GROUP, 64, 1024), BF16),
            ((GROUP, 64, 1024), BF16),
            ((GROUP, 1024, 128), F32),
            ((GROUP, 1024, 128), F32),
            ((GROUP, 512, 128), BF16),
            ((128, 512), F32),
            ((NB, 256, 128), BF16),
            ((GROUP, 1024, 128), F32),
            ((2, 1024, 256), BF16),
            ((2, 1024, 256), BF16),
            ((2, 1024, 256), BF16),
            ((3, 512, 512), BF16),
            ((3, 512, 512), BF16),
            ((3, 512, 512), BF16),
            ((2, 2 * tokens, 512), BF16),
            ((NB, 256, 128), BF16),
            ((16, SLOTS, width), BF16),
            ((2 * NB, 32, 256), BF16),
            ((2, 2 * tokens, 512), BF16),
            ((NB, 32, 512), BF16),
            ((NB, 32, 512), BF16),
            ((NB, 32, 512), BF16),
            ((NB, 32, 512), BF16),
            ((2, tokens, width), F32),
            ((tokens, width), BF16),
            ((tokens, width), BF16),
            ((2, tokens, width), F32),
            ((tokens, width), F32),
            ((24, 128), F32),
            ((4, 24, 128), F32),
            ((NB, 24, 128), F32),
            ((NB, 8, 128), F32),
            ((4, 8, 128), F32),
            ((8, 128), F32),
            ((NB, width), F32),
        ],
        [(1,)] * 8 + [(8,)] * 2 + [(1,)] * 6 + [(4,)] * 2 + [(1,)] * 2 + [(10,)] * 2 + [(6,), (12,)] + [(4,)] * 3,
        45_000_000_000,
        doc_lengths,
        attn_grad,
        context,
        wo_full,
        head_gain,
        attn_gain[None],
        ffn_part,
        router_part,
        expert_out,
        ex_grads,
        q_group,
        kv_all,
        ctx_wide,
        ctx_inv,
        w_full,
        raw,
        normed,
        both_inputs,
        turn,
        wts,
        middle,
        middle_grad,
    )
    return (
        *results[:2],
        results[6][0],
        *results[2:6],
        *[row[0] for row in results[7:10]],
        results[10],
        *[grad.astype(F32)[None] for grad in results[11:]],
    )


def solution(mesh):
    everyone = P(("blk", "head"), None)
    both = P("blk", "head")
    expert = P("blk", None, None)
    return jax.shard_map(
        body,
        mesh=mesh,
        in_specs=(everyone, P(), both, both, both, both, P(), P(), P(), P())
        + (expert, expert, expert, everyone, P(), everyone),
        out_specs=(everyone, everyone, P(), both, both, both, both, P(), P(), P(), P())
        + (expert, expert, expert),
        check_vma=False,
    )
```

```python
import jax
import jax.numpy as jnp
import numpy as np
from jax import lax
from jax.experimental import pallas as pl
from jax.experimental.pallas import tpu as pltpu
from jax.sharding import PartitionSpec as P

HEAD_SIZE = 64
TOPK = 8
BLOCK = 256
EPSILON = 1e-06
ROPE_BASE = 10000.0
PRECISE = lax.Precision.HIGHEST
SCALE = HEAD_SIZE ** (-0.5)

NB = 32
ROUNDS = 5
SLOTS = 80
GROUP = 4
MESH_ID = pl.DeviceIdType.MESH
F32 = jnp.float32
BF16 = jnp.bfloat16
NT = (((1,), (1,)), ((), ()))
NN = (((1,), (0,)), ((), ()))
TN = (((0,), (0,)), ((), ()))


def place():
    b = lax.axis_index("blk")
    h = lax.axis_index("head")
    y = b // 8
    r = lax.rem(b, 8)
    m = jnp.where(lax.rem(y, 2) == 0, r, 7 - r)
    return b, h // 2, lax.rem(h, 2), y, m


def member(m, j):
    return 8 * j + m + lax.rem(j, 2) * (7 - 2 * m)


def times(start, n, body):
    def step(i, carry):
        body(i)
        return carry

    lax.fori_loop(start, n, step, 0)


def signal(sem, blk, head):
    pl.semaphore_signal(sem, inc=1, device_id=(blk, head), device_id_type=MESH_ID)


def rows(start, size):
    return pl.ds(pl.multiple_of(start, size), size)


def to(src, dst, send, recv, blk, head):
    return pltpu.make_async_remote_copy(
        src, dst, send, recv, device_id=(blk, head), device_id_type=MESH_ID
    )


def settle(sem, part):
    pltpu.make_async_copy(part, part, sem).wait()


def settle_rows(sem, blocks, c):
    pl.when(c == 0)(lambda: settle(sem, blocks.at[pl.ds(0, 15)]))
    pl.when(c == 1)(lambda: settle(sem, blocks))


def greet_all(bar, b, xl, c, y, m):
    h = 2 * xl + c
    times(1, NB, lambda d: signal(bar, lax.rem(b + d, NB), h))
    times(0, NB, lambda d: signal(bar, lax.rem(b + d, NB), 2 * (1 - xl) + c))
    for dj in range(GROUP):
        j = member(m, lax.rem(y + dj, GROUP))
        signal(bar, j, 2 * xl + 1 - c)
    pl.semaphore_wait(bar, 2 * NB - 1 + GROUP)


def pad_queries(both, qp, i):
    left = lax.broadcasted_iota(jnp.int32, (512, 128), 1) < 64
    qp[i, 0:512] = jnp.where(left, both, 0.0).astype(BF16)
    qp[i, 512:1024] = jnp.where(left, pltpu.roll(both, 64, 1), 0.0).astype(BF16)


def on_pair(p, m, inside, edge):
    def each(i):
        qb = member(m, i)
        whole = (p >= 1) & (2 * p + 1 <= qb - 1)
        pl.when(whole)(lambda: inside(i))
        pl.when(jnp.logical_not(whole) & (2 * p <= qb + 1))(lambda: edge(i, qb))

    times(0, GROUP, each)


def by_head(values, left):
    one = jnp.sum(jnp.where(left, values, 0.0), axis=1, keepdims=True) / HEAD_SIZE
    two = jnp.sum(jnp.where(left, 0.0, values), axis=1, keepdims=True) / HEAD_SIZE
    return jnp.where(left, one, two)


def swapped(values, first):
    return jnp.where(first, pltpu.roll(values, 96, 1), pltpu.roll(values, 32, 1))


def row_scale(values):
    return lax.rsqrt(jnp.mean(values * values, axis=1, keepdims=True) + EPSILON)


def lanes_of(shape):
    lane = lax.broadcasted_iota(jnp.int32, shape, 1)
    return lane < 64, lax.rem(lane, 64) < 32


def slab(j):
    return j // 2, slice(128 * (j % 2), 128 * (j % 2) + 128), slice(
        256 + 128 * (j % 2), 384 + 128 * (j % 2)
    )


def forward_kernel(
    lengths, wq, wk, wvl, wo, li, cot, routes_t, attn_gain, q_gain, k_gain, pace, ffn_gain, router_t,
    w_out, wo_out, li_out, q_out, kv_out, c_out, raw_out, normed_out, wide_out, inv_out, turn_out, router_out,
    pick, ctx_out, mid_out, tok_out, gates_out, head_gain,
    tok, gt, raw, normed, wide_all, inv_all, turn, router,
    ws, wv, wov, li2, cot2, rt, xs, qs, kvst, qg, kvs, qp, vt, acc, accm, peer, ctx, ctx_in,
    sw, rw, so, ro, sx, rx, s1, r1, s2, r2, s5, r5, s7, r7, ls, lk,
):
    b, xl, c, y, m = place()
    h = 2 * xl + c
    sib = 2 * xl + 1 - c
    over = 2 * (1 - xl) + c
    odd = lax.rem(b + c, 2)
    e0, e1, total = lengths[0], lengths[0] + lengths[1], 512 * NB
    pairs = jnp.concatenate([wk[...].astype(F32), wvl[...].astype(F32)], axis=1)
    even = jnp.concatenate([pairs[:, 0:64], pairs[:, 128:192]], axis=1)
    other = jnp.concatenate([pairs[:, 64:128], pairs[:, 192:256]], axis=1)
    ws[:, 0:256] = wq[...]
    ws[:, 256:384] = even.astype(BF16)
    ws[:, 384:512] = other.astype(BF16)
    greet_all(pltpu.get_barrier_semaphore(), b, xl, c, y, m)

    def w_first(d):
        part = wv.at[c, rows(b * 32, 32)]
        return to(ws, part, sw.at[0], rw.at[0], lax.rem(b + d, NB), h)

    def wo_first(d):
        part = wov.at[0, c, rows(b * 32, 32)]
        return to(wo, part, so.at[0], ro.at[0], lax.rem(b + d, NB), h)

    keeps = []

    def keep(part, out):
        item = pltpu.make_async_copy(part, out, lk.at[len(keeps)])
        item.start()
        keeps.append(item)

    near = [
        to(routes_t, rt.at[c], sx.at[0], rx.at[0], b, sib),
        to(cot, cot2.at[rows(c * 128, 128)], sx.at[1], rx.at[1], b, sib),
        to(li, li2.at[xl], sx.at[2], rx.at[2], b, over),
    ]
    for item in near:
        item.start()
    times(1, NB, lambda d: w_first(d).start())
    wv[c, rows(b * 32, 32)] = ws[...]
    li2[xl] = li[...]
    cot2[rows(c * 128, 128)] = cot[...]
    rt[c] = routes_t[...]

    near[0].wait()
    both_routes = jnp.concatenate([rt[0], rt[1]], axis=1)
    mine = 2 * lax.broadcasted_iota(jnp.int32, (16, 256), 0) + odd
    chosen = jnp.zeros((16, 256), F32)
    for k in range(TOPK):
        chosen = jnp.where(both_routes[k : k + 1] == mine, 1.0, chosen)
    earlier = lax.broadcasted_iota(jnp.int32, (256, 256), 0) < lax.broadcasted_iota(
        jnp.int32, (256, 256), 1
    )
    rank = jnp.dot(
        chosen.astype(BF16), jnp.where(earlier, 1.0, 0.0).astype(BF16), preferred_element_type=F32
    )
    slot = lax.broadcasted_iota(jnp.int32, (80, 256), 0).astype(F32)
    for k in range(16):
        at = jnp.where(rank[k : k + 1] == slot, chosen[k : k + 1], 0.0)
        pick[k] = at.astype(BF16)
    near[1].wait()
    c_piece = rows_out(xs, c_out, b, xl, c, lambda r: s5.at[0], lambda r: r5.at[0])
    c_same = pltpu.make_async_copy(xs.at[b // 2], c_out.at[15], ls.at[3])

    def fetch(d):
        k = stride(b, d)
        xs[k] = jnp.dot(pick[k], cot2[...], preferred_element_type=F32).astype(BF16)

    times(1, 17, fetch)
    pl.when(c == 0)(c_same.start)
    send_pieces(c_piece, 0, 32, c)

    near[2].wait()
    keep(li2, li_out)
    source2 = li2[...].reshape(256, 1024).astype(F32)
    normed[...] = (source2 * row_scale(source2) * attn_gain[...]).astype(BF16)

    keep(normed, normed_out)
    settle(rw.at[0], wv.at[c, rows(0, 992)])
    w_sib = to(wv.at[c], wv.at[c], sx.at[3], rx.at[3], b, sib)
    w_sib.start()
    wov[0, c, rows(b * 32, 32)] = wo[...]
    left, first = lanes_of((256, 128))
    t = lax.broadcasted_iota(jnp.int32, (256, 128), 0)
    pos = 512 * b + 256 * (t // 128) + 128 * c + lax.rem(t, 128)
    opening = jnp.where(pos < e0, 0, jnp.where(pos < e1, e0, e1))
    angles = (pos - opening).astype(F32) * pace[...]
    turn[0] = jnp.cos(angles)
    sine = jnp.sin(angles)
    turn[1] = jnp.where(first, -sine, sine)
    head_gain[0:1] = jnp.concatenate([q_gain[...], q_gain[...]], axis=1)
    head_gain[1:2] = jnp.concatenate([k_gain[...], jnp.ones((1, 64), F32)], axis=1)
    router[...] = jnp.zeros_like(router)
    router[0:NB] = router_t[...]
    keep(turn, turn_out)
    keep(router, router_out)
    w_sib.wait()
    keep(wv, w_out)
    for i in range(2):
        raw[i] = jnp.dot(normed[...], wv[i], preferred_element_type=F32)
    for j in range(GROUP):
        i, q_cols, kv_cols = slab(j)
        span = slice(128 * j, 128 * j + 128)
        u = raw[i, :, q_cols]
        n = u * lax.rsqrt(by_head(u * u, left) + EPSILON) * head_gain[0:1]
        turned = n * turn[0] + swapped(n, first) * turn[1]
        qs[:, span] = (turned.astype(BF16).astype(F32) * SCALE).astype(BF16)
        u = raw[i, :, kv_cols]
        n = u * lax.rsqrt(by_head(u * u, left) + EPSILON) * head_gain[1:2]
        turned = n * turn[0] + swapped(n, first) * turn[1]
        kvst[:, span] = jnp.where(left, turned, u).astype(BF16)

    def q_piece(part, dj, dc):
        j = lax.rem(y + dj, GROUP)
        cols = pl.ds(pl.multiple_of(j * 128, 128), 128)
        k = 8 * part + 2 * dj + dc
        src, dst = qs.at[rows(part * 128, 128), cols], qg.at[y, rows(c * 256 + part * 128, 128)]
        if dj + dc == 0:
            return pltpu.make_async_copy(src, dst, s1.at[k])
        return to(src, dst, s1.at[k], r1.at[k], member(m, j), 2 * xl + lax.rem(c + dc, 2))

    q_pieces = [q_piece(n, dj, dc) for n in range(2) for dj in range(GROUP) for dc in range(2)]

    def kv_piece(i):
        d, half = lax.rem(i, NB), rows(128 * (i // NB), 128)
        peer_b = lax.rem(b + d, NB)
        cols = pl.ds(pl.multiple_of((peer_b // 8) * 128, 128), 128)
        return to(kvst.at[half, cols], kvs.at[b, half], s2.at[0], r2.at[d], peer_b, h)

    for item in q_pieces:
        item.start()
    own_cols = pl.ds(pl.multiple_of(y * 128, 128), 128)
    kv_own = pltpu.make_async_copy(kvst.at[:, own_cols], kvs.at[b], ls.at[1])
    kv_own.start()
    times(1, NB, lambda d: kv_piece(d).start())
    times(NB + 1, 2 * NB, lambda i: kv_piece(i).start())
    for item in q_pieces:
        item.wait()
    kv_own.wait()
    keep(qg, q_out)
    keep(raw, raw_out)
    for i in range(GROUP):
        pad_queries(qg[i].astype(F32), qp, i)
    acc[...] = jnp.zeros_like(acc)
    accm[...] = jnp.zeros_like(accm)
    vt[64:80] = jnp.ones((16, 512), BF16)

    def pair(dp):
        p = lax.rem(b // 2 + 16 - dp, 16)
        send_pieces(c_piece, 32 + 3 * dp, 35 + 3 * dp, c)
        times(jnp.minimum(16 * dp, NB) + (dp == 0), jnp.minimum(16 * dp + 16, NB), lambda d: wo_first(d).start())
        for kb in (2 * p, 2 * p + 1):

            @pl.when(kb != b)
            def _():
                settle(r2.at[lax.rem(b + NB - kb, NB)], kvs.at[kb])

        vt[0:64] = (
            kvs[pl.ds(2 * p, 2)].reshape(512, 128).astype(F32).T[64:128].astype(BF16)
        )

        def scores(i):
            keys = kvs[pl.ds(2 * p, 2)].reshape(512, 128)
            return jnp.exp(lax.dot_general(keys, qp[i], NT, preferred_element_type=F32))

        def inside(i):
            acc[i] += jnp.dot(vt[...], scores(i).astype(BF16), preferred_element_type=F32)

        def edge(i, qb):
            low, high = limits(query_positions((1, 1024), 1, qb), e0, e1, total)
            kpos = key_positions((512, 1), 0, 2 * p, c)
            expo = jnp.where((kpos >= low) & (kpos < high), scores(i), 0.0)
            accm[i] += jnp.dot(vt[...], expo.astype(BF16), preferred_element_type=F32)

        on_pair(p, m, inside, edge)

    times(0, 10, pair)
    settle(ro.at[0], wov.at[0, c, rows(0, 992)])
    wo_moves = [
        to(wov.at[0, c], wov.at[0, c], sx.at[6], rx.at[6], b, sib),
        to(wov.at[0, c], wov.at[1, c], sx.at[4], rx.at[4], b, over),
    ]
    for item in wo_moves:
        item.start()
    times(10, 16, pair)
    for i in range(GROUP):
        pos = query_positions((1, 1024), 1, member(m, i))
        acc[i] = accm[i] + jnp.where((pos >= e0) & (pos < e1), acc[i], 0.0)
    swap = to(acc, peer, sx.at[5], rx.at[5], b, sib)
    swap.start()
    keep(kvs, kv_out)
    for item in wo_moves:
        item.wait()
    far_sib = to(wov.at[1, c], wov.at[1, c], sx.at[7], rx.at[7], b, sib)
    far_sib.start()
    swap.wait()

    def ctx_piece(dj, dx):
        j = lax.rem(y + dj, GROUP)
        x2 = lax.rem(xl + dx, 2)
        cols = pl.ds(pl.multiple_of((4 * xl + y) * 128, 128), 128)
        src, dst = ctx.at[j, rows(c * 256 + x2 * 128, 128)], ctx_in.at[:, cols]
        k = 2 * dj + dx
        if k == 0:
            return pltpu.make_async_copy(src, dst, ls.at[6])
        return to(src, dst, s7.at[k], r7.at[k], member(m, j), 2 * x2 + c)

    ctx_pieces = [ctx_piece(dj, dx) for dj in range(GROUP) for dx in range(2)]
    for i in range(GROUP):
        both = acc[i] + peer[i]
        inverse = 1.0 / both[64:65]
        wide = both[0:64] * inverse
        flat = jnp.concatenate([wide[:, 0:512], wide[:, 512:1024]], axis=0).T
        wide_all[i] = flat
        ctx[i] = flat.astype(BF16)
        spread = jnp.broadcast_to(inverse, (64, 1024))
        inv_all[i] = jnp.concatenate([spread[:, 0:512], spread[:, 512:1024]], axis=0).T
    for item in ctx_pieces:
        item.start()
    keep(wide_all, wide_out)
    keep(inv_all, inv_out)
    far_sib.wait()
    keep(wov, wo_out)
    for item in ctx_pieces:
        item.wait()

    context = ctx_in[...]
    ctx_out[...] = context
    for i in range(2):
        for x2, part in ((xl, wov[0, i]), (1 - xl, wov[1, i])):
            cols = rows(512 * x2 + 256 * i, 256)
            mid_out[:, cols] = li[:, cols].astype(F32) + jnp.dot(
                context, part, preferred_element_type=F32
            )
    middle = mid_out[...]
    mixed = (middle * row_scale(middle) * ffn_gain[...]).astype(BF16)
    own = rows(c * 128, 128)
    tok[own] = mixed
    tok_swap = to(tok.at[own], tok.at[own], sx.at[8], rx.at[8], b, sib)
    tok_swap.start()
    logits = lax.dot_general(
        mixed.astype(F32), router[...], NT, preferred_element_type=F32, precision=PRECISE
    )
    expert = lax.broadcasted_iota(jnp.int32, (128, 128), 0)
    hit = jnp.zeros((128, 128), F32)
    for k in range(TOPK):
        hit = jnp.where(routes_t[k : k + 1] == expert, 1.0, hit)
    hit = hit.T
    top = jnp.max(jnp.where(hit > 0.0, logits, -1e30), axis=1, keepdims=True)
    weight = jnp.where(hit > 0.0, jnp.exp(logits - top), 0.0)
    gt[own] = weight / jnp.sum(weight, axis=1, keepdims=True)
    gates_swap = to(gt.at[own], gt.at[own], sx.at[9], rx.at[9], b, sib)
    gates_swap.start()

    settle(sw.at[0], wv.at[0, rows(0, 992)])
    settle(so.at[0], wov.at[0, 0, rows(0, 992)])
    settle(s2.at[0], kvs.at[pl.ds(0, NB - 1)])
    settle_rows(s5.at[0], xs, c)
    settle_rows(r5.at[0], xs, c)
    pl.when(c == 0)(c_same.wait)
    tok_swap.wait()
    gates_swap.wait()
    tok_out[...] = tok[...]
    gates_out[...] = gt[...]
    for item in keeps:
        item.wait()


def row_peer(b, xl, c, k):
    e = 2 * k + lax.rem(b + c, 2)
    apart = lax.rem(b // 4 + e // 4, 2)
    return e, 2 * (xl + apart - 2 * xl * apart) + c


def stride(b, d):
    return lax.rem(b // 2 + 5 * d, 16)


def rows_out(src, dst, b, xl, c, send, recv):
    def piece(d, r):
        k = stride(b, d)
        e, head = row_peer(b, xl, c, k)
        if src.shape[1] < 16:
            return to(src.at[k], dst.at[d - 1], send(r), recv(r), e, head)
        part = rows(16 * r, 16)
        return to(src.at[k, part], dst.at[d - 1, part], send(r), recv(r), e, head)

    return piece


def rows_home(src, dst, b, xl, c, send, recv):
    def piece(d, r):
        e, head = row_peer(b, xl, c, stride(b, 16 - d))
        if src.shape[1] < 16:
            return to(src.at[d - 1], dst.at[b // 2], send(r), recv(r), e, head)
        part = rows(16 * r, 16)
        return to(src.at[d - 1, part], dst.at[b // 2, part], send(r), recv(r), e, head)

    return piece


def send_pieces(piece, start, stop, c):
    def one(i):
        d = lax.rem(i, 16) + 1
        pl.when((d < 16) | (c == 1))(lambda: piece(d, i // 16).start())

    times(start, stop, one)


def start_tiles(piece, d, c, local):
    pl.when((d < 16) | (c == 1))(lambda: piece(d, 0).start())
    pl.when((d == 16) & (c == 0))(local.start)


def experts_kernel(
    tok, gt, pick, up_hbm, gate_hbm, upw_hbm, down_hbm, middle_hbm, cot_hbm, ffn_gain, router_hbm,
    wts_hbm, eo_hbm, ex_hbm, grad_out, low_out, small_out, router_out,
    up_rows, gate_w, up_w, down_w, middle_ref, cot, router, wts_out, eo_out, ex_out,
    xs, xl_rows, gs, gl, rs, rl, ggs, ggl, hid, gb, ub, og, mgs, ggt, mg_in, gg_in, gg_all, gcol, ggcol,
    s1, r1, s2, r2, s3, r3, s4, r4, sx, rx, ls, li, lo,
):
    b, xl, c, _, _ = place()
    h = 2 * xl + c
    sib = 2 * xl + 1 - c
    odd = lax.rem(b + c, 2)
    brought = [
        pltpu.make_async_copy(src, dst, li.at[n])
        for n, (src, dst) in enumerate(
            (
                (gate_hbm, gate_w),
                (upw_hbm, up_w),
                (down_hbm, down_w),
                (up_hbm, up_rows),
                (middle_hbm, middle_ref),
                (cot_hbm, cot),
                (router_hbm, router),
            )
        )
    ]
    for item in brought:
        item.start()
    bar = pltpu.get_barrier_semaphore()

    def greet(d):
        e, head = row_peer(b, xl, c, stride(b, d))
        signal(bar, e, head)

    times(1, 16, greet)
    signal(bar, b, sib)
    pl.when(c == 1)(lambda: greet(0))
    pl.semaphore_wait(bar, 16 + c)
    x_piece = rows_out(xs, xl_rows, b, xl, c, lambda r: s1.at[0], lambda r: r1.at[r])
    x_same = pltpu.make_async_copy(xs.at[b // 2], xl_rows.at[15], ls.at[0])

    def fetch(r):
        part = rows(16 * r, 16)
        xs[:, part] = (
            jnp.dot(pick[:, part].reshape(256, 256), tok[...], preferred_element_type=F32)
            .astype(BF16)
            .reshape(16, 16, 1024)
        )
        send_pieces(x_piece, 16 * r, 16 * r + 16, c)

    times(0, 1, fetch)
    high = gt[...].astype(BF16)
    rest = gt[...] - high.astype(F32)
    mid = rest.astype(BF16)
    low = (rest - mid.astype(F32)).astype(BF16)
    g_piece = rows_out(gs, gl, b, xl, c, lambda r: s2.at[0], lambda r: r2.at[0])
    g_same = pltpu.make_async_copy(gs.at[b // 2], gl.at[15], ls.at[1])

    def as_row(column):
        wide = jnp.concatenate([jnp.broadcast_to(column, (80, 128)), jnp.zeros((48, 128), F32)])
        return wide.T[0:8]

    spread = jnp.dot(
        pick[...].reshape(1280, 256),
        jnp.concatenate([high, mid, low], axis=1),
        preferred_element_type=F32,
    )
    spread = spread[:, 0:128] + spread[:, 128:256] + spread[:, 256:384]
    lane = lax.broadcasted_iota(jnp.int32, (1280, 128), 1)
    expert = 2 * (lax.broadcasted_iota(jnp.int32, (1280, 128), 0) // 80) + odd
    column = jnp.sum(jnp.where(lane == expert, spread, 0.0), axis=1, keepdims=True)
    for k in range(16):
        gs[k] = as_row(column[80 * k : 80 * k + 80])
    times(1, 17, lambda d: start_tiles(g_piece, d, c, g_same))
    times(1, ROUNDS, fetch)
    pl.when(c == 0)(x_same.start)
    weights = pick[...].reshape(1280, 256).astype(F32) * column
    weights_high = weights.astype(BF16)
    wts_out[0] = weights_high.reshape(16, 80, 256)
    wts_out[1] = (weights - weights_high.astype(F32)).astype(BF16).reshape(16, 80, 256)
    wts_keep = pltpu.make_async_copy(wts_out, wts_hbm, lo.at[0])
    wts_keep.start()
    for item in brought:
        item.wait()
    home = rows_home(rs, rl, b, xl, c, lambda r: s3.at[0], lambda r: r3.at[0])
    home_same = pltpu.make_async_copy(rs.at[15], rl.at[b // 2], ls.at[2])
    gg_home = rows_home(ggs, ggl, b, xl, c, lambda r: s4.at[0], lambda r: r4.at[0])
    gg_same = pltpu.make_async_copy(ggs.at[15], ggl.at[b // 2], ls.at[3])

    pl.when(c == 0)(x_same.wait)

    def group(r):
        part = rows(16 * r, 16)
        pl.when(c == 0)(lambda: settle(r1.at[r], xl_rows.at[pl.ds(0, 15), part]))
        pl.when(c == 1)(lambda: settle(r1.at[r], xl_rows.at[:, part]))
        x = xl_rows[:, part].reshape(256, 1024)
        u = up_rows[:, part].reshape(256, 1024).astype(F32)
        gate_pre = jnp.dot(x, gate_w[0], preferred_element_type=F32)
        up_pre = jnp.dot(x, up_w[0], preferred_element_type=F32)
        sig = jax.nn.sigmoid(gate_pre)
        act = gate_pre * sig
        hidden = (act * up_pre).astype(BF16)
        out = jnp.dot(hidden, down_w[0], preferred_element_type=F32).astype(BF16)
        eo_out[:, part] = out.reshape(16, 16, 1024)
        gate_grad = jnp.sum(u * out.astype(F32), axis=1, keepdims=True)
        ggcol[:, part] = jnp.broadcast_to(gate_grad, (256, 128)).reshape(16, 16, 128)
        @pl.when(r == 0)
        def _():
            settle_rows(r2.at[0], gl, c)
            pl.when(c == 0)(g_same.wait)
            for n in range(16):
                row = jnp.concatenate([gl[n], jnp.zeros((120, 128), F32)])
                gcol[n] = jnp.broadcast_to(row.T[0:80, 0:1], (80, 128))

        out_grad = (gcol[:, part].reshape(256, 128)[:, 0:1] * u).astype(BF16)
        hidden_grad = lax.dot_general(out_grad, down_w[0], NT, preferred_element_type=F32)
        gate_back = (hidden_grad * up_pre * sig * (1.0 + gate_pre * (1.0 - sig))).astype(BF16)
        up_back = (hidden_grad * act).astype(BF16)
        back = lax.dot_general(
            gate_back, gate_w[0], NT, preferred_element_type=F32
        ) + lax.dot_general(up_back, up_w[0], NT, preferred_element_type=F32)
        rs[:, part] = back.astype(BF16).reshape(16, 16, 1024)
        send_pieces(home, 16 * r, 16 * r + 16, c)
        hid[:, part] = hidden.reshape(16, 16, 512)
        gb[:, part] = gate_back.reshape(16, 16, 512)
        ub[:, part] = up_back.reshape(16, 16, 512)
        og[:, part] = out_grad.reshape(16, 16, 1024)

    times(0, ROUNDS, group)
    pl.when(c == 0)(home_same.start)
    for n in range(16):
        ggs[n] = as_row(ggcol[n, :, 0:1])
        start_tiles(gg_home, n + 1, c, gg_same)
    eo_keep = pltpu.make_async_copy(eo_out, eo_hbm, lo.at[1])
    eo_keep.start()
    for j in range(4):
        part = slice(256 * j, 256 * j + 256)
        x_turned = xl_rows[:, :, part].reshape(1280, 256)
        for n, grads in ((0, gb), (1, ub)):
            ex_out[n, part] = lax.dot_general(
                x_turned, grads[...].reshape(1280, 512), TN, preferred_element_type=F32
            ).astype(BF16)
        half = slice(512 * (j // 2), 512 * (j // 2) + 512)
        place_at = 512 * (j % 2) + 256 * (j // 2)
        turned = hid[:, :, 256 * (j % 2) : 256 * (j % 2) + 256].reshape(1280, 256)
        ex_out[2, place_at : place_at + 256] = lax.dot_general(
            turned, og[:, :, half].reshape(1280, 512), TN, preferred_element_type=F32
        ).astype(BF16)

    ex_keep = pltpu.make_async_copy(ex_out, ex_hbm, lo.at[2])
    ex_keep.start()
    settle_rows(r4.at[0], ggl, c)
    pl.when(c == 0)(gg_same.wait)
    for k in range(16):
        column = jnp.concatenate([ggl[k], jnp.zeros((120, 128), F32)]).T[0:80, 0:1]
        ggt[pl.ds(k, 1)] = jnp.sum(pick[k].astype(F32) * column, axis=0, keepdims=True)
    settle_rows(r3.at[0], rl, c)
    pl.when(c == 0)(home_same.wait)
    mgs[...] = lax.dot_general(
        pick[...].reshape(1280, 256), rl[...].reshape(1280, 1024), TN, preferred_element_type=F32
    )
    away = rows((1 - c) * 128, 128)
    own = rows(c * 128, 128)
    back_near = [
        to(ggt.at[:, away], gg_in, sx.at[3], rx.at[3], b, sib),
        to(mgs.at[away], mg_in, sx.at[2], rx.at[2], b, sib),
    ]
    for item in back_near:
        item.start()
    settle_rows(s1.at[0], xs, c)
    settle_rows(s2.at[0], gs, c)
    settle_rows(s3.at[0], rs, c)
    settle_rows(s4.at[0], ggs, c)
    back_near[0].wait()

    gg_all[...] = jnp.zeros_like(gg_all)
    for k in range(16):
        gg_all[pl.ds(2 * k + odd, 1)] = ggt[pl.ds(k, 1), own]
        gg_all[pl.ds(2 * k + 1 - odd, 1)] = gg_in[pl.ds(k, 1)]
    gate_grad = gg_all[...].T
    own_gates = gt[own]
    logit_grad = own_gates * (
        gate_grad - jnp.sum(own_gates * gate_grad, axis=1, keepdims=True)
    )
    router_out[...] = lax.dot_general(
        logit_grad, tok[own].astype(F32), TN, preferred_element_type=F32, precision=PRECISE
    )[0:NB]
    routed = jnp.dot(
        logit_grad, router[...], preferred_element_type=F32, precision=PRECISE
    )
    back_near[1].wait()
    mixed_grad = mgs[own] + mg_in[...] + routed
    middle = middle_ref[...]
    scale = row_scale(middle)
    unit = middle * scale
    small_out[...] = jnp.sum(mixed_grad * unit, axis=0, keepdims=True)
    inner = mixed_grad * ffn_gain[...]
    grad = cot[...].astype(F32) + scale * (
        inner - unit * jnp.mean(inner * unit, axis=1, keepdims=True)
    )
    grad_out[...] = grad
    low_out[...] = grad.astype(BF16)
    for item in (wts_keep, eo_keep, ex_keep):
        item.wait()


def backward_kernel(
    lengths, attn_grad, context, wo, head_gain, attn_gain, ffn_part, router_part, eo, ex,
    q_hbm, kv_hbm, wide_hbm, inv_hbm, wv_hbm, raw_hbm, normed_hbm, li_hbm, turn_hbm, wts_hbm, mid_hbm, grad_hbm,
    out, in_grad, wq_grad, wk_grad, wv_grad, wo_grad, attn_small, q_small, k_small, ffn_small, router_grad,
    exg_out, exu_out, exd_out,
    q_ref, kv_ref, wide_ref, inv_ref, wv, raw, normed, li2, turn, wts, middle, grad,
    cg, cgs, qp, gp, gi, qt, gt, gti, dt, di, dqs, dkvt, stage, dq_acc,
    wo_other, wo_in, wo_sum, ex_in, ex_sum, ex_cross, dq, dkv, home, wo_parts,
    low, w_other, w_in, w_sum, w_land, back, back_low, back_in, mix, mix_in, small, four, many,
    r_land, r_four, r_tot, router_out,
    s1, r1, s2, r2, s3, r3, s4, r4, s5, r5, s6, r6, s7, r7, s8, r8, s9, r9, sa, ra, sx, rx, ls, li, se, re, le,
):
    b, xl, c, y, m = place()
    h = 2 * xl + c
    sib = 2 * xl + 1 - c
    over = 2 * (1 - xl) + c
    e0, e1, total = lengths[0], lengths[0] + lengths[1], 512 * NB
    brought = [
        pltpu.make_async_copy(src, dst, li.at[n])
        for n, (src, dst) in enumerate(
            (
                (q_hbm, q_ref),
                (kv_hbm, kv_ref),
                (wide_hbm, wide_ref),
                (inv_hbm, inv_ref),
                (wv_hbm, wv),
                (raw_hbm, raw),
                (normed_hbm, normed),
                (li_hbm, li2),
                (turn_hbm, turn),
                (wts_hbm, wts),
                (mid_hbm, middle),
                (grad_hbm, grad),
            )
        )
    ]
    for item in brought:
        item.start()
    bar = pltpu.get_barrier_semaphore()
    for dj in range(GROUP):
        j = member(m, lax.rem(y + dj, GROUP))
        signal(bar, j, 2 * (1 - xl) + 1 - c)
        signal(bar, j, 2 * xl + 1 - c)
    times(1, NB, lambda d: signal(bar, lax.rem(b + d, NB), h))
    times(0, NB, lambda d: signal(bar, lax.rem(b + d, NB), over))
    pl.semaphore_wait(bar, 2 * NB - 1 + 2 * GROUP)

    ex_swap = to(ex.at[:, rows((1 - c) * 512, 512)], ex_in, sx.at[1], rx.at[1], b, sib)
    ex_swap.start()
    ex_own = pltpu.make_async_copy(ex.at[:, rows(c * 512, 512)], ex_sum, ls.at[1])
    ex_own.start()
    turned_back = jnp.zeros((128, 1024), F32)
    for i in range(2):
        for x2, part in ((xl, wo[0, i]), (1 - xl, wo[1, i])):
            turned_back = turned_back + lax.dot_general(
                attn_grad[:, rows(512 * x2 + 256 * i, 256)], part, NT, preferred_element_type=F32
            )
    cg[...] = turned_back.astype(BF16)
    turns = [(dj, dx, dc) for dj in range(GROUP) for dx in range(2) for dc in range(2)]
    cg_pieces = []
    for k, (dj, dx, dc) in enumerate(turns):
        j = lax.rem(y + dj, GROUP)
        x2 = lax.rem(xl + dx, 2)
        cols = pl.ds(pl.multiple_of((4 * x2 + j) * 128, 128), 128)
        src, dst = cg.at[:, cols], cgs.at[y, rows(c * 256 + xl * 128, 128)]
        if k == 0:
            cg_pieces.append(pltpu.make_async_copy(src, dst, ls.at[0]))
        else:
            head = 2 * x2 + lax.rem(c + dc, 2)
            cg_pieces.append(to(src, dst, s1.at[0], r1.at[0], member(m, j), head))
    for item in cg_pieces:
        item.start()

    def tile(n):
        return router_part.at[rows(8 * (n // 8), 8), rows(128 * lax.rem(n, 8), 128)]

    def router_first(d):
        to_b = lax.rem(b + d, NB)
        return to(tile(to_b), r_land.at[b], s8.at[0], r8.at[0], to_b, h)

    times(1, NB, lambda d: router_first(d).start())
    r_land[b] = router_part[rows(8 * (b // 8), 8), rows(128 * lax.rem(b, 8), 128)]

    eo_piece = rows_home(eo, home, b, xl, c, lambda r: s2.at[0], lambda r: r2.at[0])
    eo_same = pltpu.make_async_copy(eo.at[15], home.at[b // 2], ls.at[2])
    pl.when(c == 0)(eo_same.start)
    send_pieces(eo_piece, 0, 32, c)

    def out_part(x2, core):
        cols = pl.ds(pl.multiple_of(512 * x2 + 256 * core, 256), 256)
        return lax.dot_general(
            context[...], attn_grad[:, cols], TN, preferred_element_type=F32
        )

    for x2 in range(2):
        wo_other[x2] = out_part(x2, 1 - c).astype(BF16)
    wo_swap = to(wo_other, wo_in, sx.at[0], rx.at[0], b, sib)
    wo_swap.start()
    brought[0].wait()
    for i in range(GROUP):
        both = q_ref[i].astype(F32)
        pad_queries(both, qp, i)
        turned = both.T
        qt[i] = jnp.concatenate([turned[0:64], turned[64:128]], axis=1).astype(BF16)
    dq_acc[...] = jnp.zeros_like(dq_acc)
    wo_swap.wait()
    for x2 in range(2):
        wo_sum[x2] = (out_part(x2, c) + wo_in[x2].astype(F32)).astype(BF16)
    ex_swap.wait()
    ex_own.wait()
    ex_sum[...] = (ex_sum[...].astype(F32) + ex_in[...].astype(F32)).astype(BF16)

    def cross_piece(n, j):
        part = rows(32 * j, 32)
        return to(ex_sum.at[n, part], ex_cross.at[n, part], sx.at[2], rx.at[2], b, over)


    def wo_piece(e):
        d, x2 = lax.rem(e, NB), lax.rem(xl + e // NB, 2)
        peer_b = lax.rem(b + d, NB)
        part = wo_sum.at[x2, rows(peer_b * 32, 32)]
        return to(part, wo_parts.at[NB * (e // NB) + b], s3.at[0], r3.at[0], peer_b, 2 * x2 + c)

    for n in range(3):
        times(0, 8, lambda j, n=n: cross_piece(n, j).start())
    cg_pieces[0].wait()
    settle(r1.at[0], home.at[pl.ds(0, 3)])
    wo_parts[b] = wo_sum[xl, rows(b * 32, 32)]
    for item in brought[1:4]:
        item.wait()
    left = lax.broadcasted_iota(jnp.int32, (512, 128), 1) < 64
    for i in range(GROUP):
        scaled = cgs[i].astype(F32) * inv_ref[i]
        pos = query_positions((512, 1), 0, member(m, i))
        mid_doc = (pos >= e0) & (pos < e1)
        terms = scaled * wide_ref[i]
        one = jnp.sum(jnp.where(left, terms, 0.0), axis=1, keepdims=True)
        two = jnp.sum(jnp.where(left, 0.0, terms), axis=1, keepdims=True)
        upper = jnp.where(left, 0.0, pltpu.roll(scaled, 64, 1))
        lower = jnp.where(left, 0.0, scaled)
        for part, val, term in ((0, upper, one), (512, lower, two)):
            span = pl.ds(part, 512)
            gp[i, span] = val.astype(BF16)
            gi[i, span] = jnp.where(mid_doc, val, 0.0).astype(BF16)
            dt[i, span] = jnp.broadcast_to(term, (512, 128))
            di[i, span] = jnp.broadcast_to(jnp.where(mid_doc, term, 0.0), (512, 128))
            lanes = pl.ds(part, 512)
            gt[i, :, lanes] = val.T[64:128].astype(BF16)
            gti[i, :, lanes] = jnp.where(mid_doc, val, 0.0).T[64:128].astype(BF16)

    def dkv_piece(kb):
        return to(stage.at[kb], dkv.at[b], s4.at[0], r4.at[0], kb, h)

    def pair(dp):
        p = lax.rem(b // 2 + 1 + dp, 16)
        send_pieces(eo_piece, jnp.minimum(32 + 5 * dp, 80), jnp.minimum(37 + 5 * dp, 80), c)
        for n in range(3):
            pl.when(dp < 8)(lambda n=n: cross_piece(n, dp + 8).start())
        times(
            jnp.clip(7 * (dp - 3), 1, 2 * NB),
            jnp.clip(7 * (dp - 2), 1, 2 * NB),
            lambda e: wo_piece(e).start(),
        )
        dkvt[...] = jnp.zeros_like(dkvt)
        keys = kv_ref[pl.ds(2 * p, 2)].reshape(512, 128)

        def step(i, expo, g, gturn, dots):
            prob = lax.dot_general(g[i], keys, NT, preferred_element_type=F32)
            term = jnp.concatenate([dots[i]] * 4, axis=1)
            score_grad = (expo * (prob - term)).astype(BF16)
            dq_acc[i] += jnp.dot(score_grad, keys, preferred_element_type=F32)
            dkvt[0:64] += jnp.dot(qt[i], score_grad, preferred_element_type=F32)
            dkvt[64:128] += jnp.dot(gturn[i], expo.astype(BF16), preferred_element_type=F32)

        def scores(i):
            return jnp.exp(lax.dot_general(qp[i], keys, NT, preferred_element_type=F32))

        def inside(i):
            step(i, scores(i), gi, gti, di)

        def edge(i, qb):
            low, high = limits(query_positions((1024, 1), 0, qb), e0, e1, total)
            kpos = key_positions((1, 512), 1, 2 * p, c)
            expo = jnp.where((kpos >= low) & (kpos < high), scores(i), 0.0)
            step(i, expo, gp, gt, dt)

        on_pair(p, m, inside, edge)
        for n in range(2):
            kb = 2 * p + n
            stage[kb] = dkvt[:, 256 * n : 256 * n + 256].astype(BF16)

            @pl.when(kb != b)
            def _():
                dkv_piece(kb).start()

    times(0, 6, pair)
    settle(r8.at[0], r_land.at[pl.ds(0, NB - 1)])
    part = r_land[0]
    for n in range(1, NB):
        part = part + r_land[n]
    r_four[h] = part
    router_near = [
        to(r_four.at[h], r_four.at[h], s9.at[d], r9.at[d], b, lax.rem(h + d, 4))
        for d in range(1, 4)
    ]
    for item in router_near:
        item.start()
    times(6, 16, pair)
    dkv[b] = stage[b]
    for i in range(GROUP):
        both = jnp.where(left, dq_acc[i, 0:512], pltpu.roll(dq_acc[i, 512:1024], 64, 1))
        dqs[i] = (both * SCALE).astype(BF16)

    def dq_piece(part, dj, dc):
        j = lax.rem(y + dj, GROUP)
        c2 = lax.rem(c + dc, 2)
        cols = pl.ds(pl.multiple_of(y * 128, 128), 128)
        src = dqs.at[j, rows(c2 * 256 + part * 128, 128)]
        dst = dq.at[c, rows(part * 128, 128), cols]
        k = 8 * part + 2 * dj + dc
        if dj + dc == 0:
            return pltpu.make_async_copy(src, dst, s5.at[k])
        return to(src, dst, s5.at[k], r5.at[k], member(m, j), 2 * xl + c2)

    dq_pieces = [dq_piece(n, dj, dc) for n in range(2) for dj in range(GROUP) for dc in range(2)]
    for item in dq_pieces:
        item.start()
    for item in router_near:
        item.wait()
    r_tot[...] = r_four[0] + r_four[1] + r_four[2] + r_four[3]
    home_tile = (rows(8 * (b // 8), 8), rows(128 * lax.rem(b, 8), 128))
    router_out[home_tile] = r_tot[...]

    def router_last(d):
        return to(r_tot, router_out.at[home_tile], sa.at[0], ra.at[0], lax.rem(b + d, NB), h)

    times(1, NB, lambda d: router_last(d).start())
    settle(sx.at[2], ex_cross)
    settle(rx.at[2], ex_cross)
    ex_in[...] = (ex_sum[...].astype(F32) + ex_cross[...].astype(F32)).astype(BF16)
    half, quarter = rows(c * 512, 512), rows(c * 256, 256)
    ex_moves = []
    for n, (src, dst) in enumerate(
        (
            (ex_in.at[0], exg_out.at[half]),
            (ex_in.at[1], exu_out.at[half]),
            (ex_in.at[2, pl.ds(0, 256)], exd_out.at[quarter, pl.ds(0, 512)]),
            (ex_in.at[2, pl.ds(256, 256)], exd_out.at[quarter, pl.ds(512, 512)]),
        )
    ):
        ex_moves.append(pltpu.make_async_copy(src, dst, le.at[n]))
        ex_moves.append(to(src, dst, se.at[n], re.at[n], b, sib))
    for item in ex_moves:
        item.start()
    for item in dq_pieces:
        item.wait()
    settle(r4.at[0], dkv.at[pl.ds(0, NB - 1)])

    for item in brought[4:]:
        item.wait()
    left, first = lanes_of((256, 128))
    q_gain = jnp.zeros((1, 128), F32)
    k_gain = jnp.zeros((1, 128), F32)

    def unprep(d, u, gain, row):
        turned = d * turn[0] - swapped(d, first) * turn[1]
        scale = lax.rsqrt(by_head(u * u, left) + EPSILON)
        unit = u * scale
        inner = turned * row
        gain = gain + jnp.sum(turned * unit, axis=0, keepdims=True)
        return scale * (inner - unit * by_head(inner * unit, left)), gain

    for j in range(GROUP):
        i, q_cols, kv_cols = slab(j)
        span = slice(128 * j, 128 * j + 128)
        d = (dq[0, :, span].astype(F32) + dq[1, :, span].astype(F32)).astype(BF16).astype(F32)
        got, q_gain = unprep(d, raw[i, :, q_cols], q_gain, head_gain[0:1])
        low[i, :, q_cols] = got.astype(BF16)
        d = dkv[8 * j].astype(F32)
        for n in range(1, 8):
            d = d + dkv[8 * j + n].astype(F32)
        d = d.T.astype(BF16).astype(F32)
        got, k_gain = unprep(d, raw[i, :, kv_cols], k_gain, head_gain[1:2])
        low[i, :, kv_cols] = jnp.where(left, got, d).astype(BF16)
    normed_grad = lax.dot_general(low[0], wv[0], NT, preferred_element_type=F32) + lax.dot_general(
        low[1], wv[1], NT, preferred_element_type=F32
    )
    source2 = li2[...].reshape(256, 1024).astype(F32)
    scale = row_scale(source2)
    unit = source2 * scale
    inner = normed_grad * attn_gain[...]
    attn_part = jnp.sum(normed_grad * unit, axis=0, keepdims=True)
    small[...] = jnp.zeros_like(small)
    for n in range(8):
        lanes = slice(128 * n, 128 * n + 128)
        small[n : n + 1] = attn_part[:, lanes]
        small[8 + n : 9 + n] = ffn_part[:, lanes]
    small[16:17] = q_gain
    small[17:18] = k_gain
    near = [
        to(small, four.at[h], sx.at[6 + d], rx.at[6 + d], b, lax.rem(h + d, 4)) for d in range(1, 4)
    ]
    for item in near:
        item.start()
    four[h] = small[...]
    w_other[...] = lax.dot_general(
        normed[...], low[1 - c], TN, preferred_element_type=F32
    ).astype(BF16).reshape(NB, 32, 512)
    w_swap = to(w_other, w_in, sx.at[4], rx.at[4], b, sib)
    w_swap.start()
    back[...] = (scale * (inner - unit * jnp.mean(inner * unit, axis=1, keepdims=True))).reshape(
        2, 128, 1024
    )
    back_low[...] = back[1 - xl].astype(BF16)
    back_swap = to(back_low, back_in, sx.at[5], rx.at[5], b, over)
    back_swap.start()
    mine = lax.dot_general(normed[...], low[c], TN, preferred_element_type=F32)
    for item in near:
        item.wait()
    many[b] = four[0] + four[1] + four[2] + four[3]

    def spread(d):
        return to(many.at[b], many.at[b], s7.at[0], r7.at[0], lax.rem(b + d, NB), h)

    times(1, NB, lambda d: spread(d).start())
    w_swap.wait()
    w_sum[...] = (mine.reshape(NB, 32, 512) + w_in[...].astype(F32)).astype(BF16)

    def w_piece(d):
        peer = lax.rem(b + d, NB)
        return to(w_sum.at[peer], w_land.at[b], s6.at[0], r6.at[0], peer, h)

    times(1, NB, lambda d: w_piece(d).start())
    w_land[b] = w_sum[b]

    settle_rows(r2.at[0], home, c)
    pl.when(c == 0)(eo_same.wait)
    flat = home[...].reshape(1280, 1024)
    mix[...] = (
        lax.dot_general(wts[0].reshape(1280, 256), flat, TN, preferred_element_type=F32)
        + lax.dot_general(wts[1].reshape(1280, 256), flat, TN, preferred_element_type=F32)
    ).reshape(2, 128, 1024)
    mix_swap = to(mix.at[1 - c], mix_in, sx.at[6], rx.at[6], b, sib)
    mix_swap.start()
    back_swap.wait()
    in_grad[...] = (grad[...] + back[xl] + back_in[...].astype(F32)).astype(BF16)
    mix_swap.wait()
    out[...] = (middle[...] + mix[c] + mix_in[...]).astype(BF16)
    settle(r7.at[0], many.at[pl.ds(0, NB - 1)])
    total = many[0]
    for n in range(1, NB):
        total = total + many[n]
    for n in range(8):
        lanes = slice(128 * n, 128 * n + 128)
        attn_small[:, lanes] = total[n : n + 1]
        ffn_small[:, lanes] = total[8 + n : 9 + n]
    q_small[...] = total[16:17, 0:64] + total[16:17, 64:128]
    k_small[...] = total[17:18, 0:64]
    settle(r6.at[0], w_land.at[pl.ds(0, NB - 1)])
    shard = w_land[0].astype(F32)
    for n in range(1, NB):
        shard = shard + w_land[n].astype(F32)
    wq_grad[...] = shard[:, 0:256]
    wk_grad[...] = jnp.concatenate([shard[:, 256:320], shard[:, 384:448]], axis=1)
    wv_grad[...] = jnp.concatenate([shard[:, 320:384], shard[:, 448:512]], axis=1)
    settle(r3.at[0], wo_parts.at[pl.ds(0, 2 * NB - 1)])
    total = wo_parts[0].astype(F32)
    for n in range(1, 2 * NB):
        total = total + wo_parts[n].astype(F32)
    wo_grad[...] = total
    for item in ex_moves:
        item.wait()
    settle(ra.at[0], r_land.at[pl.ds(0, NB - 1)])
    router_grad[...] = router_out[...]
    settle(s1.at[0], home.at[pl.ds(0, 3)])
    settle_rows(s2.at[0], home, c)
    settle(s3.at[0], wo_parts.at[pl.ds(0, 2 * NB - 1)])
    settle(s4.at[0], dkv.at[pl.ds(0, NB - 1)])
    settle(s6.at[0], w_land.at[pl.ds(0, NB - 1)])
    settle(s7.at[0], many.at[pl.ds(0, NB - 1)])
    settle(s8.at[0], r_land.at[pl.ds(0, NB - 1)])
    settle(sa.at[0], r_land.at[pl.ds(0, NB - 1)])


def results_kernel(*refs):
    n = (len(refs) - 5) // 3
    ins, outs, held = refs[:n], refs[n : 2 * n], refs[2 * n : 3 * n]
    wide, (load_sem, store_sem) = refs[3 * n : 3 * n + 3], refs[3 * n + 3 :]
    loads = [pltpu.make_async_copy(ins[k], held[k], load_sem.at[k]) for k in range(n)]
    for item in loads[n - 3 :] + loads[: n - 3]:
        item.start()
    stores = []
    for k in [n - 3, n - 2, n - 1, *range(n - 3)]:
        loads[k].wait()
        src, dst = held[k], outs[k]
        if k >= n - 3:
            src, dst = wide[k - n + 3], dst.at[0]
            src[...] = held[k][...].astype(F32)
        stores.append(pltpu.make_async_copy(src, dst, store_sem.at[k]))
        stores[-1].start()
    for item in stores:
        item.wait()


def finished(results):
    n = len(results)
    shapes = [jax.ShapeDtypeStruct(r.shape, r.dtype) for r in results[: n - 3]] + [
        jax.ShapeDtypeStruct((1,) + r.shape, F32) for r in results[n - 3 :]
    ]
    return pl.pallas_call(
        results_kernel,
        out_shape=shapes,
        in_specs=[ANY] * n,
        out_specs=[ANY] * n,
        scratch_shapes=[pltpu.VMEM(r.shape, r.dtype) for r in results]
        + [pltpu.VMEM(r.shape, F32) for r in results[n - 3 :]]
        + [pltpu.SemaphoreType.DMA((n,))] * 2,
        compiler_params=pltpu.CompilerParams(vmem_limit_bytes=60 * 1024 * 1024),
    )(*results)


VM = pl.BlockSpec(memory_space=pltpu.VMEM)
SM = pl.BlockSpec(memory_space=pltpu.SMEM)
ANY = pl.BlockSpec(memory_space=pl.ANY)


def call(kernel, collective_id, ins, outs, scratch, sems, flops, *operands):
    return pl.pallas_call(
        kernel,
        out_shape=[jax.ShapeDtypeStruct(shape, dtype) for shape, dtype, _ in outs],
        in_specs=ins,
        out_specs=[spec for _, _, spec in outs],
        scratch_shapes=[pltpu.VMEM(shape, dtype) for shape, dtype in scratch]
        + [pltpu.SemaphoreType.DMA(n) for n in sems],
        compiler_params=pltpu.CompilerParams(
            collective_id=collective_id,
            has_side_effects=True,
            vmem_limit_bytes=60 * 1024 * 1024,
        ),
        cost_estimate=pl.CostEstimate(
            flops=flops, bytes_accessed=8_000_000, transcendentals=flops // 2000
        ),
    )(*operands)


def limits(pos, e0, e1, total):
    low = jnp.where(pos < e0, 0, jnp.where(pos < e1, e0, e1))
    end = jnp.where(pos < e0, e0, jnp.where(pos < e1, e1, total))
    reach = low + ((pos - low) // BLOCK + 1) * BLOCK
    return low, jnp.minimum(end, reach)


def query_positions(shape, axis, qb):
    r = lax.broadcasted_iota(jnp.int32, shape, axis)
    r = lax.rem(r, 512)
    return 512 * qb + 256 * lax.rem(r // 128, 2) + 128 * (r // 256) + lax.rem(r, 128)


def key_positions(shape, axis, kb, core):
    r = lax.broadcasted_iota(jnp.int32, shape, axis)
    return 512 * (kb + r // 256) + 256 * lax.rem(r // 128, 2) + 128 * core + lax.rem(r, 128)


def body(
    layer_input,
    attn_gain,
    w_query,
    key_weight,
    value_weight,
    w_output,
    query_gain,
    key_gain,
    ffn_gain,
    router,
    w_gate,
    w_up,
    w_down,
    routes,
    doc_lengths,
    cotangent,
):
    tokens, width = layer_input.shape
    lane = np.arange(128) % (HEAD_SIZE // 2)
    pace = jnp.asarray(ROPE_BASE ** (-2.0 * lane / HEAD_SIZE), F32)[None]
    (
        w_full, wo_full, both_inputs, q_group, kv_all, up_rows, raw, normed, ctx_wide, ctx_inv, turn, router_wide,
        pick, context, middle, mixed_in, gates, head_gain,
    ) = call(
        forward_kernel,
        0,
        [SM] + [VM] * 13,
        [
            ((2, width, 512), BF16, ANY),
            ((2, 2, width, width // 4), BF16, ANY),
            ((2, tokens, width), BF16, ANY),
            ((GROUP, 512, 128), BF16, ANY),
            ((NB, 256, 128), BF16, ANY),
            ((16, SLOTS, width), BF16, ANY),
            ((2, 2 * tokens, 512), F32, ANY),
            ((2 * tokens, width), BF16, ANY),
            ((GROUP, 512, 128), F32, ANY),
            ((GROUP, 512, 128), F32, ANY),
            ((2, 2 * tokens, 128), F32, ANY),
            ((128, width), F32, ANY),
            ((16, SLOTS, 2 * tokens), BF16, VM),
            ((tokens, width), BF16, VM),
            ((tokens, width), F32, VM),
            ((2 * tokens, width), BF16, VM),
            ((2 * tokens, 128), F32, VM),
            ((2, 128), F32, VM),
        ],
        [
            ((2 * tokens, width), BF16),
            ((2 * tokens, 128), F32),
            ((2, 2 * tokens, 512), F32),
            ((2 * tokens, width), BF16),
            ((GROUP, 512, 128), F32),
            ((GROUP, 512, 128), F32),
            ((2, 2 * tokens, 128), F32),
            ((128, width), F32),
            ((32, 512), BF16),
            ((2, width, 512), BF16),
            ((2, 2, width, width // 4), BF16),
            ((2, tokens, width), BF16),
            ((2 * tokens, width), BF16),
            ((2, 8, 128), jnp.int32),
            ((16, SLOTS, width), BF16),
            ((2 * tokens, 512), BF16),
            ((2 * tokens, 512), BF16),
            ((GROUP, 512, 128), BF16),
            ((NB, 256, 128), BF16),
            ((GROUP, 1024, 128), BF16),
            ((80, 512), BF16),
            ((GROUP, 80, 1024), F32),
            ((GROUP, 80, 1024), F32),
            ((GROUP, 80, 1024), F32),
            ((GROUP, 512, 128), BF16),
            ((tokens, width), BF16),
        ],
        [(1,)] * 4 + [(10,)] * 2 + [(16,)] * 2 + [(1,), (NB,)] + [(1,)] * 2 + [(8,)] * 2 + [(9,), (12,)],
        18_000_000_000,
        doc_lengths,
        w_query,
        key_weight,
        value_weight,
        w_output,
        layer_input,
        cotangent,
        routes.T,
        attn_gain[None],
        query_gain[None],
        key_gain[None],
        pace,
        ffn_gain[None],
        router.T,
    )
    wts, expert_out, ex_grads, middle_grad, attn_grad, ffn_part, router_part = call(
        experts_kernel,
        1,
        [VM] * 3 + [ANY] * 6 + [VM, ANY],
        [
            ((2, 16, SLOTS, 2 * tokens), BF16, ANY),
            ((16, SLOTS, width), BF16, ANY),
            ((3, 1024, 512), BF16, ANY),
            ((tokens, width), F32, VM),
            ((tokens, width), BF16, VM),
            ((1, width), F32, VM),
            ((NB, width), F32, VM),
        ],
        [
            ((16, SLOTS, width), BF16),
            ((1, width, 512), BF16),
            ((1, width, 512), BF16),
            ((1, 512, width), BF16),
            ((tokens, width), F32),
            ((tokens, width), BF16),
            ((128, width), F32),
            ((2, 16, SLOTS, 2 * tokens), BF16),
            ((16, SLOTS, width), BF16),
            ((3, 1024, 512), BF16),
            ((16, SLOTS, width), BF16),
            ((16, SLOTS, width), BF16),
            ((16, 8, 128), F32),
            ((16, 8, 128), F32),
            ((16, SLOTS, width), BF16),
            ((16, SLOTS, width), BF16),
            ((16, 8, 128), F32),
            ((16, 8, 128), F32),
            ((16, SLOTS, 512), BF16),
            ((16, SLOTS, 512), BF16),
            ((16, SLOTS, 512), BF16),
            ((16, SLOTS, width), BF16),
            ((2 * tokens, width), F32),
            ((16, 2 * tokens), F32),
            ((tokens, width), F32),
            ((16, tokens), F32),
            ((128, tokens), F32),
            ((16, SLOTS, 128), F32),
            ((16, SLOTS, 128), F32),
        ],
        [(1,), (ROUNDS,)] + [(1,)] * 6 + [(4,)] * 2 + [(4,), (7,), (3,)],
        12_000_000_000,
        mixed_in,
        gates,
        pick,
        up_rows,
        w_gate,
        w_up,
        w_down,
        middle,
        cotangent,
        ffn_gain[None],
        router_wide,
    )
    results = call(
        backward_kernel,
        2,
        [SM] + [VM] * 7 + [ANY] * 14,
        [
            ((tokens, width), BF16, VM),
            ((tokens, width), BF16, VM),
            ((32, 256), F32, VM),
            ((32, 128), F32, VM),
            ((32, 128), F32, VM),
            ((32, 256), F32, VM),
            ((1, width), F32, VM),
            ((1, HEAD_SIZE), F32, VM),
            ((1, HEAD_SIZE), F32, VM),
            ((1, width), F32, VM),
            ((NB, width), F32, VM),
            ((width, 512), BF16, ANY),
            ((width, 512), BF16, ANY),
            ((512, width), BF16, ANY),
        ],
        [
            ((GROUP, 512, 128), BF16),
            ((NB, 256, 128), BF16),
            ((GROUP, 512, 128), F32),
            ((GROUP, 512, 128), F32),
            ((2, width, 512), BF16),
            ((2, 2 * tokens, 512), F32),
            ((2 * tokens, width), BF16),
            ((2, tokens, width), BF16),
            ((2, 2 * tokens, 128), F32),
            ((2, 16, SLOTS, 2 * tokens), BF16),
            ((tokens, width), F32),
            ((tokens, width), F32),
            ((tokens, width), BF16),
            ((GROUP, 512, 128), BF16),
            ((GROUP, 1024, 128), BF16),
            ((GROUP, 1024, 128), BF16),
            ((GROUP, 1024, 128), BF16),
            ((GROUP, 64, 1024), BF16),
            ((GROUP, 64, 1024), BF16),
            ((GROUP, 64, 1024), BF16),
            ((GROUP, 1024, 128), F32),
            ((GROUP, 1024, 128), F32),
            ((GROUP, 512, 128), BF16),
            ((128, 512), F32),
            ((NB, 128, 256), BF16),
            ((GROUP, 1024, 128), F32),
            ((2, 1024, 256), BF16),
            ((2, 1024, 256), BF16),
            ((2, 1024, 256), BF16),
            ((3, 512, 512), BF16),
            ((3, 512, 512), BF16),
            ((3, 512, 512), BF16),
            ((2, 2 * tokens, 512), BF16),
            ((NB, 128, 256), BF16),
            ((16, SLOTS, width), BF16),
            ((2 * NB, 32, 256), BF16),
            ((2, 2 * tokens, 512), BF16),
            ((NB, 32, 512), BF16),
            ((NB, 32, 512), BF16),
            ((NB, 32, 512), BF16),
            ((NB, 32, 512), BF16),
            ((2, tokens, width), F32),
            ((tokens, width), BF16),
            ((tokens, width), BF16),
            ((2, tokens, width), F32),
            ((tokens, width), F32),
            ((24, 128), F32),
            ((4, 24, 128), F32),
            ((NB, 24, 128), F32),
            ((NB, 8, 128), F32),
            ((4, 8, 128), F32),
            ((8, 128), F32),
            ((NB, width), F32),
        ],
        [(1,)] * 8 + [(16,)] * 2 + [(1,)] * 6 + [(4,)] * 2 + [(1,)] * 2 + [(10,)] * 2 + [(6,), (12,)] + [(4,)] * 3,
        45_000_000_000,
        doc_lengths,
        attn_grad,
        context,
        wo_full,
        head_gain,
        attn_gain[None],
        ffn_part,
        router_part,
        expert_out,
        ex_grads,
        q_group,
        kv_all,
        ctx_wide,
        ctx_inv,
        w_full,
        raw,
        normed,
        both_inputs,
        turn,
        wts,
        middle,
        middle_grad,
    )
    results = finished(results)
    return (
        *results[:2],
        results[6][0],
        *results[2:6],
        *[row[0] for row in results[7:10]],
        results[10].T,
        *results[11:],
    )


def solution(mesh):
    everyone = P(("blk", "head"), None)
    both = P("blk", "head")
    expert = P("blk", None, None)
    return jax.shard_map(
        body,
        mesh=mesh,
        in_specs=(everyone, P(), both, both, both, both, P(), P(), P(), P())
        + (expert, expert, expert, everyone, P(), everyone),
        out_specs=(everyone, everyone, P(), both, both, both, both, P(), P(), P(), P())
        + (expert, expert, expert),
        check_vma=False,
    )
```

```python
import jax
import jax.numpy as jnp
import numpy as np
from jax import lax
from jax.experimental import pallas as pl
from jax.experimental.pallas import tpu as pltpu
from jax.sharding import PartitionSpec as P

HEAD_SIZE = 64
TOPK = 8
BLOCK = 256
EPSILON = 1e-06
ROPE_BASE = 10000.0
PRECISE = lax.Precision.HIGHEST
SCALE = HEAD_SIZE ** (-0.5)

NB = 32
ROUNDS = 5
SLOTS = 80
GROUP = 4
MESH_ID = pl.DeviceIdType.MESH
F32 = jnp.float32
BF16 = jnp.bfloat16
NT = (((1,), (1,)), ((), ()))
NN = (((1,), (0,)), ((), ()))
TN = (((0,), (0,)), ((), ()))


def place():
    b = lax.axis_index("blk")
    h = lax.axis_index("head")
    y = b // 8
    r = lax.rem(b, 8)
    m = jnp.where(lax.rem(y, 2) == 0, r, 7 - r)
    return b, h // 2, lax.rem(h, 2), y, m


def member(m, j):
    return 8 * j + m + lax.rem(j, 2) * (7 - 2 * m)


def times(start, n, body):
    def step(i, carry):
        body(i)
        return carry

    lax.fori_loop(start, n, step, 0)


def signal(sem, blk, head):
    pl.semaphore_signal(sem, inc=1, device_id=(blk, head), device_id_type=MESH_ID)


def rows(start, size):
    return pl.ds(pl.multiple_of(start, size), size)


def to(src, dst, send, recv, blk, head):
    return pltpu.make_async_remote_copy(
        src, dst, send, recv, device_id=(blk, head), device_id_type=MESH_ID
    )


def settle(sem, part):
    pltpu.make_async_copy(part, part, sem).wait()


def settle_rows(sem, blocks, c):
    pl.when(c == 0)(lambda: settle(sem, blocks.at[pl.ds(0, 15)]))
    pl.when(c == 1)(lambda: settle(sem, blocks))


def greet_all(bar, b, xl, c, y, m):
    h = 2 * xl + c
    times(1, NB, lambda d: signal(bar, lax.rem(b + d, NB), h))
    times(0, NB, lambda d: signal(bar, lax.rem(b + d, NB), 2 * (1 - xl) + c))
    for dj in range(GROUP):
        j = member(m, lax.rem(y + dj, GROUP))
        signal(bar, j, 2 * xl + 1 - c)
    pl.semaphore_wait(bar, 2 * NB - 1 + GROUP)


def pad_queries(both, qp, i):
    left = lax.broadcasted_iota(jnp.int32, (512, 128), 1) < 64
    qp[i, 0:512] = jnp.where(left, both, 0.0).astype(BF16)
    qp[i, 512:1024] = jnp.where(left, pltpu.roll(both, 64, 1), 0.0).astype(BF16)


def on_pair(p, m, inside, edge):
    def each(i):
        qb = member(m, i)
        whole = (p >= 1) & (2 * p + 1 <= qb - 1)
        pl.when(whole)(lambda: inside(i))
        pl.when(jnp.logical_not(whole) & (2 * p <= qb + 1))(lambda: edge(i, qb))

    times(0, GROUP, each)


def by_head(values, left):
    one = jnp.sum(jnp.where(left, values, 0.0), axis=1, keepdims=True) / HEAD_SIZE
    two = jnp.sum(jnp.where(left, 0.0, values), axis=1, keepdims=True) / HEAD_SIZE
    return jnp.where(left, one, two)


def swapped(values, first):
    return jnp.where(first, pltpu.roll(values, 96, 1), pltpu.roll(values, 32, 1))


def row_scale(values):
    return lax.rsqrt(jnp.mean(values * values, axis=1, keepdims=True) + EPSILON)


def lanes_of(shape):
    lane = lax.broadcasted_iota(jnp.int32, shape, 1)
    return lane < 64, lax.rem(lane, 64) < 32


def slab(j):
    return j // 2, slice(128 * (j % 2), 128 * (j % 2) + 128), slice(
        256 + 128 * (j % 2), 384 + 128 * (j % 2)
    )


def forward_kernel(
    lengths, wq, wk, wvl, wo, li, cot, routes_t, attn_gain, q_gain, k_gain, pace, ffn_gain, router_t,
    w_out, wo_out, li_out, q_out, kv_out, c_out, raw_out, normed_out, wide_out, inv_out, turn_out, router_out,
    pick, ctx_out, mid_out, tok_out, gates_out, head_gain,
    tok, gt, raw, normed, wide_all, inv_all, turn, router,
    ws, wv, wov, li2, cot2, rt, xs, qs, kvst, qg, kvs, qp, vt, acc, accm, peer, ctx, ctx_in,
    sw, rw, so, ro, sx, rx, s1, r1, s2, r2, s5, r5, s7, r7, ls, lk,
):
    b, xl, c, y, m = place()
    h = 2 * xl + c
    sib = 2 * xl + 1 - c
    over = 2 * (1 - xl) + c
    odd = lax.rem(b + c, 2)
    e0, e1, total = lengths[0], lengths[0] + lengths[1], 512 * NB
    pairs = jnp.concatenate([wk[...].astype(F32), wvl[...].astype(F32)], axis=1)
    even = jnp.concatenate([pairs[:, 0:64], pairs[:, 128:192]], axis=1)
    other = jnp.concatenate([pairs[:, 64:128], pairs[:, 192:256]], axis=1)
    ws[:, 0:256] = wq[...]
    ws[:, 256:384] = even.astype(BF16)
    ws[:, 384:512] = other.astype(BF16)
    greet_all(pltpu.get_barrier_semaphore(), b, xl, c, y, m)

    def w_first(d):
        part = wv.at[c, rows(b * 32, 32)]
        return to(ws, part, sw.at[0], rw.at[0], lax.rem(b + d, NB), h)

    def wo_first(d):
        part = wov.at[0, c, rows(b * 32, 32)]
        return to(wo, part, so.at[0], ro.at[0], lax.rem(b + d, NB), h)

    keeps = []

    def keep(part, out):
        item = pltpu.make_async_copy(part, out, lk.at[len(keeps)])
        item.start()
        keeps.append(item)

    near = [
        to(routes_t, rt.at[c], sx.at[0], rx.at[0], b, sib),
        to(cot, cot2.at[rows(c * 128, 128)], sx.at[1], rx.at[1], b, sib),
        to(li, li2.at[xl], sx.at[2], rx.at[2], b, over),
    ]
    for item in near:
        item.start()
    times(1, NB, lambda d: w_first(d).start())
    wv[c, rows(b * 32, 32)] = ws[...]
    li2[xl] = li[...]
    cot2[rows(c * 128, 128)] = cot[...]
    rt[c] = routes_t[...]

    near[0].wait()
    both_routes = jnp.concatenate([rt[0], rt[1]], axis=1)
    mine = 2 * lax.broadcasted_iota(jnp.int32, (16, 256), 0) + odd
    chosen = jnp.zeros((16, 256), F32)
    for k in range(TOPK):
        chosen = jnp.where(both_routes[k : k + 1] == mine, 1.0, chosen)
    earlier = lax.broadcasted_iota(jnp.int32, (256, 256), 0) < lax.broadcasted_iota(
        jnp.int32, (256, 256), 1
    )
    rank = jnp.dot(
        chosen.astype(BF16), jnp.where(earlier, 1.0, 0.0).astype(BF16), preferred_element_type=F32
    )
    slot = lax.broadcasted_iota(jnp.int32, (80, 256), 0).astype(F32)
    for k in range(16):
        at = jnp.where(rank[k : k + 1] == slot, chosen[k : k + 1], 0.0)
        pick[k] = at.astype(BF16)
    near[1].wait()
    c_piece = rows_out(xs, c_out, b, xl, c, lambda r: s5.at[0], lambda r: r5.at[0])
    c_same = pltpu.make_async_copy(xs.at[b // 2], c_out.at[15], ls.at[3])

    def fetch(d):
        k = stride(b, d)
        xs[k] = jnp.dot(pick[k], cot2[...], preferred_element_type=F32).astype(BF16)

    times(1, 17, fetch)
    pl.when(c == 0)(c_same.start)
    send_pieces(c_piece, 0, 32, c)

    near[2].wait()
    keep(li2, li_out)
    source2 = li2[...].reshape(256, 1024).astype(F32)
    normed[...] = (source2 * row_scale(source2) * attn_gain[...]).astype(BF16)

    keep(normed, normed_out)
    settle(rw.at[0], wv.at[c, rows(0, 992)])
    w_sib = to(wv.at[c], wv.at[c], sx.at[3], rx.at[3], b, sib)
    w_sib.start()
    wov[0, c, rows(b * 32, 32)] = wo[...]
    left, first = lanes_of((256, 128))
    t = lax.broadcasted_iota(jnp.int32, (256, 128), 0)
    pos = 512 * b + 256 * (t // 128) + 128 * c + lax.rem(t, 128)
    opening = jnp.where(pos < e0, 0, jnp.where(pos < e1, e0, e1))
    angles = (pos - opening).astype(F32) * pace[...]
    turn[0] = jnp.cos(angles)
    sine = jnp.sin(angles)
    turn[1] = jnp.where(first, -sine, sine)
    head_gain[0:1] = jnp.concatenate([q_gain[...], q_gain[...]], axis=1)
    head_gain[1:2] = jnp.concatenate([k_gain[...], jnp.ones((1, 64), F32)], axis=1)
    router[...] = jnp.zeros_like(router)
    router[0:NB] = router_t[...]
    keep(turn, turn_out)
    keep(router, router_out)
    w_sib.wait()
    keep(wv, w_out)
    for i in range(2):
        raw[i] = jnp.dot(normed[...], wv[i], preferred_element_type=F32)
    for j in range(GROUP):
        i, q_cols, kv_cols = slab(j)
        u = raw[i, :, q_cols]
        n = u * lax.rsqrt(by_head(u * u, left) + EPSILON) * head_gain[0:1]
        turned = n * turn[0] + swapped(n, first) * turn[1]
        qs[j] = (turned.astype(BF16).astype(F32) * SCALE).astype(BF16)
        u = raw[i, :, kv_cols]
        n = u * lax.rsqrt(by_head(u * u, left) + EPSILON) * head_gain[1:2]
        turned = n * turn[0] + swapped(n, first) * turn[1]
        kvst[j] = jnp.where(left, turned, u).astype(BF16)

    def q_piece(part, dj, dc):
        j = lax.rem(y + dj, GROUP)
        k = 8 * part + 2 * dj + dc
        src, dst = qs.at[j, rows(part * 128, 128)], qg.at[y, rows(c * 256 + part * 128, 128)]
        if dj + dc == 0:
            return pltpu.make_async_copy(src, dst, s1.at[k])
        return to(src, dst, s1.at[k], r1.at[k], member(m, j), 2 * xl + lax.rem(c + dc, 2))

    q_pieces = [q_piece(n, dj, dc) for n in range(2) for dj in range(GROUP) for dc in range(2)]

    def kv_piece(i):
        d, half = lax.rem(i, NB), rows(128 * (i // NB), 128)
        peer_b = lax.rem(b + d, NB)
        return to(kvst.at[peer_b // 8, half], kvs.at[b, half], s2.at[0], r2.at[d], peer_b, h)

    for item in q_pieces:
        item.start()
    kv_own = pltpu.make_async_copy(kvst.at[y], kvs.at[b], ls.at[1])
    kv_own.start()
    times(1, NB, lambda d: kv_piece(d).start())
    times(NB + 1, 2 * NB, lambda i: kv_piece(i).start())
    for item in q_pieces:
        item.wait()
    kv_own.wait()
    keep(qg, q_out)
    keep(raw, raw_out)
    for i in range(GROUP):
        pad_queries(qg[i].astype(F32), qp, i)
    acc[...] = jnp.zeros_like(acc)
    accm[...] = jnp.zeros_like(accm)
    vt[64:80] = jnp.ones((16, 512), BF16)

    def pair(dp):
        p = lax.rem(b // 2 + 16 - dp, 16)
        send_pieces(c_piece, 32 + 3 * dp, 35 + 3 * dp, c)
        times(jnp.minimum(16 * dp, NB) + (dp == 0), jnp.minimum(16 * dp + 16, NB), lambda d: wo_first(d).start())
        for kb in (2 * p, 2 * p + 1):

            @pl.when(kb != b)
            def _():
                settle(r2.at[lax.rem(b + NB - kb, NB)], kvs.at[kb])

        vt[0:64] = (
            kvs[pl.ds(2 * p, 2)].reshape(512, 128).astype(F32).T[64:128].astype(BF16)
        )

        def scores(i):
            keys = kvs[pl.ds(2 * p, 2)].reshape(512, 128)
            return jnp.exp(lax.dot_general(keys, qp[i], NT, preferred_element_type=F32))

        def inside(i):
            acc[i] += jnp.dot(vt[...], scores(i).astype(BF16), preferred_element_type=F32)

        def edge(i, qb):
            low, high = limits(query_positions((1, 1024), 1, qb), e0, e1, total)
            kpos = key_positions((512, 1), 0, 2 * p, c)
            expo = jnp.where((kpos >= low) & (kpos < high), scores(i), 0.0)
            accm[i] += jnp.dot(vt[...], expo.astype(BF16), preferred_element_type=F32)

        on_pair(p, m, inside, edge)

    times(0, 10, pair)
    settle(ro.at[0], wov.at[0, c, rows(0, 992)])
    wo_moves = [
        to(wov.at[0, c], wov.at[0, c], sx.at[6], rx.at[6], b, sib),
        to(wov.at[0, c], wov.at[1, c], sx.at[4], rx.at[4], b, over),
    ]
    for item in wo_moves:
        item.start()
    times(10, 16, pair)
    for i in range(GROUP):
        pos = query_positions((1, 1024), 1, member(m, i))
        acc[i] = accm[i] + jnp.where((pos >= e0) & (pos < e1), acc[i], 0.0)
    swap = to(acc, peer, sx.at[5], rx.at[5], b, sib)
    swap.start()
    keep(kvs, kv_out)
    for item in wo_moves:
        item.wait()
    far_sib = to(wov.at[1, c], wov.at[1, c], sx.at[7], rx.at[7], b, sib)
    far_sib.start()
    swap.wait()

    def ctx_piece(dj, dx):
        j = lax.rem(y + dj, GROUP)
        x2 = lax.rem(xl + dx, 2)
        src, dst = ctx.at[j, rows(c * 256 + x2 * 128, 128)], ctx_in.at[4 * xl + y]
        k = 2 * dj + dx
        if k == 0:
            return pltpu.make_async_copy(src, dst, ls.at[6])
        return to(src, dst, s7.at[k], r7.at[k], member(m, j), 2 * x2 + c)

    ctx_pieces = [ctx_piece(dj, dx) for dj in range(GROUP) for dx in range(2)]
    for i in range(GROUP):
        both = acc[i] + peer[i]
        inverse = 1.0 / both[64:65]
        wide = both[0:64] * inverse
        flat = jnp.concatenate([wide[:, 0:512], wide[:, 512:1024]], axis=0).T
        wide_all[i] = flat
        ctx[i] = flat.astype(BF16)
        spread = jnp.broadcast_to(inverse, (64, 1024))
        inv_all[i] = jnp.concatenate([spread[:, 0:512], spread[:, 512:1024]], axis=0).T
    for item in ctx_pieces:
        item.start()
    keep(wide_all, wide_out)
    keep(inv_all, inv_out)
    far_sib.wait()
    keep(wov, wo_out)
    for item in ctx_pieces:
        item.wait()

    context = jnp.concatenate([ctx_in[n] for n in range(2 * GROUP)], axis=1)
    ctx_out[...] = context
    for i in range(2):
        for x2, part in ((xl, wov[0, i]), (1 - xl, wov[1, i])):
            cols = rows(512 * x2 + 256 * i, 256)
            mid_out[:, cols] = li[:, cols].astype(F32) + jnp.dot(
                context, part, preferred_element_type=F32
            )
    middle = mid_out[...]
    mixed = (middle * row_scale(middle) * ffn_gain[...]).astype(BF16)
    own = rows(c * 128, 128)
    tok[own] = mixed
    tok_swap = to(tok.at[own], tok.at[own], sx.at[8], rx.at[8], b, sib)
    tok_swap.start()
    logits = lax.dot_general(
        mixed.astype(F32), router[...], NT, preferred_element_type=F32, precision=PRECISE
    )
    expert = lax.broadcasted_iota(jnp.int32, (128, 128), 0)
    hit = jnp.zeros((128, 128), F32)
    for k in range(TOPK):
        hit = jnp.where(routes_t[k : k + 1] == expert, 1.0, hit)
    hit = hit.T
    top = jnp.max(jnp.where(hit > 0.0, logits, -1e30), axis=1, keepdims=True)
    weight = jnp.where(hit > 0.0, jnp.exp(logits - top), 0.0)
    gt[own] = weight / jnp.sum(weight, axis=1, keepdims=True)
    gates_swap = to(gt.at[own], gt.at[own], sx.at[9], rx.at[9], b, sib)
    gates_swap.start()

    settle(sw.at[0], wv.at[0, rows(0, 992)])
    settle(so.at[0], wov.at[0, 0, rows(0, 992)])
    settle(s2.at[0], kvs.at[pl.ds(0, NB - 1)])
    settle_rows(s5.at[0], xs, c)
    settle_rows(r5.at[0], xs, c)
    pl.when(c == 0)(c_same.wait)
    tok_swap.wait()
    gates_swap.wait()
    tok_out[...] = tok[...]
    gates_out[...] = gt[...]
    for item in keeps:
        item.wait()


def row_peer(b, xl, c, k):
    e = 2 * k + lax.rem(b + c, 2)
    apart = lax.rem(b // 4 + e // 4, 2)
    return e, 2 * (xl + apart - 2 * xl * apart) + c


def stride(b, d):
    return lax.rem(b // 2 + 5 * d, 16)


def rows_out(src, dst, b, xl, c, send, recv):
    def piece(d, r):
        k = stride(b, d)
        e, head = row_peer(b, xl, c, k)
        if src.shape[1] < 16:
            return to(src.at[k], dst.at[d - 1], send(r), recv(r), e, head)
        part = rows(16 * r, 16)
        return to(src.at[k, part], dst.at[d - 1, part], send(r), recv(r), e, head)

    return piece


def rows_home(src, dst, b, xl, c, send, recv):
    def piece(d, r):
        e, head = row_peer(b, xl, c, stride(b, 16 - d))
        if src.shape[1] < 16:
            return to(src.at[d - 1], dst.at[b // 2], send(r), recv(r), e, head)
        part = rows(16 * r, 16)
        return to(src.at[d - 1, part], dst.at[b // 2, part], send(r), recv(r), e, head)

    return piece


def send_pieces(piece, start, stop, c):
    def one(i):
        d = lax.rem(i, 16) + 1
        pl.when((d < 16) | (c == 1))(lambda: piece(d, i // 16).start())

    times(start, stop, one)


def start_tiles(piece, d, c, local):
    pl.when((d < 16) | (c == 1))(lambda: piece(d, 0).start())
    pl.when((d == 16) & (c == 0))(local.start)


def experts_kernel(
    tok, gt, pick, up_hbm, gate_hbm, upw_hbm, down_hbm, middle_hbm, cot_hbm, ffn_gain, router_hbm,
    wts_hbm, eo_hbm, ex_hbm, grad_out, low_out, small_out, router_out,
    up_rows, gate_w, up_w, down_w, middle_ref, cot, router, wts_out, eo_out, ex_out,
    xs, xl_rows, gs, gl, rs, rl, ggs, ggl, hid, gb, ub, og, mgs, ggt, mg_in, gg_in, gg_all, gcol, ggcol,
    s1, r1, s2, r2, s3, r3, s4, r4, sx, rx, ls, li, lo,
):
    b, xl, c, _, _ = place()
    h = 2 * xl + c
    sib = 2 * xl + 1 - c
    odd = lax.rem(b + c, 2)
    brought = [
        pltpu.make_async_copy(src, dst, li.at[n])
        for n, (src, dst) in enumerate(
            (
                (gate_hbm, gate_w),
                (upw_hbm, up_w),
                (down_hbm, down_w),
                (up_hbm, up_rows),
                (middle_hbm, middle_ref),
                (cot_hbm, cot),
                (router_hbm, router),
            )
        )
    ]
    for item in brought:
        item.start()
    bar = pltpu.get_barrier_semaphore()

    def greet(d):
        e, head = row_peer(b, xl, c, stride(b, d))
        signal(bar, e, head)

    times(1, 16, greet)
    signal(bar, b, sib)
    pl.when(c == 1)(lambda: greet(0))
    pl.semaphore_wait(bar, 16 + c)
    x_piece = rows_out(xs, xl_rows, b, xl, c, lambda r: s1.at[0], lambda r: r1.at[r])
    x_same = pltpu.make_async_copy(xs.at[b // 2], xl_rows.at[15], ls.at[0])

    def fetch(r):
        part = rows(16 * r, 16)
        xs[:, part] = (
            jnp.dot(pick[:, part].reshape(256, 256), tok[...], preferred_element_type=F32)
            .astype(BF16)
            .reshape(16, 16, 1024)
        )
        send_pieces(x_piece, 16 * r, 16 * r + 16, c)

    times(0, 1, fetch)
    high = gt[...].astype(BF16)
    rest = gt[...] - high.astype(F32)
    mid = rest.astype(BF16)
    low = (rest - mid.astype(F32)).astype(BF16)
    g_piece = rows_out(gs, gl, b, xl, c, lambda r: s2.at[0], lambda r: r2.at[0])
    g_same = pltpu.make_async_copy(gs.at[b // 2], gl.at[15], ls.at[1])

    def as_row(column):
        wide = jnp.concatenate([jnp.broadcast_to(column, (80, 128)), jnp.zeros((48, 128), F32)])
        return wide.T[0:8]

    spread = jnp.dot(
        pick[...].reshape(1280, 256),
        jnp.concatenate([high, mid, low], axis=1),
        preferred_element_type=F32,
    )
    spread = spread[:, 0:128] + spread[:, 128:256] + spread[:, 256:384]
    lane = lax.broadcasted_iota(jnp.int32, (1280, 128), 1)
    expert = 2 * (lax.broadcasted_iota(jnp.int32, (1280, 128), 0) // 80) + odd
    column = jnp.sum(jnp.where(lane == expert, spread, 0.0), axis=1, keepdims=True)
    for k in range(16):
        gs[k] = as_row(column[80 * k : 80 * k + 80])
    times(1, 17, lambda d: start_tiles(g_piece, d, c, g_same))
    times(1, ROUNDS, fetch)
    pl.when(c == 0)(x_same.start)
    weights = pick[...].reshape(1280, 256).astype(F32) * column
    weights_high = weights.astype(BF16)
    wts_out[0] = weights_high.reshape(16, 80, 256)
    wts_out[1] = (weights - weights_high.astype(F32)).astype(BF16).reshape(16, 80, 256)
    wts_keep = pltpu.make_async_copy(wts_out, wts_hbm, lo.at[0])
    wts_keep.start()
    for item in brought:
        item.wait()
    home = rows_home(rs, rl, b, xl, c, lambda r: s3.at[0], lambda r: r3.at[0])
    home_same = pltpu.make_async_copy(rs.at[15], rl.at[b // 2], ls.at[2])
    gg_home = rows_home(ggs, ggl, b, xl, c, lambda r: s4.at[0], lambda r: r4.at[0])
    gg_same = pltpu.make_async_copy(ggs.at[15], ggl.at[b // 2], ls.at[3])

    pl.when(c == 0)(x_same.wait)

    def group(r):
        part = rows(16 * r, 16)
        pl.when(c == 0)(lambda: settle(r1.at[r], xl_rows.at[pl.ds(0, 15), part]))
        pl.when(c == 1)(lambda: settle(r1.at[r], xl_rows.at[:, part]))
        x = xl_rows[:, part].reshape(256, 1024)
        u = up_rows[:, part].reshape(256, 1024).astype(F32)
        gate_pre = jnp.dot(x, gate_w[0], preferred_element_type=F32)
        up_pre = jnp.dot(x, up_w[0], preferred_element_type=F32)
        sig = jax.nn.sigmoid(gate_pre)
        act = gate_pre * sig
        hidden = (act * up_pre).astype(BF16)
        out = jnp.dot(hidden, down_w[0], preferred_element_type=F32).astype(BF16)
        eo_out[:, part] = out.reshape(16, 16, 1024)
        gate_grad = jnp.sum(u * out.astype(F32), axis=1, keepdims=True)
        ggcol[:, part] = jnp.broadcast_to(gate_grad, (256, 128)).reshape(16, 16, 128)
        @pl.when(r == 0)
        def _():
            settle_rows(r2.at[0], gl, c)
            pl.when(c == 0)(g_same.wait)
            for n in range(16):
                row = jnp.concatenate([gl[n], jnp.zeros((120, 128), F32)])
                gcol[n] = jnp.broadcast_to(row.T[0:80, 0:1], (80, 128))

        out_grad = (gcol[:, part].reshape(256, 128)[:, 0:1] * u).astype(BF16)
        hidden_grad = lax.dot_general(out_grad, down_w[0], NT, preferred_element_type=F32)
        gate_back = (hidden_grad * up_pre * sig * (1.0 + gate_pre * (1.0 - sig))).astype(BF16)
        up_back = (hidden_grad * act).astype(BF16)
        back = lax.dot_general(
            gate_back, gate_w[0], NT, preferred_element_type=F32
        ) + lax.dot_general(up_back, up_w[0], NT, preferred_element_type=F32)
        rs[:, part] = back.astype(BF16).reshape(16, 16, 1024)
        send_pieces(home, 16 * r, 16 * r + 16, c)
        hid[:, part] = hidden.reshape(16, 16, 512)
        gb[:, part] = gate_back.reshape(16, 16, 512)
        ub[:, part] = up_back.reshape(16, 16, 512)
        og[:, part] = out_grad.reshape(16, 16, 1024)

    times(0, ROUNDS, group)
    pl.when(c == 0)(home_same.start)
    for n in range(16):
        ggs[n] = as_row(ggcol[n, :, 0:1])
        start_tiles(gg_home, n + 1, c, gg_same)
    eo_keep = pltpu.make_async_copy(eo_out, eo_hbm, lo.at[1])
    eo_keep.start()
    for j in range(4):
        part = slice(256 * j, 256 * j + 256)
        x_turned = xl_rows[:, :, part].reshape(1280, 256)
        for n, grads in ((0, gb), (1, ub)):
            ex_out[n, part] = lax.dot_general(
                x_turned, grads[...].reshape(1280, 512), TN, preferred_element_type=F32
            ).astype(BF16)
        half = slice(512 * (j // 2), 512 * (j // 2) + 512)
        place_at = 512 * (j % 2) + 256 * (j // 2)
        turned = hid[:, :, 256 * (j % 2) : 256 * (j % 2) + 256].reshape(1280, 256)
        ex_out[2, place_at : place_at + 256] = lax.dot_general(
            turned, og[:, :, half].reshape(1280, 512), TN, preferred_element_type=F32
        ).astype(BF16)

    ex_keep = pltpu.make_async_copy(ex_out, ex_hbm, lo.at[2])
    ex_keep.start()
    settle_rows(r4.at[0], ggl, c)
    pl.when(c == 0)(gg_same.wait)
    for k in range(16):
        column = jnp.concatenate([ggl[k], jnp.zeros((120, 128), F32)]).T[0:80, 0:1]
        ggt[pl.ds(k, 1)] = jnp.sum(pick[k].astype(F32) * column, axis=0, keepdims=True)
    settle_rows(r3.at[0], rl, c)
    pl.when(c == 0)(home_same.wait)
    mgs[...] = lax.dot_general(
        pick[...].reshape(1280, 256), rl[...].reshape(1280, 1024), TN, preferred_element_type=F32
    )
    away = rows((1 - c) * 128, 128)
    own = rows(c * 128, 128)
    back_near = [
        to(ggt.at[:, away], gg_in, sx.at[3], rx.at[3], b, sib),
        to(mgs.at[away], mg_in, sx.at[2], rx.at[2], b, sib),
    ]
    for item in back_near:
        item.start()
    settle_rows(s1.at[0], xs, c)
    settle_rows(s2.at[0], gs, c)
    settle_rows(s3.at[0], rs, c)
    settle_rows(s4.at[0], ggs, c)
    back_near[0].wait()

    gg_all[...] = jnp.zeros_like(gg_all)
    for k in range(16):
        gg_all[pl.ds(2 * k + odd, 1)] = ggt[pl.ds(k, 1), own]
        gg_all[pl.ds(2 * k + 1 - odd, 1)] = gg_in[pl.ds(k, 1)]
    gate_grad = gg_all[...].T
    own_gates = gt[own]
    logit_grad = own_gates * (
        gate_grad - jnp.sum(own_gates * gate_grad, axis=1, keepdims=True)
    )
    router_out[...] = lax.dot_general(
        logit_grad, tok[own].astype(F32), TN, preferred_element_type=F32, precision=PRECISE
    )[0:NB]
    routed = jnp.dot(
        logit_grad, router[...], preferred_element_type=F32, precision=PRECISE
    )
    back_near[1].wait()
    mixed_grad = mgs[own] + mg_in[...] + routed
    middle = middle_ref[...]
    scale = row_scale(middle)
    unit = middle * scale
    small_out[...] = jnp.sum(mixed_grad * unit, axis=0, keepdims=True)
    inner = mixed_grad * ffn_gain[...]
    grad = cot[...].astype(F32) + scale * (
        inner - unit * jnp.mean(inner * unit, axis=1, keepdims=True)
    )
    grad_out[...] = grad
    low_out[...] = grad.astype(BF16)
    for item in (wts_keep, eo_keep, ex_keep):
        item.wait()


def backward_kernel(
    lengths, attn_grad, context, wo, head_gain, attn_gain, ffn_part, router_part, eo, ex,
    q_hbm, kv_hbm, wide_hbm, inv_hbm, wv_hbm, raw_hbm, normed_hbm, li_hbm, turn_hbm, wts_hbm, mid_hbm, grad_hbm,
    out, in_grad, wq_grad, wk_grad, wv_grad, wo_grad, attn_small, q_small, k_small, ffn_small, router_grad,
    exg_out, exu_out, exd_out,
    q_ref, kv_ref, wide_ref, inv_ref, wv, raw, normed, li2, turn, wts, middle, grad,
    cg, cgs, qp, gp, gi, qt, gt, gti, dt, di, dqs, dkvt, stage, dq_acc,
    wo_other, wo_in, wo_sum, ex_in, ex_sum, ex_cross, dq, dkv, home, wo_parts,
    low, w_other, w_in, w_sum, w_land, back, back_low, back_in, mix, mix_in, small, four, many,
    r_land, r_four, r_tot, router_out,
    s1, r1, s2, r2, s3, r3, s4, r4, s5, r5, s6, r6, s7, r7, s8, r8, s9, r9, sa, ra, sx, rx, ls, li, se, re, le,
):
    b, xl, c, y, m = place()
    h = 2 * xl + c
    sib = 2 * xl + 1 - c
    over = 2 * (1 - xl) + c
    e0, e1, total = lengths[0], lengths[0] + lengths[1], 512 * NB
    brought = [
        pltpu.make_async_copy(src, dst, li.at[n])
        for n, (src, dst) in enumerate(
            (
                (q_hbm, q_ref),
                (kv_hbm, kv_ref),
                (wide_hbm, wide_ref),
                (inv_hbm, inv_ref),
                (wv_hbm, wv),
                (raw_hbm, raw),
                (normed_hbm, normed),
                (li_hbm, li2),
                (turn_hbm, turn),
                (wts_hbm, wts),
                (mid_hbm, middle),
                (grad_hbm, grad),
            )
        )
    ]
    for item in brought:
        item.start()
    bar = pltpu.get_barrier_semaphore()
    for dj in range(GROUP):
        j = member(m, lax.rem(y + dj, GROUP))
        signal(bar, j, 2 * (1 - xl) + 1 - c)
        signal(bar, j, 2 * xl + 1 - c)
    times(1, NB, lambda d: signal(bar, lax.rem(b + d, NB), h))
    times(0, NB, lambda d: signal(bar, lax.rem(b + d, NB), over))
    pl.semaphore_wait(bar, 2 * NB - 1 + 2 * GROUP)

    ex_swap = to(ex.at[:, rows((1 - c) * 512, 512)], ex_in, sx.at[1], rx.at[1], b, sib)
    ex_swap.start()
    ex_own = pltpu.make_async_copy(ex.at[:, rows(c * 512, 512)], ex_sum, ls.at[1])
    ex_own.start()
    turned_back = jnp.zeros((128, 1024), F32)
    for i in range(2):
        for x2, part in ((xl, wo[0, i]), (1 - xl, wo[1, i])):
            turned_back = turned_back + lax.dot_general(
                attn_grad[:, rows(512 * x2 + 256 * i, 256)], part, NT, preferred_element_type=F32
            )
    for n in range(2 * GROUP):
        cg[n] = turned_back[:, 128 * n : 128 * n + 128].astype(BF16)
    turns = [(dj, dx, dc) for dj in range(GROUP) for dx in range(2) for dc in range(2)]
    cg_pieces = []
    for k, (dj, dx, dc) in enumerate(turns):
        j = lax.rem(y + dj, GROUP)
        x2 = lax.rem(xl + dx, 2)
        src, dst = cg.at[4 * x2 + j], cgs.at[y, rows(c * 256 + xl * 128, 128)]
        if k == 0:
            cg_pieces.append(pltpu.make_async_copy(src, dst, ls.at[0]))
        else:
            head = 2 * x2 + lax.rem(c + dc, 2)
            cg_pieces.append(to(src, dst, s1.at[0], r1.at[0], member(m, j), head))
    for item in cg_pieces:
        item.start()

    def tile(n):
        return router_part.at[rows(8 * (n // 8), 8), rows(128 * lax.rem(n, 8), 128)]

    def router_first(d):
        to_b = lax.rem(b + d, NB)
        return to(tile(to_b), r_land.at[b], s8.at[0], r8.at[0], to_b, h)

    times(1, NB, lambda d: router_first(d).start())
    r_land[b] = router_part[rows(8 * (b // 8), 8), rows(128 * lax.rem(b, 8), 128)]

    eo_piece = rows_home(eo, home, b, xl, c, lambda r: s2.at[0], lambda r: r2.at[0])
    eo_same = pltpu.make_async_copy(eo.at[15], home.at[b // 2], ls.at[2])
    pl.when(c == 0)(eo_same.start)
    send_pieces(eo_piece, 0, 32, c)

    def out_part(x2, core):
        cols = pl.ds(pl.multiple_of(512 * x2 + 256 * core, 256), 256)
        return lax.dot_general(
            context[...], attn_grad[:, cols], TN, preferred_element_type=F32
        )

    for x2 in range(2):
        wo_other[x2] = out_part(x2, 1 - c).astype(BF16)
    wo_swap = to(wo_other, wo_in, sx.at[0], rx.at[0], b, sib)
    wo_swap.start()
    brought[0].wait()
    for i in range(GROUP):
        both = q_ref[i].astype(F32)
        pad_queries(both, qp, i)
        turned = both.T
        qt[i] = jnp.concatenate([turned[0:64], turned[64:128]], axis=1).astype(BF16)
    dq_acc[...] = jnp.zeros_like(dq_acc)
    wo_swap.wait()
    for x2 in range(2):
        wo_sum[x2] = (out_part(x2, c) + wo_in[x2].astype(F32)).astype(BF16)
    ex_swap.wait()
    ex_own.wait()
    ex_sum[...] = (ex_sum[...].astype(F32) + ex_in[...].astype(F32)).astype(BF16)

    def cross_piece(n, j):
        part = rows(32 * j, 32)
        return to(ex_sum.at[n, part], ex_cross.at[n, part], sx.at[2], rx.at[2], b, over)


    def wo_piece(e):
        d, x2 = lax.rem(e, NB), lax.rem(xl + e // NB, 2)
        peer_b = lax.rem(b + d, NB)
        part = wo_sum.at[x2, rows(peer_b * 32, 32)]
        return to(part, wo_parts.at[NB * (e // NB) + b], s3.at[0], r3.at[0], peer_b, 2 * x2 + c)

    for n in range(3):
        times(0, 8, lambda j, n=n: cross_piece(n, j).start())
    cg_pieces[0].wait()
    settle(r1.at[0], home.at[pl.ds(0, 3)])
    wo_parts[b] = wo_sum[xl, rows(b * 32, 32)]
    for item in brought[1:4]:
        item.wait()
    left = lax.broadcasted_iota(jnp.int32, (512, 128), 1) < 64
    for i in range(GROUP):
        scaled = cgs[i].astype(F32) * inv_ref[i]
        pos = query_positions((512, 1), 0, member(m, i))
        mid_doc = (pos >= e0) & (pos < e1)
        terms = scaled * wide_ref[i]
        one = jnp.sum(jnp.where(left, terms, 0.0), axis=1, keepdims=True)
        two = jnp.sum(jnp.where(left, 0.0, terms), axis=1, keepdims=True)
        upper = jnp.where(left, 0.0, pltpu.roll(scaled, 64, 1))
        lower = jnp.where(left, 0.0, scaled)
        for part, val, term in ((0, upper, one), (512, lower, two)):
            span = pl.ds(part, 512)
            gp[i, span] = val.astype(BF16)
            gi[i, span] = jnp.where(mid_doc, val, 0.0).astype(BF16)
            dt[i, span] = jnp.broadcast_to(term, (512, 128))
            di[i, span] = jnp.broadcast_to(jnp.where(mid_doc, term, 0.0), (512, 128))
            lanes = pl.ds(part, 512)
            gt[i, :, lanes] = val.T[64:128].astype(BF16)
            gti[i, :, lanes] = jnp.where(mid_doc, val, 0.0).T[64:128].astype(BF16)

    def dkv_piece(kb):
        return to(stage.at[kb], dkv.at[b], s4.at[0], r4.at[0], kb, h)

    def pair(dp):
        p = lax.rem(b // 2 + 1 + dp, 16)
        send_pieces(eo_piece, jnp.minimum(32 + 8 * dp, 80), jnp.minimum(40 + 8 * dp, 80), c)
        for n in range(3):
            pl.when(dp < 8)(lambda n=n: cross_piece(n, dp + 8).start())
        times(
            jnp.clip(8 * (dp - 2), 1, 2 * NB),
            jnp.clip(8 * (dp - 1), 1, 2 * NB),
            lambda e: wo_piece(e).start(),
        )
        dkvt[...] = jnp.zeros_like(dkvt)
        keys = kv_ref[pl.ds(2 * p, 2)].reshape(512, 128)

        def step(i, expo, g, gturn, dots):
            prob = lax.dot_general(g[i], keys, NT, preferred_element_type=F32)
            term = jnp.concatenate([dots[i]] * 4, axis=1)
            score_grad = (expo * (prob - term)).astype(BF16)
            dq_acc[i] += jnp.dot(score_grad, keys, preferred_element_type=F32)
            dkvt[0:64] += jnp.dot(qt[i], score_grad, preferred_element_type=F32)
            dkvt[64:128] += jnp.dot(gturn[i], expo.astype(BF16), preferred_element_type=F32)

        def scores(i):
            return jnp.exp(lax.dot_general(qp[i], keys, NT, preferred_element_type=F32))

        def inside(i):
            step(i, scores(i), gi, gti, di)

        def edge(i, qb):
            low, high = limits(query_positions((1024, 1), 0, qb), e0, e1, total)
            kpos = key_positions((1, 512), 1, 2 * p, c)
            expo = jnp.where((kpos >= low) & (kpos < high), scores(i), 0.0)
            step(i, expo, gp, gt, dt)

        on_pair(p, m, inside, edge)
        for n in range(2):
            kb = 2 * p + n
            stage[kb] = dkvt[:, 256 * n : 256 * n + 256].astype(BF16)

            @pl.when(kb != b)
            def _():
                dkv_piece(kb).start()

    times(0, 6, pair)
    settle(r8.at[0], r_land.at[pl.ds(0, NB - 1)])
    part = r_land[0]
    for n in range(1, NB):
        part = part + r_land[n]
    r_four[h] = part
    router_near = [
        to(r_four.at[h], r_four.at[h], s9.at[d], r9.at[d], b, lax.rem(h + d, 4))
        for d in range(1, 4)
    ]
    for item in router_near:
        item.start()
    times(6, 16, pair)
    dkv[b] = stage[b]
    for i in range(GROUP):
        both = jnp.where(left, dq_acc[i, 0:512], pltpu.roll(dq_acc[i, 512:1024], 64, 1))
        dqs[i] = (both * SCALE).astype(BF16)

    def dq_piece(part, dj, dc):
        j = lax.rem(y + dj, GROUP)
        c2 = lax.rem(c + dc, 2)
        src = dqs.at[j, rows(c2 * 256 + part * 128, 128)]
        dst = dq.at[c, y, rows(part * 128, 128)]
        k = 8 * part + 2 * dj + dc
        if dj + dc == 0:
            return pltpu.make_async_copy(src, dst, s5.at[k])
        return to(src, dst, s5.at[k], r5.at[k], member(m, j), 2 * xl + c2)

    dq_pieces = [dq_piece(n, dj, dc) for n in range(2) for dj in range(GROUP) for dc in range(2)]
    for item in dq_pieces:
        item.start()
    for item in router_near:
        item.wait()
    r_tot[...] = r_four[0] + r_four[1] + r_four[2] + r_four[3]
    home_tile = (rows(8 * (b // 8), 8), rows(128 * lax.rem(b, 8), 128))
    router_out[home_tile] = r_tot[...]

    def router_last(d):
        return to(r_tot, router_out.at[home_tile], sa.at[0], ra.at[0], lax.rem(b + d, NB), h)

    times(1, NB, lambda d: router_last(d).start())
    settle(sx.at[2], ex_cross)
    settle(rx.at[2], ex_cross)
    ex_in[...] = (ex_sum[...].astype(F32) + ex_cross[...].astype(F32)).astype(BF16)
    half, quarter = rows(c * 512, 512), rows(c * 256, 256)
    ex_moves = []
    for n, (src, dst) in enumerate(
        (
            (ex_in.at[0], exg_out.at[half]),
            (ex_in.at[1], exu_out.at[half]),
            (ex_in.at[2, pl.ds(0, 256)], exd_out.at[quarter, pl.ds(0, 512)]),
            (ex_in.at[2, pl.ds(256, 256)], exd_out.at[quarter, pl.ds(512, 512)]),
        )
    ):
        ex_moves.append(pltpu.make_async_copy(src, dst, le.at[n]))
        ex_moves.append(to(src, dst, se.at[n], re.at[n], b, sib))
    for item in ex_moves:
        item.start()
    for item in dq_pieces:
        item.wait()
    settle(r4.at[0], dkv.at[pl.ds(0, NB - 1)])

    for item in brought[4:]:
        item.wait()
    left, first = lanes_of((256, 128))
    q_gain = jnp.zeros((1, 128), F32)
    k_gain = jnp.zeros((1, 128), F32)

    def unprep(d, u, gain, row):
        turned = d * turn[0] - swapped(d, first) * turn[1]
        scale = lax.rsqrt(by_head(u * u, left) + EPSILON)
        unit = u * scale
        inner = turned * row
        gain = gain + jnp.sum(turned * unit, axis=0, keepdims=True)
        return scale * (inner - unit * by_head(inner * unit, left)), gain

    for j in range(GROUP):
        i, q_cols, kv_cols = slab(j)
        span = slice(128 * j, 128 * j + 128)
        d = (dq[0, j].astype(F32) + dq[1, j].astype(F32)).astype(BF16).astype(F32)
        got, q_gain = unprep(d, raw[i, :, q_cols], q_gain, head_gain[0:1])
        low[i, :, q_cols] = got.astype(BF16)
        d = dkv[8 * j].astype(F32)
        for n in range(1, 8):
            d = d + dkv[8 * j + n].astype(F32)
        d = d.T.astype(BF16).astype(F32)
        got, k_gain = unprep(d, raw[i, :, kv_cols], k_gain, head_gain[1:2])
        low[i, :, kv_cols] = jnp.where(left, got, d).astype(BF16)
    normed_grad = lax.dot_general(low[0], wv[0], NT, preferred_element_type=F32) + lax.dot_general(
        low[1], wv[1], NT, preferred_element_type=F32
    )
    source2 = li2[...].reshape(256, 1024).astype(F32)
    scale = row_scale(source2)
    unit = source2 * scale
    inner = normed_grad * attn_gain[...]
    attn_part = jnp.sum(normed_grad * unit, axis=0, keepdims=True)
    small[...] = jnp.zeros_like(small)
    for n in range(8):
        lanes = slice(128 * n, 128 * n + 128)
        small[n : n + 1] = attn_part[:, lanes]
        small[8 + n : 9 + n] = ffn_part[:, lanes]
    small[16:17] = q_gain
    small[17:18] = k_gain
    near = [
        to(small, four.at[h], sx.at[6 + d], rx.at[6 + d], b, lax.rem(h + d, 4)) for d in range(1, 4)
    ]
    for item in near:
        item.start()
    four[h] = small[...]
    w_other[...] = lax.dot_general(
        normed[...], low[1 - c], TN, preferred_element_type=F32
    ).astype(BF16).reshape(NB, 32, 512)
    w_swap = to(w_other, w_in, sx.at[4], rx.at[4], b, sib)
    w_swap.start()
    back[...] = (scale * (inner - unit * jnp.mean(inner * unit, axis=1, keepdims=True))).reshape(
        2, 128, 1024
    )
    back_low[...] = back[1 - xl].astype(BF16)
    back_swap = to(back_low, back_in, sx.at[5], rx.at[5], b, over)
    back_swap.start()
    mine = lax.dot_general(normed[...], low[c], TN, preferred_element_type=F32)
    for item in near:
        item.wait()
    many[b] = four[0] + four[1] + four[2] + four[3]

    def spread(d):
        return to(many.at[b], many.at[b], s7.at[0], r7.at[0], lax.rem(b + d, NB), h)

    times(1, NB, lambda d: spread(d).start())
    w_swap.wait()
    w_sum[...] = (mine.reshape(NB, 32, 512) + w_in[...].astype(F32)).astype(BF16)

    def w_piece(d):
        peer = lax.rem(b + d, NB)
        return to(w_sum.at[peer], w_land.at[b], s6.at[0], r6.at[0], peer, h)

    times(1, NB, lambda d: w_piece(d).start())
    w_land[b] = w_sum[b]

    settle_rows(r2.at[0], home, c)
    pl.when(c == 0)(eo_same.wait)
    flat = home[...].reshape(1280, 1024)
    mix[...] = (
        lax.dot_general(wts[0].reshape(1280, 256), flat, TN, preferred_element_type=F32)
        + lax.dot_general(wts[1].reshape(1280, 256), flat, TN, preferred_element_type=F32)
    ).reshape(2, 128, 1024)
    mix_swap = to(mix.at[1 - c], mix_in, sx.at[6], rx.at[6], b, sib)
    mix_swap.start()
    back_swap.wait()
    in_grad[...] = (grad[...] + back[xl] + back_in[...].astype(F32)).astype(BF16)
    mix_swap.wait()
    out[...] = (middle[...] + mix[c] + mix_in[...]).astype(BF16)
    settle(r7.at[0], many.at[pl.ds(0, NB - 1)])
    total = many[0]
    for n in range(1, NB):
        total = total + many[n]
    for n in range(8):
        lanes = slice(128 * n, 128 * n + 128)
        attn_small[:, lanes] = total[n : n + 1]
        ffn_small[:, lanes] = total[8 + n : 9 + n]
    q_small[...] = total[16:17, 0:64] + total[16:17, 64:128]
    k_small[...] = total[17:18, 0:64]
    settle(r6.at[0], w_land.at[pl.ds(0, NB - 1)])
    shard = w_land[0].astype(F32)
    for n in range(1, NB):
        shard = shard + w_land[n].astype(F32)
    wq_grad[...] = shard[:, 0:256]
    wk_grad[...] = jnp.concatenate([shard[:, 256:320], shard[:, 384:448]], axis=1)
    wv_grad[...] = jnp.concatenate([shard[:, 320:384], shard[:, 448:512]], axis=1)
    settle(r3.at[0], wo_parts.at[pl.ds(0, 2 * NB - 1)])
    total = wo_parts[0].astype(F32)
    for n in range(1, 2 * NB):
        total = total + wo_parts[n].astype(F32)
    wo_grad[...] = total
    for item in ex_moves:
        item.wait()
    settle(ra.at[0], r_land.at[pl.ds(0, NB - 1)])
    router_grad[...] = router_out[...]
    settle(s1.at[0], home.at[pl.ds(0, 3)])
    settle_rows(s2.at[0], home, c)
    settle(s3.at[0], wo_parts.at[pl.ds(0, 2 * NB - 1)])
    settle(s4.at[0], dkv.at[pl.ds(0, NB - 1)])
    settle(s6.at[0], w_land.at[pl.ds(0, NB - 1)])
    settle(s7.at[0], many.at[pl.ds(0, NB - 1)])
    settle(s8.at[0], r_land.at[pl.ds(0, NB - 1)])
    settle(sa.at[0], r_land.at[pl.ds(0, NB - 1)])


def results_kernel(*refs):
    n = (len(refs) - 5) // 3
    ins, outs, held = refs[:n], refs[n : 2 * n], refs[2 * n : 3 * n]
    wide, (load_sem, store_sem) = refs[3 * n : 3 * n + 3], refs[3 * n + 3 :]
    loads = [pltpu.make_async_copy(ins[k], held[k], load_sem.at[k]) for k in range(n)]
    for item in loads[n - 3 :] + loads[: n - 3]:
        item.start()
    stores = []
    for k in [n - 3, n - 2, n - 1, *range(n - 3)]:
        loads[k].wait()
        src, dst = held[k], outs[k]
        if k >= n - 3:
            src, dst = wide[k - n + 3], dst.at[0]
            src[...] = held[k][...].astype(F32)
        stores.append(pltpu.make_async_copy(src, dst, store_sem.at[k]))
        stores[-1].start()
    for item in stores:
        item.wait()


def finished(results):
    n = len(results)
    shapes = [jax.ShapeDtypeStruct(r.shape, r.dtype) for r in results[: n - 3]] + [
        jax.ShapeDtypeStruct((1,) + r.shape, F32) for r in results[n - 3 :]
    ]
    return pl.pallas_call(
        results_kernel,
        out_shape=shapes,
        in_specs=[ANY] * n,
        out_specs=[ANY] * n,
        scratch_shapes=[pltpu.VMEM(r.shape, r.dtype) for r in results]
        + [pltpu.VMEM(r.shape, F32) for r in results[n - 3 :]]
        + [pltpu.SemaphoreType.DMA((n,))] * 2,
        compiler_params=pltpu.CompilerParams(vmem_limit_bytes=60 * 1024 * 1024),
    )(*results)


VM = pl.BlockSpec(memory_space=pltpu.VMEM)
SM = pl.BlockSpec(memory_space=pltpu.SMEM)
ANY = pl.BlockSpec(memory_space=pl.ANY)


def call(kernel, collective_id, ins, outs, scratch, sems, flops, *operands):
    return pl.pallas_call(
        kernel,
        out_shape=[jax.ShapeDtypeStruct(shape, dtype) for shape, dtype, _ in outs],
        in_specs=ins,
        out_specs=[spec for _, _, spec in outs],
        scratch_shapes=[pltpu.VMEM(shape, dtype) for shape, dtype in scratch]
        + [pltpu.SemaphoreType.DMA(n) for n in sems],
        compiler_params=pltpu.CompilerParams(
            collective_id=collective_id,
            has_side_effects=True,
            vmem_limit_bytes=60 * 1024 * 1024,
        ),
        cost_estimate=pl.CostEstimate(
            flops=flops, bytes_accessed=8_000_000, transcendentals=flops // 2000
        ),
    )(*operands)


def limits(pos, e0, e1, total):
    low = jnp.where(pos < e0, 0, jnp.where(pos < e1, e0, e1))
    end = jnp.where(pos < e0, e0, jnp.where(pos < e1, e1, total))
    reach = low + ((pos - low) // BLOCK + 1) * BLOCK
    return low, jnp.minimum(end, reach)


def query_positions(shape, axis, qb):
    r = lax.broadcasted_iota(jnp.int32, shape, axis)
    r = lax.rem(r, 512)
    return 512 * qb + 256 * lax.rem(r // 128, 2) + 128 * (r // 256) + lax.rem(r, 128)


def key_positions(shape, axis, kb, core):
    r = lax.broadcasted_iota(jnp.int32, shape, axis)
    return 512 * (kb + r // 256) + 256 * lax.rem(r // 128, 2) + 128 * core + lax.rem(r, 128)


def body(
    layer_input,
    attn_gain,
    w_query,
    key_weight,
    value_weight,
    w_output,
    query_gain,
    key_gain,
    ffn_gain,
    router,
    w_gate,
    w_up,
    w_down,
    routes,
    doc_lengths,
    cotangent,
):
    tokens, width = layer_input.shape
    lane = np.arange(128) % (HEAD_SIZE // 2)
    pace = jnp.asarray(ROPE_BASE ** (-2.0 * lane / HEAD_SIZE), F32)[None]
    (
        w_full, wo_full, both_inputs, q_group, kv_all, up_rows, raw, normed, ctx_wide, ctx_inv, turn, router_wide,
        pick, context, middle, mixed_in, gates, head_gain,
    ) = call(
        forward_kernel,
        0,
        [SM] + [VM] * 13,
        [
            ((2, width, 512), BF16, ANY),
            ((2, 2, width, width // 4), BF16, ANY),
            ((2, tokens, width), BF16, ANY),
            ((GROUP, 512, 128), BF16, ANY),
            ((NB, 256, 128), BF16, ANY),
            ((16, SLOTS, width), BF16, ANY),
            ((2, 2 * tokens, 512), F32, ANY),
            ((2 * tokens, width), BF16, ANY),
            ((GROUP, 512, 128), F32, ANY),
            ((GROUP, 512, 128), F32, ANY),
            ((2, 2 * tokens, 128), F32, ANY),
            ((128, width), F32, ANY),
            ((16, SLOTS, 2 * tokens), BF16, VM),
            ((tokens, width), BF16, VM),
            ((tokens, width), F32, VM),
            ((2 * tokens, width), BF16, VM),
            ((2 * tokens, 128), F32, VM),
            ((2, 128), F32, VM),
        ],
        [
            ((2 * tokens, width), BF16),
            ((2 * tokens, 128), F32),
            ((2, 2 * tokens, 512), F32),
            ((2 * tokens, width), BF16),
            ((GROUP, 512, 128), F32),
            ((GROUP, 512, 128), F32),
            ((2, 2 * tokens, 128), F32),
            ((128, width), F32),
            ((32, 512), BF16),
            ((2, width, 512), BF16),
            ((2, 2, width, width // 4), BF16),
            ((2, tokens, width), BF16),
            ((2 * tokens, width), BF16),
            ((2, 8, 128), jnp.int32),
            ((16, SLOTS, width), BF16),
            ((GROUP, 2 * tokens, 128), BF16),
            ((GROUP, 2 * tokens, 128), BF16),
            ((GROUP, 512, 128), BF16),
            ((NB, 256, 128), BF16),
            ((GROUP, 1024, 128), BF16),
            ((80, 512), BF16),
            ((GROUP, 80, 1024), F32),
            ((GROUP, 80, 1024), F32),
            ((GROUP, 80, 1024), F32),
            ((GROUP, 512, 128), BF16),
            ((2 * GROUP, tokens, 128), BF16),
        ],
        [(1,)] * 4 + [(10,)] * 2 + [(16,)] * 2 + [(1,), (NB,)] + [(1,)] * 2 + [(8,)] * 2 + [(9,), (12,)],
        18_000_000_000,
        doc_lengths,
        w_query,
        key_weight,
        value_weight,
        w_output,
        layer_input,
        cotangent,
        routes.T,
        attn_gain[None],
        query_gain[None],
        key_gain[None],
        pace,
        ffn_gain[None],
        router.T,
    )
    wts, expert_out, ex_grads, middle_grad, attn_grad, ffn_part, router_part = call(
        experts_kernel,
        1,
        [VM] * 3 + [ANY] * 6 + [VM, ANY],
        [
            ((2, 16, SLOTS, 2 * tokens), BF16, ANY),
            ((16, SLOTS, width), BF16, ANY),
            ((3, 1024, 512), BF16, ANY),
            ((tokens, width), F32, VM),
            ((tokens, width), BF16, VM),
            ((1, width), F32, VM),
            ((NB, width), F32, VM),
        ],
        [
            ((16, SLOTS, width), BF16),
            ((1, width, 512), BF16),
            ((1, width, 512), BF16),
            ((1, 512, width), BF16),
            ((tokens, width), F32),
            ((tokens, width), BF16),
            ((128, width), F32),
            ((2, 16, SLOTS, 2 * tokens), BF16),
            ((16, SLOTS, width), BF16),
            ((3, 1024, 512), BF16),
            ((16, SLOTS, width), BF16),
            ((16, SLOTS, width), BF16),
            ((16, 8, 128), F32),
            ((16, 8, 128), F32),
            ((16, SLOTS, width), BF16),
            ((16, SLOTS, width), BF16),
            ((16, 8, 128), F32),
            ((16, 8, 128), F32),
            ((16, SLOTS, 512), BF16),
            ((16, SLOTS, 512), BF16),
            ((16, SLOTS, 512), BF16),
            ((16, SLOTS, width), BF16),
            ((2 * tokens, width), F32),
            ((16, 2 * tokens), F32),
            ((tokens, width), F32),
            ((16, tokens), F32),
            ((128, tokens), F32),
            ((16, SLOTS, 128), F32),
            ((16, SLOTS, 128), F32),
        ],
        [(1,), (ROUNDS,)] + [(1,)] * 6 + [(4,)] * 2 + [(4,), (7,), (3,)],
        12_000_000_000,
        mixed_in,
        gates,
        pick,
        up_rows,
        w_gate,
        w_up,
        w_down,
        middle,
        cotangent,
        ffn_gain[None],
        router_wide,
    )
    results = call(
        backward_kernel,
        2,
        [SM] + [VM] * 7 + [ANY] * 14,
        [
            ((tokens, width), BF16, VM),
            ((tokens, width), BF16, VM),
            ((32, 256), F32, VM),
            ((32, 128), F32, VM),
            ((32, 128), F32, VM),
            ((32, 256), F32, VM),
            ((1, width), F32, VM),
            ((1, HEAD_SIZE), F32, VM),
            ((1, HEAD_SIZE), F32, VM),
            ((1, width), F32, VM),
            ((NB, width), F32, VM),
            ((width, 512), BF16, ANY),
            ((width, 512), BF16, ANY),
            ((512, width), BF16, ANY),
        ],
        [
            ((GROUP, 512, 128), BF16),
            ((NB, 256, 128), BF16),
            ((GROUP, 512, 128), F32),
            ((GROUP, 512, 128), F32),
            ((2, width, 512), BF16),
            ((2, 2 * tokens, 512), F32),
            ((2 * tokens, width), BF16),
            ((2, tokens, width), BF16),
            ((2, 2 * tokens, 128), F32),
            ((2, 16, SLOTS, 2 * tokens), BF16),
            ((tokens, width), F32),
            ((tokens, width), F32),
            ((2 * GROUP, tokens, 128), BF16),
            ((GROUP, 512, 128), BF16),
            ((GROUP, 1024, 128), BF16),
            ((GROUP, 1024, 128), BF16),
            ((GROUP, 1024, 128), BF16),
            ((GROUP, 64, 1024), BF16),
            ((GROUP, 64, 1024), BF16),
            ((GROUP, 64, 1024), BF16),
            ((GROUP, 1024, 128), F32),
            ((GROUP, 1024, 128), F32),
            ((GROUP, 512, 128), BF16),
            ((128, 512), F32),
            ((NB, 128, 256), BF16),
            ((GROUP, 1024, 128), F32),
            ((2, 1024, 256), BF16),
            ((2, 1024, 256), BF16),
            ((2, 1024, 256), BF16),
            ((3, 512, 512), BF16),
            ((3, 512, 512), BF16),
            ((3, 512, 512), BF16),
            ((2, GROUP, 2 * tokens, 128), BF16),
            ((NB, 128, 256), BF16),
            ((16, SLOTS, width), BF16),
            ((2 * NB, 32, 256), BF16),
            ((2, 2 * tokens, 512), BF16),
            ((NB, 32, 512), BF16),
            ((NB, 32, 512), BF16),
            ((NB, 32, 512), BF16),
            ((NB, 32, 512), BF16),
            ((2, tokens, width), F32),
            ((tokens, width), BF16),
            ((tokens, width), BF16),
            ((2, tokens, width), F32),
            ((tokens, width), F32),
            ((24, 128), F32),
            ((4, 24, 128), F32),
            ((NB, 24, 128), F32),
            ((NB, 8, 128), F32),
            ((4, 8, 128), F32),
            ((8, 128), F32),
            ((NB, width), F32),
        ],
        [(1,)] * 8 + [(16,)] * 2 + [(1,)] * 6 + [(4,)] * 2 + [(1,)] * 2 + [(10,)] * 2 + [(6,), (12,)] + [(4,)] * 3,
        45_000_000_000,
        doc_lengths,
        attn_grad,
        context,
        wo_full,
        head_gain,
        attn_gain[None],
        ffn_part,
        router_part,
        expert_out,
        ex_grads,
        q_group,
        kv_all,
        ctx_wide,
        ctx_inv,
        w_full,
        raw,
        normed,
        both_inputs,
        turn,
        wts,
        middle,
        middle_grad,
    )
    results = finished(results)
    return (
        *results[:2],
        results[6][0],
        *results[2:6],
        *[row[0] for row in results[7:10]],
        results[10].T,
        *results[11:],
    )


def solution(mesh):
    everyone = P(("blk", "head"), None)
    both = P("blk", "head")
    expert = P("blk", None, None)
    return jax.shard_map(
        body,
        mesh=mesh,
        in_specs=(everyone, P(), both, both, both, both, P(), P(), P(), P())
        + (expert, expert, expert, everyone, P(), everyone),
        out_specs=(everyone, everyone, P(), both, both, both, both, P(), P(), P(), P())
        + (expert, expert, expert),
        check_vma=False,
    )
```

```python
import jax
import jax.numpy as jnp
import numpy as np
from jax import lax
from jax.experimental import pallas as pl
from jax.experimental.pallas import tpu as pltpu
from jax.sharding import PartitionSpec as P

HEAD_SIZE = 64
TOPK = 8
BLOCK = 256
EPSILON = 1e-06
ROPE_BASE = 10000.0
PRECISE = lax.Precision.HIGHEST
SCALE = HEAD_SIZE ** (-0.5)

NB = 32
ROUNDS = 5
SLOTS = 80
GROUP = 4
MESH_ID = pl.DeviceIdType.MESH
F32 = jnp.float32
BF16 = jnp.bfloat16
NT = (((1,), (1,)), ((), ()))
NN = (((1,), (0,)), ((), ()))
TN = (((0,), (0,)), ((), ()))


def place():
    b = lax.axis_index("blk")
    h = lax.axis_index("head")
    y = b // 8
    r = lax.rem(b, 8)
    m = jnp.where(lax.rem(y, 2) == 0, r, 7 - r)
    return b, h // 2, lax.rem(h, 2), y, m


def member(m, j):
    return 8 * j + m + lax.rem(j, 2) * (7 - 2 * m)


def times(start, n, body):
    def step(i, carry):
        body(i)
        return carry

    lax.fori_loop(start, n, step, 0)


def signal(sem, blk, head):
    pl.semaphore_signal(sem, inc=1, device_id=(blk, head), device_id_type=MESH_ID)


def rows(start, size):
    return pl.ds(pl.multiple_of(start, size), size)


def to(src, dst, send, recv, blk, head):
    return pltpu.make_async_remote_copy(
        src, dst, send, recv, device_id=(blk, head), device_id_type=MESH_ID
    )


def settle(sem, part):
    pltpu.make_async_copy(part, part, sem).wait()


def settle_rows(sem, blocks, c):
    pl.when(c == 0)(lambda: settle(sem, blocks.at[pl.ds(0, 15)]))
    pl.when(c == 1)(lambda: settle(sem, blocks))


def greet_all(bar, b, xl, c, y, m):
    h = 2 * xl + c
    times(1, NB, lambda d: signal(bar, lax.rem(b + d, NB), h))
    times(0, NB, lambda d: signal(bar, lax.rem(b + d, NB), 2 * (1 - xl) + c))
    for dj in range(GROUP):
        j = member(m, lax.rem(y + dj, GROUP))
        signal(bar, j, 2 * xl + 1 - c)
    pl.semaphore_wait(bar, 2 * NB - 1 + GROUP)


def pad_queries(both, qp, i):
    left = lax.broadcasted_iota(jnp.int32, (512, 128), 1) < 64
    qp[i, 0:512] = jnp.where(left, both, 0.0).astype(BF16)
    qp[i, 512:1024] = jnp.where(left, pltpu.roll(both, 64, 1), 0.0).astype(BF16)


def on_pair(p, m, inside, edge):
    def each(i):
        qb = member(m, i)
        whole = (p >= 1) & (2 * p + 1 <= qb - 1)
        pl.when(whole)(lambda: inside(i))
        pl.when(jnp.logical_not(whole) & (2 * p <= qb))(lambda: edge(i, qb, 512))
        pl.when(2 * p == qb + 1)(lambda: edge(i, qb, 128))

    times(0, GROUP, each)


def by_head(values, left):
    one = jnp.sum(jnp.where(left, values, 0.0), axis=1, keepdims=True) / HEAD_SIZE
    two = jnp.sum(jnp.where(left, 0.0, values), axis=1, keepdims=True) / HEAD_SIZE
    return jnp.where(left, one, two)


def swapped(values, first):
    return jnp.where(first, pltpu.roll(values, 96, 1), pltpu.roll(values, 32, 1))


def row_scale(values):
    return lax.rsqrt(jnp.mean(values * values, axis=1, keepdims=True) + EPSILON)


def lanes_of(shape):
    lane = lax.broadcasted_iota(jnp.int32, shape, 1)
    return lane < 64, lax.rem(lane, 64) < 32


def slab(j):
    return j // 2, slice(128 * (j % 2), 128 * (j % 2) + 128), slice(
        256 + 128 * (j % 2), 384 + 128 * (j % 2)
    )


def forward_kernel(
    lengths, wq, wk, wvl, wo, li, cot, routes_t, attn_gain, q_gain, k_gain, pace, ffn_gain, router_t,
    w_out, wo_out, li_out, q_out, kv_out, c_out, raw_out, normed_out, wide_out, inv_out, turn_out, router_out,
    pick, ctx_out, mid_out, tok_out, gates_out, head_gain,
    tok, gt, raw, normed, wide_all, inv_all, turn, router,
    ws, wv, wov, li2, cot2, rt, xs, qs, kvst, qg, kvs, qp, vt, acc, accm, peer, ctx, ctx_in,
    sw, rw, so, ro, sx, rx, s1, r1, s2, r2, s5, r5, s7, r7, ls, lk,
):
    b, xl, c, y, m = place()
    h = 2 * xl + c
    sib = 2 * xl + 1 - c
    over = 2 * (1 - xl) + c
    odd = lax.rem(b + c, 2)
    e0, e1, total = lengths[0], lengths[0] + lengths[1], 512 * NB
    pairs = jnp.concatenate([wk[...].astype(F32), wvl[...].astype(F32)], axis=1)
    even = jnp.concatenate([pairs[:, 0:64], pairs[:, 128:192]], axis=1)
    other = jnp.concatenate([pairs[:, 64:128], pairs[:, 192:256]], axis=1)
    ws[:, 0:256] = wq[...]
    ws[:, 256:384] = even.astype(BF16)
    ws[:, 384:512] = other.astype(BF16)
    greet_all(pltpu.get_barrier_semaphore(), b, xl, c, y, m)

    def w_first(d):
        part = wv.at[c, rows(b * 32, 32)]
        return to(ws, part, sw.at[0], rw.at[0], lax.rem(b + d, NB), h)

    def wo_first(d):
        part = wov.at[0, c, rows(b * 32, 32)]
        return to(wo, part, so.at[0], ro.at[0], lax.rem(b + d, NB), h)

    keeps = []

    def keep(part, out):
        item = pltpu.make_async_copy(part, out, lk.at[len(keeps)])
        item.start()
        keeps.append(item)

    near = [
        to(routes_t, rt.at[c], sx.at[0], rx.at[0], b, sib),
        to(cot, cot2.at[rows(c * 128, 128)], sx.at[1], rx.at[1], b, sib),
        to(li, li2.at[xl], sx.at[2], rx.at[2], b, over),
    ]
    for item in near:
        item.start()
    times(1, NB, lambda d: w_first(d).start())
    wv[c, rows(b * 32, 32)] = ws[...]
    li2[xl] = li[...]
    cot2[rows(c * 128, 128)] = cot[...]
    rt[c] = routes_t[...]

    near[0].wait()
    both_routes = jnp.concatenate([rt[0], rt[1]], axis=1)
    mine = 2 * lax.broadcasted_iota(jnp.int32, (16, 256), 0) + odd
    chosen = jnp.zeros((16, 256), F32)
    for k in range(TOPK):
        chosen = jnp.where(both_routes[k : k + 1] == mine, 1.0, chosen)
    earlier = lax.broadcasted_iota(jnp.int32, (256, 256), 0) < lax.broadcasted_iota(
        jnp.int32, (256, 256), 1
    )
    rank = jnp.dot(
        chosen.astype(BF16), jnp.where(earlier, 1.0, 0.0).astype(BF16), preferred_element_type=F32
    )
    slot = lax.broadcasted_iota(jnp.int32, (80, 256), 0).astype(F32)
    for k in range(16):
        at = jnp.where(rank[k : k + 1] == slot, chosen[k : k + 1], 0.0)
        pick[k] = at.astype(BF16)
    near[1].wait()
    c_piece = rows_out(xs, c_out, b, xl, c, lambda r: s5.at[0], lambda r: r5.at[0])
    c_same = pltpu.make_async_copy(xs.at[b // 2], c_out.at[15], ls.at[3])

    def fetch(d):
        k = stride(b, d)
        xs[k] = jnp.dot(pick[k], cot2[...], preferred_element_type=F32).astype(BF16)

    times(1, 17, fetch)
    pl.when(c == 0)(c_same.start)
    send_pieces(c_piece, 0, 32, c)

    near[2].wait()
    keep(li2, li_out)
    source2 = li2[...].reshape(256, 1024).astype(F32)
    normed[...] = (source2 * row_scale(source2) * attn_gain[...]).astype(BF16)

    keep(normed, normed_out)
    settle(rw.at[0], wv.at[c, rows(0, 992)])
    w_sib = to(wv.at[c], wv.at[c], sx.at[3], rx.at[3], b, sib)
    w_sib.start()
    wov[0, c, rows(b * 32, 32)] = wo[...]
    left, first = lanes_of((256, 128))
    t = lax.broadcasted_iota(jnp.int32, (256, 128), 0)
    pos = 512 * b + 256 * (t // 128) + 128 * c + lax.rem(t, 128)
    opening = jnp.where(pos < e0, 0, jnp.where(pos < e1, e0, e1))
    angles = (pos - opening).astype(F32) * pace[...]
    turn[0] = jnp.cos(angles)
    sine = jnp.sin(angles)
    turn[1] = jnp.where(first, -sine, sine)
    head_gain[0:1] = jnp.concatenate([q_gain[...], q_gain[...]], axis=1)
    head_gain[1:2] = jnp.concatenate([k_gain[...], jnp.ones((1, 64), F32)], axis=1)
    router[...] = jnp.zeros_like(router)
    router[0:NB] = router_t[...]
    keep(turn, turn_out)
    keep(router, router_out)
    w_sib.wait()
    keep(wv, w_out)
    for i in range(2):
        raw[i] = jnp.dot(normed[...], wv[i], preferred_element_type=F32)
    for j in range(GROUP):
        i, q_cols, kv_cols = slab(j)
        u = raw[i, :, q_cols]
        n = u * lax.rsqrt(by_head(u * u, left) + EPSILON) * head_gain[0:1]
        turned = n * turn[0] + swapped(n, first) * turn[1]
        qs[j] = (turned.astype(BF16).astype(F32) * SCALE).astype(BF16)
        u = raw[i, :, kv_cols]
        n = u * lax.rsqrt(by_head(u * u, left) + EPSILON) * head_gain[1:2]
        turned = n * turn[0] + swapped(n, first) * turn[1]
        kvst[j] = jnp.where(left, turned, u).astype(BF16)

    def q_piece(part, dj, dc):
        j = lax.rem(y + dj, GROUP)
        k = 8 * part + 2 * dj + dc
        src, dst = qs.at[j, rows(part * 128, 128)], qg.at[y, rows(c * 256 + part * 128, 128)]
        if dj + dc == 0:
            return pltpu.make_async_copy(src, dst, s1.at[k])
        return to(src, dst, s1.at[k], r1.at[k], member(m, j), 2 * xl + lax.rem(c + dc, 2))

    q_pieces = [q_piece(n, dj, dc) for n in range(2) for dj in range(GROUP) for dc in range(2)]

    def kv_piece(i):
        d, half = lax.rem(i, NB), rows(128 * (i // NB), 128)
        peer_b = lax.rem(b + d, NB)
        return to(kvst.at[peer_b // 8, half], kvs.at[b, half], s2.at[0], r2.at[d], peer_b, h)

    for item in q_pieces:
        item.start()
    kv_own = pltpu.make_async_copy(kvst.at[y], kvs.at[b], ls.at[1])
    kv_own.start()
    times(1, NB, lambda d: kv_piece(d).start())
    times(NB + 1, 2 * NB, lambda i: kv_piece(i).start())
    for item in q_pieces:
        item.wait()
    kv_own.wait()
    keep(qg, q_out)
    keep(raw, raw_out)
    for i in range(GROUP):
        pad_queries(qg[i].astype(F32), qp, i)
    acc[...] = jnp.zeros_like(acc)
    accm[...] = jnp.zeros_like(accm)
    vt[64:80] = jnp.ones((16, 512), BF16)

    def pair(dp):
        p = lax.rem(b // 2 + 16 - dp, 16)
        send_pieces(c_piece, 32 + 3 * dp, 35 + 3 * dp, c)
        times(jnp.minimum(16 * dp, NB) + (dp == 0), jnp.minimum(16 * dp + 16, NB), lambda d: wo_first(d).start())
        for kb in (2 * p, 2 * p + 1):

            @pl.when(kb != b)
            def _():
                settle(r2.at[lax.rem(b + NB - kb, NB)], kvs.at[kb])

        vt[0:64] = (
            kvs[pl.ds(2 * p, 2)].reshape(512, 128).astype(F32).T[64:128].astype(BF16)
        )

        def scores(i, size):
            keys = kvs[pl.ds(2 * p, 2)].reshape(512, 128)[0:size]
            return jnp.exp(lax.dot_general(keys, qp[i], NT, preferred_element_type=F32))

        def inside(i):
            acc[i] += jnp.dot(vt[...], scores(i, 512).astype(BF16), preferred_element_type=F32)

        def edge(i, qb, size):
            low, high = limits(query_positions((1, 1024), 1, qb), e0, e1, total)
            kpos = key_positions((size, 1), 0, 2 * p, c)
            expo = jnp.where((kpos >= low) & (kpos < high), scores(i, size), 0.0)
            accm[i] += jnp.dot(vt[:, 0:size], expo.astype(BF16), preferred_element_type=F32)

        on_pair(p, m, inside, edge)

    times(0, 10, pair)
    settle(ro.at[0], wov.at[0, c, rows(0, 992)])
    wo_moves = [
        to(wov.at[0, c], wov.at[0, c], sx.at[6], rx.at[6], b, sib),
        to(wov.at[0, c], wov.at[1, c], sx.at[4], rx.at[4], b, over),
    ]
    for item in wo_moves:
        item.start()
    times(10, 16, pair)
    for i in range(GROUP):
        pos = query_positions((1, 1024), 1, member(m, i))
        acc[i] = accm[i] + jnp.where((pos >= e0) & (pos < e1), acc[i], 0.0)
    swap = to(acc, peer, sx.at[5], rx.at[5], b, sib)
    swap.start()
    keep(kvs, kv_out)
    for item in wo_moves:
        item.wait()
    far_sib = to(wov.at[1, c], wov.at[1, c], sx.at[7], rx.at[7], b, sib)
    far_sib.start()
    swap.wait()

    def ctx_piece(dj, dx):
        j = lax.rem(y + dj, GROUP)
        x2 = lax.rem(xl + dx, 2)
        src, dst = ctx.at[j, rows(c * 256 + x2 * 128, 128)], ctx_in.at[4 * xl + y]
        k = 2 * dj + dx
        if k == 0:
            return pltpu.make_async_copy(src, dst, ls.at[6])
        return to(src, dst, s7.at[k], r7.at[k], member(m, j), 2 * x2 + c)

    ctx_pieces = [ctx_piece(dj, dx) for dj in range(GROUP) for dx in range(2)]
    for i in range(GROUP):
        both = acc[i] + peer[i]
        inverse = 1.0 / both[64:65]
        wide = both[0:64] * inverse
        flat = jnp.concatenate([wide[:, 0:512], wide[:, 512:1024]], axis=0).T
        wide_all[i] = flat
        ctx[i] = flat.astype(BF16)
        spread = jnp.broadcast_to(inverse, (64, 1024))
        inv_all[i] = jnp.concatenate([spread[:, 0:512], spread[:, 512:1024]], axis=0).T
    for item in ctx_pieces:
        item.start()
    keep(wide_all, wide_out)
    keep(inv_all, inv_out)
    far_sib.wait()
    keep(wov, wo_out)
    for item in ctx_pieces:
        item.wait()

    context = jnp.concatenate([ctx_in[n] for n in range(2 * GROUP)], axis=1)
    ctx_out[...] = context
    for i in range(2):
        for x2, part in ((xl, wov[0, i]), (1 - xl, wov[1, i])):
            cols = rows(512 * x2 + 256 * i, 256)
            mid_out[:, cols] = li[:, cols].astype(F32) + jnp.dot(
                context, part, preferred_element_type=F32
            )
    middle = mid_out[...]
    mixed = (middle * row_scale(middle) * ffn_gain[...]).astype(BF16)
    own = rows(c * 128, 128)
    tok[own] = mixed
    tok_swap = to(tok.at[own], tok.at[own], sx.at[8], rx.at[8], b, sib)
    tok_swap.start()
    logits = lax.dot_general(
        mixed.astype(F32), router[...], NT, preferred_element_type=F32, precision=PRECISE
    )
    expert = lax.broadcasted_iota(jnp.int32, (128, 128), 0)
    hit = jnp.zeros((128, 128), F32)
    for k in range(TOPK):
        hit = jnp.where(routes_t[k : k + 1] == expert, 1.0, hit)
    hit = hit.T
    top = jnp.max(jnp.where(hit > 0.0, logits, -1e30), axis=1, keepdims=True)
    weight = jnp.where(hit > 0.0, jnp.exp(logits - top), 0.0)
    gt[own] = weight / jnp.sum(weight, axis=1, keepdims=True)
    gates_swap = to(gt.at[own], gt.at[own], sx.at[9], rx.at[9], b, sib)
    gates_swap.start()

    settle(sw.at[0], wv.at[0, rows(0, 992)])
    settle(so.at[0], wov.at[0, 0, rows(0, 992)])
    settle(s2.at[0], kvs.at[pl.ds(0, NB - 1)])
    settle_rows(s5.at[0], xs, c)
    settle_rows(r5.at[0], xs, c)
    pl.when(c == 0)(c_same.wait)
    tok_swap.wait()
    gates_swap.wait()
    tok_out[...] = tok[...]
    gates_out[...] = gt[...]
    for item in keeps:
        item.wait()


def row_peer(b, xl, c, k):
    e = 2 * k + lax.rem(b + c, 2)
    apart = lax.rem(b // 4 + e // 4, 2)
    return e, 2 * (xl + apart - 2 * xl * apart) + c


def stride(b, d):
    return lax.rem(b // 2 + 5 * d, 16)


def rows_out(src, dst, b, xl, c, send, recv):
    def piece(d, r):
        k = stride(b, d)
        e, head = row_peer(b, xl, c, k)
        if src.shape[1] < 16:
            return to(src.at[k], dst.at[d - 1], send(r), recv(r), e, head)
        part = rows(16 * r, 16)
        return to(src.at[k, part], dst.at[d - 1, part], send(r), recv(r), e, head)

    return piece


def rows_home(src, dst, b, xl, c, send, recv):
    def piece(d, r):
        e, head = row_peer(b, xl, c, stride(b, 16 - d))
        if src.shape[1] < 16:
            return to(src.at[d - 1], dst.at[b // 2], send(r), recv(r), e, head)
        part = rows(16 * r, 16)
        return to(src.at[d - 1, part], dst.at[b // 2, part], send(r), recv(r), e, head)

    return piece


def send_pieces(piece, start, stop, c):
    def one(i):
        d = lax.rem(i, 16) + 1
        pl.when((d < 16) | (c == 1))(lambda: piece(d, i // 16).start())

    times(start, stop, one)


def start_tiles(piece, d, c, local):
    pl.when((d < 16) | (c == 1))(lambda: piece(d, 0).start())
    pl.when((d == 16) & (c == 0))(local.start)


def experts_kernel(
    tok, gt, pick, up_hbm, gate_hbm, upw_hbm, down_hbm, middle_hbm, cot_hbm, ffn_gain, router_hbm,
    wts_hbm, eo_hbm, ex_hbm, grad_out, low_out, small_out, router_out,
    up_rows, gate_w, up_w, down_w, middle_ref, cot, router, wts_out, eo_out, ex_out,
    xs, xl_rows, gs, gl, rs, rl, ggs, ggl, hid, gb, ub, og, mgs, ggt, mg_in, gg_in, gg_all, gcol, ggcol,
    s1, r1, s2, r2, s3, r3, s4, r4, sx, rx, ls, li, lo,
):
    b, xl, c, _, _ = place()
    h = 2 * xl + c
    sib = 2 * xl + 1 - c
    odd = lax.rem(b + c, 2)
    brought = [
        pltpu.make_async_copy(src, dst, li.at[n])
        for n, (src, dst) in enumerate(
            (
                (gate_hbm, gate_w),
                (upw_hbm, up_w),
                (down_hbm, down_w),
                (up_hbm, up_rows),
                (middle_hbm, middle_ref),
                (cot_hbm, cot),
                (router_hbm, router),
            )
        )
    ]
    for item in brought:
        item.start()
    bar = pltpu.get_barrier_semaphore()

    def greet(d):
        e, head = row_peer(b, xl, c, stride(b, d))
        signal(bar, e, head)

    times(1, 16, greet)
    signal(bar, b, sib)
    pl.when(c == 1)(lambda: greet(0))
    pl.semaphore_wait(bar, 16 + c)
    x_piece = rows_out(xs, xl_rows, b, xl, c, lambda r: s1.at[0], lambda r: r1.at[r])
    x_same = pltpu.make_async_copy(xs.at[b // 2], xl_rows.at[15], ls.at[0])

    def fetch(r):
        part = rows(16 * r, 16)
        xs[:, part] = (
            jnp.dot(pick[:, part].reshape(256, 256), tok[...], preferred_element_type=F32)
            .astype(BF16)
            .reshape(16, 16, 1024)
        )
        send_pieces(x_piece, 16 * r, 16 * r + 16, c)

    times(0, 1, fetch)
    high = gt[...].astype(BF16)
    rest = gt[...] - high.astype(F32)
    mid = rest.astype(BF16)
    low = (rest - mid.astype(F32)).astype(BF16)
    g_piece = rows_out(gs, gl, b, xl, c, lambda r: s2.at[0], lambda r: r2.at[0])
    g_same = pltpu.make_async_copy(gs.at[b // 2], gl.at[15], ls.at[1])

    def as_row(column):
        wide = jnp.concatenate([jnp.broadcast_to(column, (80, 128)), jnp.zeros((48, 128), F32)])
        return wide.T[0:8]

    spread = jnp.dot(
        pick[...].reshape(1280, 256),
        jnp.concatenate([high, mid, low], axis=1),
        preferred_element_type=F32,
    )
    spread = spread[:, 0:128] + spread[:, 128:256] + spread[:, 256:384]
    lane = lax.broadcasted_iota(jnp.int32, (1280, 128), 1)
    expert = 2 * (lax.broadcasted_iota(jnp.int32, (1280, 128), 0) // 80) + odd
    column = jnp.sum(jnp.where(lane == expert, spread, 0.0), axis=1, keepdims=True)
    for k in range(16):
        gs[k] = as_row(column[80 * k : 80 * k + 80])
    times(1, 17, lambda d: start_tiles(g_piece, d, c, g_same))
    times(1, ROUNDS, fetch)
    pl.when(c == 0)(x_same.start)
    weights = pick[...].reshape(1280, 256).astype(F32) * column
    weights_high = weights.astype(BF16)
    wts_out[0] = weights_high.reshape(16, 80, 256)
    wts_out[1] = (weights - weights_high.astype(F32)).astype(BF16).reshape(16, 80, 256)
    wts_keep = pltpu.make_async_copy(wts_out, wts_hbm, lo.at[0])
    wts_keep.start()
    for item in brought:
        item.wait()
    home = rows_home(rs, rl, b, xl, c, lambda r: s3.at[0], lambda r: r3.at[0])
    home_same = pltpu.make_async_copy(rs.at[15], rl.at[b // 2], ls.at[2])
    gg_home = rows_home(ggs, ggl, b, xl, c, lambda r: s4.at[0], lambda r: r4.at[0])
    gg_same = pltpu.make_async_copy(ggs.at[15], ggl.at[b // 2], ls.at[3])

    pl.when(c == 0)(x_same.wait)

    def group(r):
        part = rows(16 * r, 16)
        pl.when(c == 0)(lambda: settle(r1.at[r], xl_rows.at[pl.ds(0, 15), part]))
        pl.when(c == 1)(lambda: settle(r1.at[r], xl_rows.at[:, part]))
        x = xl_rows[:, part].reshape(256, 1024)
        u = up_rows[:, part].reshape(256, 1024).astype(F32)
        gate_pre = jnp.dot(x, gate_w[0], preferred_element_type=F32)
        up_pre = jnp.dot(x, up_w[0], preferred_element_type=F32)
        sig = jax.nn.sigmoid(gate_pre)
        act = gate_pre * sig
        hidden = (act * up_pre).astype(BF16)
        out = jnp.dot(hidden, down_w[0], preferred_element_type=F32).astype(BF16)
        eo_out[:, part] = out.reshape(16, 16, 1024)
        gate_grad = jnp.sum(u * out.astype(F32), axis=1, keepdims=True)
        ggcol[:, part] = jnp.broadcast_to(gate_grad, (256, 128)).reshape(16, 16, 128)
        @pl.when(r == 0)
        def _():
            settle_rows(r2.at[0], gl, c)
            pl.when(c == 0)(g_same.wait)
            for n in range(16):
                row = jnp.concatenate([gl[n], jnp.zeros((120, 128), F32)])
                gcol[n] = jnp.broadcast_to(row.T[0:80, 0:1], (80, 128))

        out_grad = (gcol[:, part].reshape(256, 128)[:, 0:1] * u).astype(BF16)
        hidden_grad = lax.dot_general(out_grad, down_w[0], NT, preferred_element_type=F32)
        gate_back = (hidden_grad * up_pre * sig * (1.0 + gate_pre * (1.0 - sig))).astype(BF16)
        up_back = (hidden_grad * act).astype(BF16)
        back = lax.dot_general(
            gate_back, gate_w[0], NT, preferred_element_type=F32
        ) + lax.dot_general(up_back, up_w[0], NT, preferred_element_type=F32)
        rs[:, part] = back.astype(BF16).reshape(16, 16, 1024)
        send_pieces(home, 16 * r, 16 * r + 16, c)
        hid[:, part] = hidden.reshape(16, 16, 512)
        gb[:, part] = gate_back.reshape(16, 16, 512)
        ub[:, part] = up_back.reshape(16, 16, 512)
        og[:, part] = out_grad.reshape(16, 16, 1024)

    times(0, ROUNDS, group)
    pl.when(c == 0)(home_same.start)
    for n in range(16):
        ggs[n] = as_row(ggcol[n, :, 0:1])
        start_tiles(gg_home, n + 1, c, gg_same)
    eo_keep = pltpu.make_async_copy(eo_out, eo_hbm, lo.at[1])
    eo_keep.start()
    for j in range(4):
        part = slice(256 * j, 256 * j + 256)
        x_turned = xl_rows[:, :, part].reshape(1280, 256)
        for n, grads in ((0, gb), (1, ub)):
            ex_out[n, part] = lax.dot_general(
                x_turned, grads[...].reshape(1280, 512), TN, preferred_element_type=F32
            ).astype(BF16)
        half = slice(512 * (j // 2), 512 * (j // 2) + 512)
        place_at = 512 * (j % 2) + 256 * (j // 2)
        turned = hid[:, :, 256 * (j % 2) : 256 * (j % 2) + 256].reshape(1280, 256)
        ex_out[2, place_at : place_at + 256] = lax.dot_general(
            turned, og[:, :, half].reshape(1280, 512), TN, preferred_element_type=F32
        ).astype(BF16)

    ex_keep = pltpu.make_async_copy(ex_out, ex_hbm, lo.at[2])
    ex_keep.start()
    settle_rows(r4.at[0], ggl, c)
    pl.when(c == 0)(gg_same.wait)
    for k in range(16):
        column = jnp.concatenate([ggl[k], jnp.zeros((120, 128), F32)]).T[0:80, 0:1]
        ggt[pl.ds(k, 1)] = jnp.sum(pick[k].astype(F32) * column, axis=0, keepdims=True)
    settle_rows(r3.at[0], rl, c)
    pl.when(c == 0)(home_same.wait)
    mgs[...] = lax.dot_general(
        pick[...].reshape(1280, 256), rl[...].reshape(1280, 1024), TN, preferred_element_type=F32
    )
    away = rows((1 - c) * 128, 128)
    own = rows(c * 128, 128)
    back_near = [
        to(ggt.at[:, away], gg_in, sx.at[3], rx.at[3], b, sib),
        to(mgs.at[away], mg_in, sx.at[2], rx.at[2], b, sib),
    ]
    for item in back_near:
        item.start()
    settle_rows(s1.at[0], xs, c)
    settle_rows(s2.at[0], gs, c)
    settle_rows(s3.at[0], rs, c)
    settle_rows(s4.at[0], ggs, c)
    back_near[0].wait()

    gg_all[...] = jnp.zeros_like(gg_all)
    for k in range(16):
        gg_all[pl.ds(2 * k + odd, 1)] = ggt[pl.ds(k, 1), own]
        gg_all[pl.ds(2 * k + 1 - odd, 1)] = gg_in[pl.ds(k, 1)]
    gate_grad = gg_all[...].T
    own_gates = gt[own]
    logit_grad = own_gates * (
        gate_grad - jnp.sum(own_gates * gate_grad, axis=1, keepdims=True)
    )
    router_out[...] = lax.dot_general(
        logit_grad, tok[own].astype(F32), TN, preferred_element_type=F32, precision=PRECISE
    )[0:NB]
    routed = jnp.dot(
        logit_grad, router[...], preferred_element_type=F32, precision=PRECISE
    )
    back_near[1].wait()
    mixed_grad = mgs[own] + mg_in[...] + routed
    middle = middle_ref[...]
    scale = row_scale(middle)
    unit = middle * scale
    small_out[...] = jnp.sum(mixed_grad * unit, axis=0, keepdims=True)
    inner = mixed_grad * ffn_gain[...]
    grad = cot[...].astype(F32) + scale * (
        inner - unit * jnp.mean(inner * unit, axis=1, keepdims=True)
    )
    grad_out[...] = grad
    low_out[...] = grad.astype(BF16)
    for item in (wts_keep, eo_keep, ex_keep):
        item.wait()


def backward_kernel(
    lengths, attn_grad, context, wo, head_gain, attn_gain, ffn_part, router_part, eo, ex,
    q_hbm, kv_hbm, wide_hbm, inv_hbm, wv_hbm, raw_hbm, normed_hbm, li_hbm, turn_hbm, wts_hbm, mid_hbm, grad_hbm,
    out, in_grad, wq_grad, wk_grad, wv_grad, wo_grad, attn_small, q_small, k_small, ffn_small, router_grad,
    exg_out, exu_out, exd_out,
    q_ref, kv_ref, wide_ref, inv_ref, wv, raw, normed, li2, turn, wts, middle, grad,
    cg, cgs, qp, gp, gi, qt, gt, gti, dt, di, dqs, dkvt, stage, dq_acc,
    wo_other, wo_in, wo_sum, ex_in, ex_sum, ex_cross, dq, dkv, home, wo_parts,
    low, w_other, w_in, w_sum, w_land, back, back_low, back_in, mix, mix_in, small, four, many,
    r_land, r_four, r_tot, router_out,
    s1, r1, s2, r2, s3, r3, s4, r4, s5, r5, s6, r6, s7, r7, s8, r8, s9, r9, sa, ra, sx, rx, ls, li, se, re, le,
):
    b, xl, c, y, m = place()
    h = 2 * xl + c
    sib = 2 * xl + 1 - c
    over = 2 * (1 - xl) + c
    e0, e1, total = lengths[0], lengths[0] + lengths[1], 512 * NB
    brought = [
        pltpu.make_async_copy(src, dst, li.at[n])
        for n, (src, dst) in enumerate(
            (
                (q_hbm, q_ref),
                (kv_hbm, kv_ref),
                (wide_hbm, wide_ref),
                (inv_hbm, inv_ref),
                (wv_hbm, wv),
                (raw_hbm, raw),
                (normed_hbm, normed),
                (li_hbm, li2),
                (turn_hbm, turn),
                (wts_hbm, wts),
                (mid_hbm, middle),
                (grad_hbm, grad),
            )
        )
    ]
    for item in brought:
        item.start()
    bar = pltpu.get_barrier_semaphore()
    for dj in range(GROUP):
        j = member(m, lax.rem(y + dj, GROUP))
        signal(bar, j, 2 * (1 - xl) + 1 - c)
        signal(bar, j, 2 * xl + 1 - c)
    times(1, NB, lambda d: signal(bar, lax.rem(b + d, NB), h))
    times(0, NB, lambda d: signal(bar, lax.rem(b + d, NB), over))
    pl.semaphore_wait(bar, 2 * NB - 1 + 2 * GROUP)

    ex_swap = to(ex.at[:, rows((1 - c) * 512, 512)], ex_in, sx.at[1], rx.at[1], b, sib)
    ex_swap.start()
    ex_own = pltpu.make_async_copy(ex.at[:, rows(c * 512, 512)], ex_sum, ls.at[1])
    ex_own.start()
    turned_back = jnp.zeros((128, 1024), F32)
    for i in range(2):
        for x2, part in ((xl, wo[0, i]), (1 - xl, wo[1, i])):
            turned_back = turned_back + lax.dot_general(
                attn_grad[:, rows(512 * x2 + 256 * i, 256)], part, NT, preferred_element_type=F32
            )
    for n in range(2 * GROUP):
        cg[n] = turned_back[:, 128 * n : 128 * n + 128].astype(BF16)
    turns = [(dj, dx, dc) for dj in range(GROUP) for dx in range(2) for dc in range(2)]
    cg_pieces = []
    for k, (dj, dx, dc) in enumerate(turns):
        j = lax.rem(y + dj, GROUP)
        x2 = lax.rem(xl + dx, 2)
        src, dst = cg.at[4 * x2 + j], cgs.at[y, rows(c * 256 + xl * 128, 128)]
        if k == 0:
            cg_pieces.append(pltpu.make_async_copy(src, dst, ls.at[0]))
        else:
            head = 2 * x2 + lax.rem(c + dc, 2)
            cg_pieces.append(to(src, dst, s1.at[0], r1.at[0], member(m, j), head))
    for item in cg_pieces:
        item.start()

    def tile(n):
        return router_part.at[rows(8 * (n // 8), 8), rows(128 * lax.rem(n, 8), 128)]

    def router_first(d):
        to_b = lax.rem(b + d, NB)
        return to(tile(to_b), r_land.at[b], s8.at[0], r8.at[0], to_b, h)

    times(1, NB, lambda d: router_first(d).start())
    r_land[b] = router_part[rows(8 * (b // 8), 8), rows(128 * lax.rem(b, 8), 128)]

    eo_piece = rows_home(eo, home, b, xl, c, lambda r: s2.at[0], lambda r: r2.at[0])
    eo_same = pltpu.make_async_copy(eo.at[15], home.at[b // 2], ls.at[2])
    pl.when(c == 0)(eo_same.start)
    send_pieces(eo_piece, 0, 32, c)

    def out_part(x2, core):
        cols = pl.ds(pl.multiple_of(512 * x2 + 256 * core, 256), 256)
        return lax.dot_general(
            context[...], attn_grad[:, cols], TN, preferred_element_type=F32
        )

    for x2 in range(2):
        wo_other[x2] = out_part(x2, 1 - c).astype(BF16)
    wo_swap = to(wo_other, wo_in, sx.at[0], rx.at[0], b, sib)
    wo_swap.start()
    brought[0].wait()
    for i in range(GROUP):
        both = q_ref[i].astype(F32)
        pad_queries(both, qp, i)
        turned = both.T
        qt[i] = jnp.concatenate([turned[0:64], turned[64:128]], axis=1).astype(BF16)
    dq_acc[...] = jnp.zeros_like(dq_acc)
    wo_swap.wait()
    for x2 in range(2):
        wo_sum[x2] = (out_part(x2, c) + wo_in[x2].astype(F32)).astype(BF16)
    ex_swap.wait()
    ex_own.wait()
    ex_sum[...] = (ex_sum[...].astype(F32) + ex_in[...].astype(F32)).astype(BF16)

    def cross_piece(n, j):
        part = rows(32 * j, 32)
        return to(ex_sum.at[n, part], ex_cross.at[n, part], sx.at[2], rx.at[2], b, over)


    def wo_piece(e):
        d, x2 = lax.rem(e, NB), lax.rem(xl + e // NB, 2)
        peer_b = lax.rem(b + d, NB)
        part = wo_sum.at[x2, rows(peer_b * 32, 32)]
        return to(part, wo_parts.at[NB * (e // NB) + b], s3.at[0], r3.at[0], peer_b, 2 * x2 + c)

    for n in range(3):
        times(0, 8, lambda j, n=n: cross_piece(n, j).start())
    cg_pieces[0].wait()
    settle(r1.at[0], home.at[pl.ds(0, 3)])
    wo_parts[b] = wo_sum[xl, rows(b * 32, 32)]
    for item in brought[1:4]:
        item.wait()
    left = lax.broadcasted_iota(jnp.int32, (512, 128), 1) < 64
    for i in range(GROUP):
        scaled = cgs[i].astype(F32) * inv_ref[i]
        pos = query_positions((512, 1), 0, member(m, i))
        mid_doc = (pos >= e0) & (pos < e1)
        terms = scaled * wide_ref[i]
        one = jnp.sum(jnp.where(left, terms, 0.0), axis=1, keepdims=True)
        two = jnp.sum(jnp.where(left, 0.0, terms), axis=1, keepdims=True)
        upper = jnp.where(left, 0.0, pltpu.roll(scaled, 64, 1))
        lower = jnp.where(left, 0.0, scaled)
        for part, val, term in ((0, upper, one), (512, lower, two)):
            span = pl.ds(part, 512)
            gp[i, span] = val.astype(BF16)
            gi[i, span] = jnp.where(mid_doc, val, 0.0).astype(BF16)
            dt[i, span] = jnp.broadcast_to(term, (512, 128))
            di[i, span] = jnp.broadcast_to(jnp.where(mid_doc, term, 0.0), (512, 128))
            lanes = pl.ds(part, 512)
            gt[i, :, lanes] = val.T[64:128].astype(BF16)
            gti[i, :, lanes] = jnp.where(mid_doc, val, 0.0).T[64:128].astype(BF16)

    def dkv_piece(kb):
        return to(stage.at[kb], dkv.at[b], s4.at[0], r4.at[0], kb, h)

    def pair(dp):
        p = lax.rem(b // 2 + 1 + dp, 16)
        send_pieces(eo_piece, jnp.minimum(32 + 8 * dp, 80), jnp.minimum(40 + 8 * dp, 80), c)
        for n in range(3):
            pl.when(dp < 8)(lambda n=n: cross_piece(n, dp + 8).start())
        times(
            jnp.clip(8 * (dp - 2), 1, 2 * NB),
            jnp.clip(8 * (dp - 1), 1, 2 * NB),
            lambda e: wo_piece(e).start(),
        )
        dkvt[...] = jnp.zeros_like(dkvt)
        keys = kv_ref[pl.ds(2 * p, 2)].reshape(512, 128)

        def step(i, expo, g, gturn, dots):
            size = expo.shape[1]
            part = keys[0:size]
            prob = lax.dot_general(g[i], part, NT, preferred_element_type=F32)
            term = jnp.concatenate([dots[i]] * (size // 128), axis=1)
            score_grad = (expo * (prob - term)).astype(BF16)
            dq_acc[i] += jnp.dot(score_grad, part, preferred_element_type=F32)
            dkvt[0:64, 0:size] += jnp.dot(qt[i], score_grad, preferred_element_type=F32)
            dkvt[64:128, 0:size] += jnp.dot(
                gturn[i], expo.astype(BF16), preferred_element_type=F32
            )

        def scores(i, size):
            return jnp.exp(
                lax.dot_general(qp[i], keys[0:size], NT, preferred_element_type=F32)
            )

        def inside(i):
            step(i, scores(i, 512), gi, gti, di)

        def edge(i, qb, size):
            low, high = limits(query_positions((1024, 1), 0, qb), e0, e1, total)
            kpos = key_positions((1, size), 1, 2 * p, c)
            expo = jnp.where((kpos >= low) & (kpos < high), scores(i, size), 0.0)
            step(i, expo, gp, gt, dt)

        on_pair(p, m, inside, edge)
        for n in range(2):
            kb = 2 * p + n
            stage[kb] = dkvt[:, 256 * n : 256 * n + 256].astype(BF16)

            @pl.when(kb != b)
            def _():
                dkv_piece(kb).start()

    times(0, 6, pair)
    settle(r8.at[0], r_land.at[pl.ds(0, NB - 1)])
    part = r_land[0]
    for n in range(1, NB):
        part = part + r_land[n]
    r_four[h] = part
    router_near = [
        to(r_four.at[h], r_four.at[h], s9.at[d], r9.at[d], b, lax.rem(h + d, 4))
        for d in range(1, 4)
    ]
    for item in router_near:
        item.start()
    times(6, 16, pair)
    dkv[b] = stage[b]
    for i in range(GROUP):
        both = jnp.where(left, dq_acc[i, 0:512], pltpu.roll(dq_acc[i, 512:1024], 64, 1))
        dqs[i] = (both * SCALE).astype(BF16)

    def dq_piece(part, dj, dc):
        j = lax.rem(y + dj, GROUP)
        c2 = lax.rem(c + dc, 2)
        src = dqs.at[j, rows(c2 * 256 + part * 128, 128)]
        dst = dq.at[c, y, rows(part * 128, 128)]
        k = 8 * part + 2 * dj + dc
        if dj + dc == 0:
            return pltpu.make_async_copy(src, dst, s5.at[k])
        return to(src, dst, s5.at[k], r5.at[k], member(m, j), 2 * xl + c2)

    dq_pieces = [dq_piece(n, dj, dc) for n in range(2) for dj in range(GROUP) for dc in range(2)]
    for item in dq_pieces:
        item.start()
    for item in router_near:
        item.wait()
    r_tot[...] = r_four[0] + r_four[1] + r_four[2] + r_four[3]
    home_tile = (rows(8 * (b // 8), 8), rows(128 * lax.rem(b, 8), 128))
    router_out[home_tile] = r_tot[...]

    def router_last(d):
        return to(r_tot, router_out.at[home_tile], sa.at[0], ra.at[0], lax.rem(b + d, NB), h)

    times(1, NB, lambda d: router_last(d).start())
    settle(sx.at[2], ex_cross)
    settle(rx.at[2], ex_cross)
    ex_in[...] = (ex_sum[...].astype(F32) + ex_cross[...].astype(F32)).astype(BF16)
    half, quarter = rows(c * 512, 512), rows(c * 256, 256)
    ex_moves = []
    for n, (src, dst) in enumerate(
        (
            (ex_in.at[0], exg_out.at[half]),
            (ex_in.at[1], exu_out.at[half]),
            (ex_in.at[2, pl.ds(0, 256)], exd_out.at[quarter, pl.ds(0, 512)]),
            (ex_in.at[2, pl.ds(256, 256)], exd_out.at[quarter, pl.ds(512, 512)]),
        )
    ):
        ex_moves.append(pltpu.make_async_copy(src, dst, le.at[n]))
        ex_moves.append(to(src, dst, se.at[n], re.at[n], b, sib))
    for item in ex_moves:
        item.start()
    for item in dq_pieces:
        item.wait()
    settle(r4.at[0], dkv.at[pl.ds(0, NB - 1)])

    for item in brought[4:]:
        item.wait()
    left, first = lanes_of((256, 128))
    q_gain = jnp.zeros((1, 128), F32)
    k_gain = jnp.zeros((1, 128), F32)

    def unprep(d, u, gain, row):
        turned = d * turn[0] - swapped(d, first) * turn[1]
        scale = lax.rsqrt(by_head(u * u, left) + EPSILON)
        unit = u * scale
        inner = turned * row
        gain = gain + jnp.sum(turned * unit, axis=0, keepdims=True)
        return scale * (inner - unit * by_head(inner * unit, left)), gain

    for j in range(GROUP):
        i, q_cols, kv_cols = slab(j)
        span = slice(128 * j, 128 * j + 128)
        d = (dq[0, j].astype(F32) + dq[1, j].astype(F32)).astype(BF16).astype(F32)
        got, q_gain = unprep(d, raw[i, :, q_cols], q_gain, head_gain[0:1])
        low[i, :, q_cols] = got.astype(BF16)
        d = dkv[8 * j].astype(F32)
        for n in range(1, 8):
            d = d + dkv[8 * j + n].astype(F32)
        d = d.T.astype(BF16).astype(F32)
        got, k_gain = unprep(d, raw[i, :, kv_cols], k_gain, head_gain[1:2])
        low[i, :, kv_cols] = jnp.where(left, got, d).astype(BF16)
    normed_grad = lax.dot_general(low[0], wv[0], NT, preferred_element_type=F32) + lax.dot_general(
        low[1], wv[1], NT, preferred_element_type=F32
    )
    source2 = li2[...].reshape(256, 1024).astype(F32)
    scale = row_scale(source2)
    unit = source2 * scale
    inner = normed_grad * attn_gain[...]
    attn_part = jnp.sum(normed_grad * unit, axis=0, keepdims=True)
    small[...] = jnp.zeros_like(small)
    for n in range(8):
        lanes = slice(128 * n, 128 * n + 128)
        small[n : n + 1] = attn_part[:, lanes]
        small[8 + n : 9 + n] = ffn_part[:, lanes]
    small[16:17] = q_gain
    small[17:18] = k_gain
    near = [
        to(small, four.at[h], sx.at[6 + d], rx.at[6 + d], b, lax.rem(h + d, 4)) for d in range(1, 4)
    ]
    for item in near:
        item.start()
    four[h] = small[...]
    w_other[...] = lax.dot_general(
        normed[...], low[1 - c], TN, preferred_element_type=F32
    ).astype(BF16).reshape(NB, 32, 512)
    w_swap = to(w_other, w_in, sx.at[4], rx.at[4], b, sib)
    w_swap.start()
    back[...] = (scale * (inner - unit * jnp.mean(inner * unit, axis=1, keepdims=True))).reshape(
        2, 128, 1024
    )
    back_low[...] = back[1 - xl].astype(BF16)
    back_swap = to(back_low, back_in, sx.at[5], rx.at[5], b, over)
    back_swap.start()
    mine = lax.dot_general(normed[...], low[c], TN, preferred_element_type=F32)
    for item in near:
        item.wait()
    many[b] = four[0] + four[1] + four[2] + four[3]

    def spread(d):
        return to(many.at[b], many.at[b], s7.at[0], r7.at[0], lax.rem(b + d, NB), h)

    times(1, NB, lambda d: spread(d).start())
    w_swap.wait()
    w_sum[...] = (mine.reshape(NB, 32, 512) + w_in[...].astype(F32)).astype(BF16)

    def w_piece(d):
        peer = lax.rem(b + d, NB)
        return to(w_sum.at[peer], w_land.at[b], s6.at[0], r6.at[0], peer, h)

    times(1, NB, lambda d: w_piece(d).start())
    w_land[b] = w_sum[b]

    settle_rows(r2.at[0], home, c)
    pl.when(c == 0)(eo_same.wait)
    flat = home[...].reshape(1280, 1024)
    mix[...] = (
        lax.dot_general(wts[0].reshape(1280, 256), flat, TN, preferred_element_type=F32)
        + lax.dot_general(wts[1].reshape(1280, 256), flat, TN, preferred_element_type=F32)
    ).reshape(2, 128, 1024)
    mix_swap = to(mix.at[1 - c], mix_in, sx.at[6], rx.at[6], b, sib)
    mix_swap.start()
    back_swap.wait()
    in_grad[...] = (grad[...] + back[xl] + back_in[...].astype(F32)).astype(BF16)
    mix_swap.wait()
    out[...] = (middle[...] + mix[c] + mix_in[...]).astype(BF16)
    settle(r7.at[0], many.at[pl.ds(0, NB - 1)])
    total = many[0]
    for n in range(1, NB):
        total = total + many[n]
    for n in range(8):
        lanes = slice(128 * n, 128 * n + 128)
        attn_small[:, lanes] = total[n : n + 1]
        ffn_small[:, lanes] = total[8 + n : 9 + n]
    q_small[...] = total[16:17, 0:64] + total[16:17, 64:128]
    k_small[...] = total[17:18, 0:64]
    settle(r6.at[0], w_land.at[pl.ds(0, NB - 1)])
    shard = w_land[0].astype(F32)
    for n in range(1, NB):
        shard = shard + w_land[n].astype(F32)
    wq_grad[...] = shard[:, 0:256]
    wk_grad[...] = jnp.concatenate([shard[:, 256:320], shard[:, 384:448]], axis=1)
    wv_grad[...] = jnp.concatenate([shard[:, 320:384], shard[:, 448:512]], axis=1)
    settle(r3.at[0], wo_parts.at[pl.ds(0, 2 * NB - 1)])
    total = wo_parts[0].astype(F32)
    for n in range(1, 2 * NB):
        total = total + wo_parts[n].astype(F32)
    wo_grad[...] = total
    for item in ex_moves:
        item.wait()
    settle(ra.at[0], r_land.at[pl.ds(0, NB - 1)])
    router_grad[...] = router_out[...]
    settle(s1.at[0], home.at[pl.ds(0, 3)])
    settle_rows(s2.at[0], home, c)
    settle(s3.at[0], wo_parts.at[pl.ds(0, 2 * NB - 1)])
    settle(s4.at[0], dkv.at[pl.ds(0, NB - 1)])
    settle(s6.at[0], w_land.at[pl.ds(0, NB - 1)])
    settle(s7.at[0], many.at[pl.ds(0, NB - 1)])
    settle(s8.at[0], r_land.at[pl.ds(0, NB - 1)])
    settle(sa.at[0], r_land.at[pl.ds(0, NB - 1)])


def results_kernel(*refs):
    n = (len(refs) - 5) // 3
    ins, outs, held = refs[:n], refs[n : 2 * n], refs[2 * n : 3 * n]
    wide, (load_sem, store_sem) = refs[3 * n : 3 * n + 3], refs[3 * n + 3 :]
    loads = [pltpu.make_async_copy(ins[k], held[k], load_sem.at[k]) for k in range(n)]
    for item in loads[n - 3 :] + loads[: n - 3]:
        item.start()
    stores = []
    for k in [n - 3, n - 2, n - 1, *range(n - 3)]:
        loads[k].wait()
        src, dst = held[k], outs[k]
        if k >= n - 3:
            src, dst = wide[k - n + 3], dst.at[0]
            src[...] = held[k][...].astype(F32)
        stores.append(pltpu.make_async_copy(src, dst, store_sem.at[k]))
        stores[-1].start()
    for item in stores:
        item.wait()


def finished(results):
    n = len(results)
    shapes = [jax.ShapeDtypeStruct(r.shape, r.dtype) for r in results[: n - 3]] + [
        jax.ShapeDtypeStruct((1,) + r.shape, F32) for r in results[n - 3 :]
    ]
    return pl.pallas_call(
        results_kernel,
        out_shape=shapes,
        in_specs=[ANY] * n,
        out_specs=[ANY] * n,
        scratch_shapes=[pltpu.VMEM(r.shape, r.dtype) for r in results]
        + [pltpu.VMEM(r.shape, F32) for r in results[n - 3 :]]
        + [pltpu.SemaphoreType.DMA((n,))] * 2,
        compiler_params=pltpu.CompilerParams(vmem_limit_bytes=60 * 1024 * 1024),
    )(*results)


VM = pl.BlockSpec(memory_space=pltpu.VMEM)
SM = pl.BlockSpec(memory_space=pltpu.SMEM)
ANY = pl.BlockSpec(memory_space=pl.ANY)


def call(kernel, collective_id, ins, outs, scratch, sems, flops, *operands):
    return pl.pallas_call(
        kernel,
        out_shape=[jax.ShapeDtypeStruct(shape, dtype) for shape, dtype, _ in outs],
        in_specs=ins,
        out_specs=[spec for _, _, spec in outs],
        scratch_shapes=[pltpu.VMEM(shape, dtype) for shape, dtype in scratch]
        + [pltpu.SemaphoreType.DMA(n) for n in sems],
        compiler_params=pltpu.CompilerParams(
            collective_id=collective_id,
            has_side_effects=True,
            vmem_limit_bytes=60 * 1024 * 1024,
        ),
        cost_estimate=pl.CostEstimate(
            flops=flops, bytes_accessed=8_000_000, transcendentals=flops // 2000
        ),
    )(*operands)


def limits(pos, e0, e1, total):
    low = jnp.where(pos < e0, 0, jnp.where(pos < e1, e0, e1))
    end = jnp.where(pos < e0, e0, jnp.where(pos < e1, e1, total))
    reach = low + ((pos - low) // BLOCK + 1) * BLOCK
    return low, jnp.minimum(end, reach)


def query_positions(shape, axis, qb):
    r = lax.broadcasted_iota(jnp.int32, shape, axis)
    r = lax.rem(r, 512)
    return 512 * qb + 256 * lax.rem(r // 128, 2) + 128 * (r // 256) + lax.rem(r, 128)


def key_positions(shape, axis, kb, core):
    r = lax.broadcasted_iota(jnp.int32, shape, axis)
    return 512 * (kb + r // 256) + 256 * lax.rem(r // 128, 2) + 128 * core + lax.rem(r, 128)


def body(
    layer_input,
    attn_gain,
    w_query,
    key_weight,
    value_weight,
    w_output,
    query_gain,
    key_gain,
    ffn_gain,
    router,
    w_gate,
    w_up,
    w_down,
    routes,
    doc_lengths,
    cotangent,
):
    tokens, width = layer_input.shape
    lane = np.arange(128) % (HEAD_SIZE // 2)
    pace = jnp.asarray(ROPE_BASE ** (-2.0 * lane / HEAD_SIZE), F32)[None]
    (
        w_full, wo_full, both_inputs, q_group, kv_all, up_rows, raw, normed, ctx_wide, ctx_inv, turn, router_wide,
        pick, context, middle, mixed_in, gates, head_gain,
    ) = call(
        forward_kernel,
        0,
        [SM] + [VM] * 13,
        [
            ((2, width, 512), BF16, ANY),
            ((2, 2, width, width // 4), BF16, ANY),
            ((2, tokens, width), BF16, ANY),
            ((GROUP, 512, 128), BF16, ANY),
            ((NB, 256, 128), BF16, ANY),
            ((16, SLOTS, width), BF16, ANY),
            ((2, 2 * tokens, 512), F32, ANY),
            ((2 * tokens, width), BF16, ANY),
            ((GROUP, 512, 128), F32, ANY),
            ((GROUP, 512, 128), F32, ANY),
            ((2, 2 * tokens, 128), F32, ANY),
            ((128, width), F32, ANY),
            ((16, SLOTS, 2 * tokens), BF16, VM),
            ((tokens, width), BF16, VM),
            ((tokens, width), F32, VM),
            ((2 * tokens, width), BF16, VM),
            ((2 * tokens, 128), F32, VM),
            ((2, 128), F32, VM),
        ],
        [
            ((2 * tokens, width), BF16),
            ((2 * tokens, 128), F32),
            ((2, 2 * tokens, 512), F32),
            ((2 * tokens, width), BF16),
            ((GROUP, 512, 128), F32),
            ((GROUP, 512, 128), F32),
            ((2, 2 * tokens, 128), F32),
            ((128, width), F32),
            ((32, 512), BF16),
            ((2, width, 512), BF16),
            ((2, 2, width, width // 4), BF16),
            ((2, tokens, width), BF16),
            ((2 * tokens, width), BF16),
            ((2, 8, 128), jnp.int32),
            ((16, SLOTS, width), BF16),
            ((GROUP, 2 * tokens, 128), BF16),
            ((GROUP, 2 * tokens, 128), BF16),
            ((GROUP, 512, 128), BF16),
            ((NB, 256, 128), BF16),
            ((GROUP, 1024, 128), BF16),
            ((80, 512), BF16),
            ((GROUP, 80, 1024), F32),
            ((GROUP, 80, 1024), F32),
            ((GROUP, 80, 1024), F32),
            ((GROUP, 512, 128), BF16),
            ((2 * GROUP, tokens, 128), BF16),
        ],
        [(1,)] * 4 + [(10,)] * 2 + [(16,)] * 2 + [(1,), (NB,)] + [(1,)] * 2 + [(8,)] * 2 + [(9,), (12,)],
        18_000_000_000,
        doc_lengths,
        w_query,
        key_weight,
        value_weight,
        w_output,
        layer_input,
        cotangent,
        routes.T,
        attn_gain[None],
        query_gain[None],
        key_gain[None],
        pace,
        ffn_gain[None],
        router.T,
    )
    wts, expert_out, ex_grads, middle_grad, attn_grad, ffn_part, router_part = call(
        experts_kernel,
        1,
        [VM] * 3 + [ANY] * 6 + [VM, ANY],
        [
            ((2, 16, SLOTS, 2 * tokens), BF16, ANY),
            ((16, SLOTS, width), BF16, ANY),
            ((3, 1024, 512), BF16, ANY),
            ((tokens, width), F32, VM),
            ((tokens, width), BF16, VM),
            ((1, width), F32, VM),
            ((NB, width), F32, VM),
        ],
        [
            ((16, SLOTS, width), BF16),
            ((1, width, 512), BF16),
            ((1, width, 512), BF16),
            ((1, 512, width), BF16),
            ((tokens, width), F32),
            ((tokens, width), BF16),
            ((128, width), F32),
            ((2, 16, SLOTS, 2 * tokens), BF16),
            ((16, SLOTS, width), BF16),
            ((3, 1024, 512), BF16),
            ((16, SLOTS, width), BF16),
            ((16, SLOTS, width), BF16),
            ((16, 8, 128), F32),
            ((16, 8, 128), F32),
            ((16, SLOTS, width), BF16),
            ((16, SLOTS, width), BF16),
            ((16, 8, 128), F32),
            ((16, 8, 128), F32),
            ((16, SLOTS, 512), BF16),
            ((16, SLOTS, 512), BF16),
            ((16, SLOTS, 512), BF16),
            ((16, SLOTS, width), BF16),
            ((2 * tokens, width), F32),
            ((16, 2 * tokens), F32),
            ((tokens, width), F32),
            ((16, tokens), F32),
            ((128, tokens), F32),
            ((16, SLOTS, 128), F32),
            ((16, SLOTS, 128), F32),
        ],
        [(1,), (ROUNDS,)] + [(1,)] * 6 + [(4,)] * 2 + [(4,), (7,), (3,)],
        12_000_000_000,
        mixed_in,
        gates,
        pick,
        up_rows,
        w_gate,
        w_up,
        w_down,
        middle,
        cotangent,
        ffn_gain[None],
        router_wide,
    )
    results = call(
        backward_kernel,
        2,
        [SM] + [VM] * 7 + [ANY] * 14,
        [
            ((tokens, width), BF16, VM),
            ((tokens, width), BF16, VM),
            ((32, 256), F32, VM),
            ((32, 128), F32, VM),
            ((32, 128), F32, VM),
            ((32, 256), F32, VM),
            ((1, width), F32, VM),
            ((1, HEAD_SIZE), F32, VM),
            ((1, HEAD_SIZE), F32, VM),
            ((1, width), F32, VM),
            ((NB, width), F32, VM),
            ((width, 512), BF16, ANY),
            ((width, 512), BF16, ANY),
            ((512, width), BF16, ANY),
        ],
        [
            ((GROUP, 512, 128), BF16),
            ((NB, 256, 128), BF16),
            ((GROUP, 512, 128), F32),
            ((GROUP, 512, 128), F32),
            ((2, width, 512), BF16),
            ((2, 2 * tokens, 512), F32),
            ((2 * tokens, width), BF16),
            ((2, tokens, width), BF16),
            ((2, 2 * tokens, 128), F32),
            ((2, 16, SLOTS, 2 * tokens), BF16),
            ((tokens, width), F32),
            ((tokens, width), F32),
            ((2 * GROUP, tokens, 128), BF16),
            ((GROUP, 512, 128), BF16),
            ((GROUP, 1024, 128), BF16),
            ((GROUP, 1024, 128), BF16),
            ((GROUP, 1024, 128), BF16),
            ((GROUP, 64, 1024), BF16),
            ((GROUP, 64, 1024), BF16),
            ((GROUP, 64, 1024), BF16),
            ((GROUP, 1024, 128), F32),
            ((GROUP, 1024, 128), F32),
            ((GROUP, 512, 128), BF16),
            ((128, 512), F32),
            ((NB, 128, 256), BF16),
            ((GROUP, 1024, 128), F32),
            ((2, 1024, 256), BF16),
            ((2, 1024, 256), BF16),
            ((2, 1024, 256), BF16),
            ((3, 512, 512), BF16),
            ((3, 512, 512), BF16),
            ((3, 512, 512), BF16),
            ((2, GROUP, 2 * tokens, 128), BF16),
            ((NB, 128, 256), BF16),
            ((16, SLOTS, width), BF16),
            ((2 * NB, 32, 256), BF16),
            ((2, 2 * tokens, 512), BF16),
            ((NB, 32, 512), BF16),
            ((NB, 32, 512), BF16),
            ((NB, 32, 512), BF16),
            ((NB, 32, 512), BF16),
            ((2, tokens, width), F32),
            ((tokens, width), BF16),
            ((tokens, width), BF16),
            ((2, tokens, width), F32),
            ((tokens, width), F32),
            ((24, 128), F32),
            ((4, 24, 128), F32),
            ((NB, 24, 128), F32),
            ((NB, 8, 128), F32),
            ((4, 8, 128), F32),
            ((8, 128), F32),
            ((NB, width), F32),
        ],
        [(1,)] * 8 + [(16,)] * 2 + [(1,)] * 6 + [(4,)] * 2 + [(1,)] * 2 + [(10,)] * 2 + [(6,), (12,)] + [(4,)] * 3,
        45_000_000_000,
        doc_lengths,
        attn_grad,
        context,
        wo_full,
        head_gain,
        attn_gain[None],
        ffn_part,
        router_part,
        expert_out,
        ex_grads,
        q_group,
        kv_all,
        ctx_wide,
        ctx_inv,
        w_full,
        raw,
        normed,
        both_inputs,
        turn,
        wts,
        middle,
        middle_grad,
    )
    results = finished(results)
    return (
        *results[:2],
        results[6][0],
        *results[2:6],
        *[row[0] for row in results[7:10]],
        results[10].T,
        *results[11:],
    )


def solution(mesh):
    everyone = P(("blk", "head"), None)
    both = P("blk", "head")
    expert = P("blk", None, None)
    return jax.shard_map(
        body,
        mesh=mesh,
        in_specs=(everyone, P(), both, both, both, both, P(), P(), P(), P())
        + (expert, expert, expert, everyone, P(), everyone),
        out_specs=(everyone, everyone, P(), both, both, both, both, P(), P(), P(), P())
        + (expert, expert, expert),
        check_vma=False,
    )
```
